32 devices in a mesh: expert: 4 (over y, x), context: 2 (over core), dp: 4 (over z).
Axes of the slice: x: 2, y: 2, z: 4, core: 2. Of those that a mesh axis runs over, the one named last changes fastest.
Arguments:
- hidden_in: bfloat16 [16, 1024, 1536], P(('expert', 'dp'), 'context'), may hold values from -6 to 6
- out_grad: bfloat16 [16, 1024, 1536], P(('expert', 'dp'), 'context'), may hold values from -6 to 6
- routes: int32 [16, 1024, 4], P(('expert', 'dp'), 'context'), may hold values from 0 to 15, all different within a row; in each aligned block of 512 rows (0 to 511, 512 to 1023, ..., all dimensions but the last counted through in order) at most 256 rows name the same one
- attn_gain: float32 [1536], P(('context', 'dp')), may hold values from 0.5 to 1.5
- w_query: float32 [1536, 1536], P(('context', 'dp')), may hold values from -0.15625 to 0.15625
- key_projection: float32 [1536, 256], P(('context', 'dp')), may hold values from -0.15625 to 0.15625
- value_projection: float32 [1536, 256], P(('context', 'dp')), may hold values from -0.15625 to 0.15625
- w_out: float32 [1536, 1536], P(('context', 'dp')), may hold values from -1.75 to 1.75
- ffn_gain: float32 [1536], P(('context', 'dp')), may hold values from 0.5 to 1.5
- w_router: float32 [1536, 16], P(('context', 'dp')), may hold values from -0.078125 to 0.078125
- w_gate: float32 [16, 1536, 768], P('expert', ('context', 'dp')), may hold values from -0.15625 to 0.15625
- w_up: float32 [16, 1536, 768], P('expert', ('context', 'dp')), may hold values from -0.15625 to 0.15625
- w_down: float32 [16, 768, 1536], P('expert', None, ('context', 'dp')), may hold values from -0.4375 to 0.4375
Outputs:
- block_out: bfloat16 [16, 1024, 1536], P(('expert', 'dp'), 'context')
- grad_in: float32 [16, 1024, 1536], P(('expert', 'dp'), 'context')
- grad_attn_gain: float32 [1536], P(('context', 'dp'))
- grad_query: float32 [1536, 1536], P(('context', 'dp'))
- grad_key: float32 [1536, 256], P(('context', 'dp'))
- grad_value: float32 [1536, 256], P(('context', 'dp'))
- grad_out: float32 [1536, 1536], P(('context', 'dp'))
- grad_ffn_gain: float32 [1536], P(('context', 'dp'))
- grad_router: float32 [1536, 16], P(('context', 'dp'))
- grad_gate: float32 [16, 1536, 768], P('expert', ('context', 'dp'))
- grad_up: float32 [16, 1536, 768], P('expert', ('context', 'dp'))
- grad_down: float32 [16, 768, 1536], P('expert', None, ('context', 'dp'))
The draws below stay inside these ranges and needn't reach their ends.
Inputs may be any that keep to these rules, and one draw needn't show every extreme that they name: `routes`: each row names 4 different experts; among the 512 rows of one sequence block no expert is named by more than 256 rows, a bound that some block reaches.
All inputs are finite; a program needn't handle non-finite values.
Results may differ from the reference program's by a relative error of at most 0.022.
Values may be sent and summed in bfloat16 or wider, within the bound.
No kernel may reach another device: no remote copies, remote signals or barrier semaphores. Data moves between devices by JAX's collectives and lax.ppermute only.
A program may use at most 384 MiB of HBM per device.

```python
import math
import jax
import jax.numpy as jnp
import numpy as np
from jax import lax

MODEL_WIDTH = 1536
QUERY_HEADS = 12
KEY_VALUE_HEADS = 2
HEAD_SIZE = 128
FF = 768
TOP = 4
TOK_DEV = 512
EXPERTS = 16
SEQUENCE_LENGTH = 1024
SEQS = 16
CAP = 160
MOST = 256
N_CONTEXT = 2


def levels(stream_key, extent, pieces, least, largest):
    loudness = 1.0
    for dim, shards_of in pieces:
        steps = jax.random.uniform(jax.random.fold_in(jax.random.fold_in(stream_key, 6), dim), (shards_of,), jnp.float32, least / len(pieces), largest / len(pieces))
        loudness = loudness * jnp.repeat(jnp.exp(steps), extent[dim] // shards_of).reshape((-1,) + (1,) * (len(extent) - 1 - dim))
    return loudness


def assign_block(own_key, own, number, rows, count, top, bound, lean):
    ranking = jax.random.permutation(own_key, count)
    heavy_load, ordinary = load_shares(count, rows * top, bound, lean, True), load_shares(count, rows * top, bound, lean, False)
    places = jnp.arange(count)

    def named(lengths, offset_by):
        used = int((lengths > 0).sum())
        fixed = max(1, used // 4)
        passed = fixed + (places - fixed + offset_by * (used - fixed)) % max(1, count - fixed)
        return jnp.zeros((count,), jnp.int32).at[ranking[jnp.where(places < fixed, places, passed)]].set(jnp.asarray(lengths, jnp.int32))

    lengths = jnp.where(number % 4 == 0, named(heavy_load, number // 4), named(ordinary, number - number // 4 - 1))
    mixed = jax.random.permutation(jax.random.fold_in(own, 3), count)
    giver, taker = mixed[0:count // 2 * 2:2], mixed[1:count // 2 * 2:2]
    margin = jnp.minimum(lengths[giver] - 1, bound - lengths[taker]) // 2
    margin = jnp.where((giver == ranking[0]) | (taker == ranking[0]) | (lengths[taker] == 0), 0, jnp.maximum(margin, 0))
    passed = jax.random.randint(jax.random.fold_in(own, 4), (count // 2,), 0, 1 << 20) % (margin + 1)
    lengths = lengths.at[giver].add(-passed).at[taker].add(passed)
    labels = jnp.searchsorted(jnp.cumsum(lengths), jnp.arange(rows * top), side="right").astype(jnp.int32)
    table = labels.reshape(top, rows).T
    table = table[jax.random.permutation(jax.random.fold_in(own, 1), rows)]
    offset_by = jax.random.randint(jax.random.fold_in(own, 2), (rows, 1), 0, top)
    return jnp.take_along_axis(table, (jnp.arange(top)[None, :] + offset_by) % top, axis=1)


def load_shares(count, total, reach, lean, full):
    weights = [(1 << 20) // math.isqrt(rank ** lean) + 1 for rank in range(1, count + 1)]
    largest = reach if full else min(reach, max(-(-total // count), total * weights[0] // sum(weights)))
    least = 1 if total - largest >= count - 1 else 0
    counts, spare = [largest] + [least] * (count - 1), total - largest - least * (count - 1)
    while spare > 0:
        movable = [i for i in range(1, count) if counts[i] < largest] or [i for i in range(1, count) if counts[i] < reach]
        whole, left = sum([weights[i] for i in movable]), spare
        for i in movable:
            extra = min(reach - counts[i], max(1, left * weights[i] // whole), spare)
            counts[i] = counts[i] + extra
            spare = spare - extra
    return np.array(counts)


def noise(stream_key, dims, spread, limit, pieces=(), held_as=jnp.bfloat16):
    values = spread * jax.random.normal(stream_key, dims, jnp.float32)
    if pieces:
        values = values * levels(stream_key, dims, pieces, -0.22, 0.18)
    return jnp.clip(values, -limit, limit).astype(held_as)


def setup_inputs(seed: int = 0) -> dict:
    key_of = jax.random.split(jax.random.key(seed), 14)
    hidden_in = noise(key_of[0], (SEQS, SEQUENCE_LENGTH, MODEL_WIDTH), 1.0, 6.0, ((0, 16), (1, 2)))
    out_grad = noise(key_of[1], (SEQS, SEQUENCE_LENGTH, MODEL_WIDTH), 1.0, 6.0, ((0, 16), (1, 2)))
    routes_keys = jax.random.split(jax.random.fold_in(key_of[2], 1), SEQS * SEQUENCE_LENGTH // TOK_DEV)
    routes_turns = jax.random.permutation(jax.random.fold_in(key_of[2], 3), SEQS * SEQUENCE_LENGTH // TOK_DEV)
    routes = jax.vmap(lambda own, number: assign_block(jax.random.fold_in(key_of[2], 2), own, number, TOK_DEV, EXPERTS, TOP, MOST, 1))(routes_keys, routes_turns).reshape((SEQS, SEQUENCE_LENGTH, TOP))
    attn_gain = jnp.clip(1.0 + 0.1 * jax.random.normal(key_of[3], (MODEL_WIDTH,), jnp.float32), 0.5, 1.5)
    w_query = noise(key_of[4], (MODEL_WIDTH, QUERY_HEADS * HEAD_SIZE), MODEL_WIDTH ** -0.5, 0.15625, ((0, 8),), jnp.float32)
    key_projection = noise(key_of[5], (MODEL_WIDTH, KEY_VALUE_HEADS * HEAD_SIZE), MODEL_WIDTH ** -0.5, 0.15625, ((0, 8),), jnp.float32)
    value_projection = noise(key_of[6], (MODEL_WIDTH, KEY_VALUE_HEADS * HEAD_SIZE), MODEL_WIDTH ** -0.5, 0.15625, ((0, 8),), jnp.float32)
    w_out = noise(key_of[7], (QUERY_HEADS * HEAD_SIZE, MODEL_WIDTH), (max(1, QUERY_HEADS * HEAD_SIZE * 8 // SEQUENCE_LENGTH)) ** -0.5, 1.75, ((0, 8),), jnp.float32)
    ffn_gain = jnp.clip(1.0 + 0.1 * jax.random.normal(key_of[8], (MODEL_WIDTH,), jnp.float32), 0.5, 1.5)
    w_router = noise(key_of[9], (MODEL_WIDTH, EXPERTS), (4 * MODEL_WIDTH) ** -0.5, 0.078125, ((0, 8),), jnp.float32)
    w_gate = noise(key_of[10], (EXPERTS, MODEL_WIDTH, FF), MODEL_WIDTH ** -0.5, 0.15625, ((0, 4), (1, 8)), jnp.float32)
    w_up = noise(key_of[11], (EXPERTS, MODEL_WIDTH, FF), MODEL_WIDTH ** -0.5, 0.15625, ((0, 4), (1, 8)), jnp.float32)
    w_down = noise(key_of[12], (EXPERTS, FF, MODEL_WIDTH), (FF // 4) ** -0.5, 0.4375, ((0, 4), (2, 8)), jnp.float32)
    return {"hidden_in": hidden_in, "out_grad": out_grad, "routes": routes, "attn_gain": attn_gain, "w_query": w_query, "key_projection": key_projection, "value_projection": value_projection, "w_out": w_out, "ffn_gain": ffn_gain, "w_router": w_router, "w_gate": w_gate, "w_up": w_up, "w_down": w_down}


@jax.custom_vjp
def lower_precision(v):
    return lax.optimization_barrier(v.astype(jnp.bfloat16)).astype(jnp.float32)

@jax.custom_vjp
def lower_precision_backward(v):
    return v

def low_keep(v):
    return (lower_precision(v), None)

def low_pass(kept, grad):
    return (grad,)

def back_keep(v):
    return (v, None)

def back_low(kept, grad):
    return (lower_precision(grad),)
lower_precision.defvjp(low_keep, low_pass)
lower_precision_backward.defvjp(back_keep, back_low)
norm_eps = 1e-06
rope_base = 1000000.0
mask_fill = -1e+30
highest = lax.Precision.HIGHEST

def normalize(values, gain):
    return values * lax.rsqrt(lax.optimization_barrier(jnp.mean(values * values, axis=-1, keepdims=True)) + norm_eps) * gain

def rope_tables(start_pos, length, head_dim):
    half_dim = head_dim // 2
    freqs = rope_base ** (-(2.0 * jnp.arange(half_dim, dtype=jnp.float32)) / head_dim)
    places = (start_pos + jnp.arange(length, dtype=jnp.int32)).astype(jnp.float32)
    angles = places[:, None] * freqs[None, :]
    return (jnp.cos(angles), jnp.sin(angles))

def apply_rotary(heads, cosine_table, sine_values_table):
    half_dim = heads.shape[-1] // 2
    front_half = heads[..., :half_dim]
    back_half = heads[..., half_dim:]
    cos_wide = cosine_table[:, None, :]
    sin_wide = sine_values_table[:, None, :]
    return jnp.concatenate([front_half * cos_wide - back_half * sin_wide, back_half * cos_wide + front_half * sin_wide], axis=-1)

def matrix_product(left, right):
    return jnp.dot(left, right, precision=highest)

def sequence_tables(route_ids):
    flat_ids = route_ids.reshape(N_CONTEXT, TOK_DEV * TOP)
    expert_ids = jnp.arange(EXPERTS, dtype=jnp.int32)
    onehot = (flat_ids[:, :, None] == expert_ids[None, None, :]).astype(jnp.int32)
    ranks = lax.optimization_barrier(jnp.sum(jnp.cumsum(onehot, axis=1) * onehot, axis=2)) - 1
    block_ids = jnp.arange(N_CONTEXT, dtype=jnp.int32)[:, None]
    kept = ranks < CAP
    slot_count = EXPERTS * N_CONTEXT * CAP
    targets = flat_ids * (N_CONTEXT * CAP) + block_ids * CAP + ranks
    pair_pos = jnp.where(kept, targets, -1).reshape(SEQUENCE_LENGTH, TOP)
    token_ids = block_ids * TOK_DEV + jnp.arange(TOK_DEV * TOP, dtype=jnp.int32)[None, :] // TOP
    token_ids = jnp.broadcast_to(token_ids, flat_ids.shape)
    placed = jnp.where(kept, targets, slot_count).reshape(-1)
    slot_token = jnp.full((slot_count,), -1, jnp.int32).at[placed].set(token_ids.reshape(-1), mode='drop')
    return (slot_token, pair_pos)

def sequence_layer(weights, inputs_f, route_ids):
    gain_one, query_w, key_weight_matrix, value_weight_matrix, out_w, gain_two, router_w, gate_w, up_w, down_w = weights
    slot_token, pair_pos = sequence_tables(route_ids)
    query_group_width = QUERY_HEADS // KEY_VALUE_HEADS
    scale_factor = 1.0 / math.sqrt(HEAD_SIZE)
    cosine_table, sine_values_table = rope_tables(0, SEQUENCE_LENGTH, HEAD_SIZE)
    first_activation = lower_precision(normalize(inputs_f, gain_one))
    query_flat = lower_precision_backward(matrix_product(first_activation, query_w)).reshape(SEQUENCE_LENGTH, QUERY_HEADS, HEAD_SIZE)
    key_flat = lower_precision_backward(matrix_product(first_activation, key_weight_matrix)).reshape(SEQUENCE_LENGTH, KEY_VALUE_HEADS, HEAD_SIZE)
    value_blocks = lower_precision(lower_precision_backward(matrix_product(first_activation, value_weight_matrix))).reshape(SEQUENCE_LENGTH, KEY_VALUE_HEADS, HEAD_SIZE)
    query_blocks = lower_precision(apply_rotary(query_flat, cosine_table, sine_values_table)).reshape(SEQUENCE_LENGTH, KEY_VALUE_HEADS, query_group_width, HEAD_SIZE)
    key_b = lower_precision(apply_rotary(key_flat, cosine_table, sine_values_table))
    raw_scores = jnp.einsum('qgrd,kgd->grqk', query_blocks, key_b, precision=highest)
    places = jnp.arange(SEQUENCE_LENGTH, dtype=jnp.int32)
    causal = places[None, :] <= places[:, None]
    scores = lower_precision_backward(jnp.where(causal[None, None], raw_scores * scale_factor, mask_fill))
    probs = lower_precision(jax.nn.softmax(scores, axis=-1))
    mixed = jnp.einsum('grqk,kgd->qgrd', probs, value_blocks, precision=highest).reshape(SEQUENCE_LENGTH, QUERY_HEADS * HEAD_SIZE)
    mixed_b = lower_precision(lower_precision_backward(mixed))
    resid_one = inputs_f + lower_precision_backward(matrix_product(mixed_b, out_w))
    act_two = lower_precision(normalize(resid_one, gain_two))
    logits = lower_precision_backward(matrix_product(act_two, router_w))
    gates = jax.nn.softmax(jnp.take_along_axis(logits, route_ids, axis=1), axis=-1)
    slot_used = slot_token >= 0
    picked = jnp.where(slot_used[:, None], act_two[jnp.maximum(slot_token, 0)], 0.0)
    picked = picked.reshape(EXPERTS, N_CONTEXT * CAP, MODEL_WIDTH)
    gate_h = lower_precision_backward(jnp.einsum('ecd,edf->ecf', picked, gate_w, precision=highest))
    up_h = lower_precision_backward(jnp.einsum('ecd,edf->ecf', picked, up_w, precision=highest))
    hidden_b = lower_precision(jax.nn.gelu(gate_h) * up_h)
    expert_res = lower_precision(lower_precision_backward(jnp.einsum('ecf,efd->ecd', hidden_b, down_w, precision=highest)))
    expert_res = expert_res.reshape(EXPERTS * N_CONTEXT * CAP, MODEL_WIDTH)
    pair_kept = pair_pos >= 0
    returned = jnp.where(pair_kept[:, :, None], expert_res[jnp.maximum(pair_pos, 0)], 0.0)
    return resid_one + lax.optimization_barrier(jnp.sum(gates[:, :, None] * returned, axis=1))

def reference(hidden_in, out_grad, routes, attn_gain, w_query, key_projection, value_projection, w_out, ffn_gain, w_router, w_gate, w_up, w_down):
    masters = (attn_gain, w_query, key_projection, value_projection, w_out, ffn_gain, w_router, w_gate, w_up, w_down)

    def forward(inputs_all, *params):
        weights = tuple((lower_precision(master) for master in params))

        def step(carry, item):
            return (carry, sequence_layer(weights, item[0], item[1]))
        _, outputs = lax.scan(jax.checkpoint(step), jnp.zeros((), jnp.float32), (inputs_all, routes))
        return outputs
    inputs_all = hidden_in.astype(jnp.float32)
    result, pullback = jax.vjp(forward, inputs_all, *masters)
    grads = pullback(out_grad.astype(jnp.float32))
    return (result.astype(jnp.bfloat16), grads[0], grads[1], grads[2], grads[3], grads[4], grads[5], grads[6], grads[7], grads[8], grads[9], grads[10])
```

```python
import functools
import math

import jax
import jax.numpy as jnp
from jax import lax
from jax.experimental import pallas as pl
from jax.experimental.pallas import tpu as pltpu
from jax.sharding import PartitionSpec as P

MODEL_WIDTH = 1536
QUERY_HEADS = 12
KEY_VALUE_HEADS = 2
HEAD_SIZE = 128
FF = 768
TOP = 4
EXP_DEV = 4
GROUP = QUERY_HEADS // KEY_VALUE_HEADS
Q_WIDTH = QUERY_HEADS * HEAD_SIZE
KV_WIDTH = KEY_VALUE_HEADS * HEAD_SIZE
SMALL = 128

norm_eps = 1e-06
rope_base = 1000000.0
mask_fill = -1e30
bf16 = jnp.bfloat16
f32 = jnp.float32
VMEM_LIMIT = 60 * 1024 * 1024


def dot(a, b, dims=((1,), (0,))):
    return lax.dot_general(a, b, (dims, ((), ())), preferred_element_type=f32)


def after(value, *others):
    return lax.optimization_barrier((value,) + others)[0]


def flip(value, step):
    count = lax.axis_size("expert")
    return lax.ppermute(value, "expert", [(i, i ^ step) for i in range(count)])


def swap(value):
    return lax.ppermute(value, "context", [(0, 1), (1, 0)])


def rope_tables(start_pos, length, head_dim):
    half_dim = head_dim // 2
    freqs = rope_base ** (-(2.0 * jnp.arange(half_dim, dtype=f32)) / head_dim)
    places = (start_pos + jnp.arange(length, dtype=jnp.int32)).astype(f32)
    angles = places[:, None] * freqs[None, :]
    return (jnp.cos(angles), jnp.sin(angles))


def rotate(heads, cosine, sine):
    half_dim = heads.shape[-1] // 2
    a = heads[..., :half_dim]
    b = heads[..., half_dim:]
    c = cosine[:, None, :]
    s = sine[:, None, :]
    return jnp.concatenate([a * c - b * s, b * c + a * s], axis=-1)


def norm_parts(values):
    scale = lax.rsqrt(jnp.mean(values * values, axis=-1, keepdims=True) + norm_eps)
    return scale, values * scale


def assemble(own, other, context, expert):
    count = len(own)
    z, r, n = own[0].shape
    if r % 16 != 0:
        blocks = jnp.stack([jnp.stack(own), jnp.stack(other)])
        order = jnp.arange(count) ^ expert
        blocks = jnp.take(blocks, order, axis=1)
        blocks = jnp.take(blocks, jnp.arange(2) ^ context, axis=0)
        return jnp.transpose(blocks, (0, 2, 1, 3, 4)).reshape(2 * z * count * r, n)

    def kernel(place, *refs):
        sources, out, sems = refs[: 2 * count], refs[2 * count], refs[2 * count + 1]
        copies = []
        for k in range(count):
            for half in range(2):
                at = place[0] if half == 0 else 1 - place[0]
                copies.append(
                    pltpu.make_async_copy(
                        sources[half * count + k],
                        out.at[at, :, jnp.bitwise_xor(place[1], k)],
                        sems.at[half * count + k],
                    )
                )
        for copy in copies:
            copy.start()
        for copy in copies:
            copy.wait()

    size = 2 * z * count * r * n * 2
    shape = (2, z, count, r, n)
    out = pl.pallas_call(
        kernel,
        out_shape=jax.ShapeDtypeStruct(shape, bf16),
        grid_spec=pltpu.PrefetchScalarGridSpec(
            num_scalar_prefetch=1,
            grid=(1,),
            in_specs=[pl.BlockSpec(memory_space=pl.ANY)] * (2 * count),
            out_specs=pl.BlockSpec(shape, lambda i, place: (0, 0, 0, 0, 0)),
            scratch_shapes=[pltpu.SemaphoreType.DMA((2 * count,))],
        ),
        compiler_params=pltpu.CompilerParams(vmem_limit_bytes=VMEM_LIMIT),
        cost_estimate=pl.CostEstimate(flops=0, bytes_accessed=2 * size, transcendentals=0),
        name="assemble",
    )(jnp.stack([context, expert]).astype(jnp.int32), *own, *other)
    return out.reshape(2 * z * count * r, n)


def spread(block):
    count = lax.axis_size("expert")
    own = [block] + [flip(block, k) for k in range(1, count)]
    return own, [swap(b) for b in own]


GELU_C = math.sqrt(2.0 / math.pi)


def expert_kernel(count, tokens, capacity, place, *refs):
    acts, dys = refs[: 2 * count], refs[2 * count : 4 * count]
    w_ref, refs = refs[4 * count], refs[4 * count + 1 :]
    earlier, refs = refs[: len(refs) - 12], refs[len(refs) - 12 :]
    y_refs, d_refs, (x_ref, gdy_ref, h_ref, dg_ref, du_ref, abuf, dbuf, sems) = refs[:2], refs[2:4], refs[4:]
    step = pl.program_id(0)
    slot = lax.rem(step, 2)

    def copies(k, at):
        out = []
        for s in range(2):
            out.append(pltpu.make_async_copy(acts[s * count + k], abuf.at[at, s], sems.at[at, s]))
            out.append(pltpu.make_async_copy(dys[s * count + k], dbuf.at[at, s], sems.at[at, 2 + s]))
        return out

    @pl.when(step == 0)
    def _():
        for c in copies(0, 0):
            c.start()

    for k in range(1, count):

        @pl.when(step == k - 1)
        def _(k=k):
            for c in copies(k, k % 2):
                c.start()

    for k in range(count):

        @pl.when(step == k)
        def _(k=k):
            for c in copies(k, k % 2):
                c.wait()

    row = place[0]
    extra = abuf.shape[2] - tokens
    row_ids = lax.broadcasted_iota(jnp.int32, (extra, 3 * tokens), 0)
    slot_ids = lax.broadcasted_iota(jnp.int32, (capacity, tokens), 0).astype(f32)
    hits = []
    gate_cols = []
    for s in range(2):
        meta = abuf[slot, s, tokens:, :].astype(f32)
        line = jnp.sum(jnp.where(row_ids == row, meta, 0.0), axis=0, keepdims=True)
        gate_line = line[:, :tokens] + line[:, tokens : 2 * tokens]
        hit = slot_ids == line[:, 2 * tokens :]
        hits.append(hit)
        gate_col = jnp.sum(jnp.where(hit, gate_line, 0.0), axis=1, keepdims=True)
        gate_cols.append(gate_col)
        one = jnp.where(hit, 1.0, 0.0).astype(bf16)
        at = pl.ds(s * capacity, capacity)
        x_ref[at, :] = dot(one, abuf[slot, s, :tokens, :]).astype(bf16)
        gdy_ref[at, :] = dot(one, dbuf[slot, s]).astype(bf16)
    gate_col = jnp.concatenate(gate_cols, axis=0)
    wide = w_ref.shape[0] * w_ref.shape[3]
    w_gate = w_ref[:, 0, 0].reshape(wide, FF)
    w_up = w_ref[:, 0, 1].reshape(wide, FF)
    w_down = w_ref[:, 0, 2].reshape(wide, FF)
    x = x_ref[...]
    dy = gdy_ref[...]
    gate_h = dot(x, w_gate)
    up_h = dot(x, w_up)
    back = dot(dy, w_down)
    square = gate_h * gate_h
    tanh = jnp.tanh(GELU_C * gate_h * (1.0 + 0.044715 * square))
    half = 0.5 * (1.0 + tanh)
    gelu = gate_h * half
    slope = half + 0.5 * gate_h * (1.0 - tanh * tanh) * (GELU_C * (1.0 + 3 * 0.044715 * square))
    hidden = (gelu * up_h).astype(bf16)
    dgate_col = jnp.sum(hidden.astype(f32) * back, axis=1, keepdims=True)
    dhidden = back * gate_col
    dgate_h = (dhidden * up_h * slope).astype(bf16)
    dup_h = (dhidden * gelu).astype(bf16)
    h_ref[...] = hidden
    dg_ref[...] = dgate_h
    du_ref[...] = dup_h
    gdy_ref[...] = (dy.astype(f32) * gate_col).astype(bf16)
    result = (dot(hidden, w_down, ((1,), (1,))) * gate_col).astype(bf16)
    dx = (dot(dgate_h, w_gate, ((1,), (1,))) + dot(dup_h, w_up, ((1,), (1,)))).astype(bf16)
    for s in range(2):
        one = jnp.where(hits[s], 1.0, 0.0).astype(bf16)
        rows = slice(s * capacity, (s + 1) * capacity)
        y = dot(one, result[rows], ((0,), (0,)))
        d = dot(one, dx[rows], ((0,), (0,)))
        line = jnp.sum(jnp.where(hits[s], dgate_col[rows], 0.0), axis=0, keepdims=True)
        high = line.astype(bf16).astype(f32)
        line = jnp.concatenate([high, line - high, jnp.zeros_like(high)], axis=1)
        line = jnp.where(row_ids == row, line, 0.0)
        if earlier:
            y = y + earlier[s][0].astype(f32)
            d = d + earlier[2 + s][0, :tokens].astype(f32)
            line = line + earlier[2 + s][0, tokens:].astype(f32)
        y_refs[s][0] = y.astype(bf16)
        d_refs[s][0, :tokens] = d.astype(bf16)
        d_refs[s][0, tokens:] = line.astype(bf16)


def run_expert(acts, dys, weights, place, capacity, earlier=()):
    count = len(acts) // 2
    tokens = dys[0].shape[0]
    rows = acts[0].shape[0]
    cz, _, _, local, _ = weights.shape
    slots = 2 * capacity
    total = count * slots

    def row_block(width):
        return pl.BlockSpec((slots, width), lambda i, place: (i, 0))

    macs = total * (9 * MODEL_WIDTH * FF - 3 * MODEL_WIDTH * FF + 4 * tokens * MODEL_WIDTH)
    moved = 2 * (
        4 * count * (rows + tokens) * MODEL_WIDTH + total * (2 * MODEL_WIDTH + 3 * FF) + 3 * MODEL_WIDTH * FF
    )
    sums = [pl.BlockSpec((1, n, MODEL_WIDTH), lambda i, place: (i, 0, 0)) for n in (tokens, tokens, rows, rows)]
    return pl.pallas_call(
        functools.partial(expert_kernel, count, tokens, capacity),
        out_shape=(
            jax.ShapeDtypeStruct((count, tokens, MODEL_WIDTH), bf16),
            jax.ShapeDtypeStruct((count, tokens, MODEL_WIDTH), bf16),
            jax.ShapeDtypeStruct((count, rows, MODEL_WIDTH), bf16),
            jax.ShapeDtypeStruct((count, rows, MODEL_WIDTH), bf16),
            jax.ShapeDtypeStruct((total, MODEL_WIDTH), bf16),
            jax.ShapeDtypeStruct((total, MODEL_WIDTH), bf16),
            jax.ShapeDtypeStruct((total, FF), bf16),
            jax.ShapeDtypeStruct((total, FF), bf16),
            jax.ShapeDtypeStruct((total, FF), bf16),
        ),
        grid_spec=pltpu.PrefetchScalarGridSpec(
            num_scalar_prefetch=1,
            grid=(count,),
            in_specs=[pl.BlockSpec(memory_space=pl.ANY)] * (4 * count)
            + [
                pl.BlockSpec(
                    (cz, 1, 3, local, FF),
                    lambda i, place: (0, place[1], 0, 0, 0),
                    pipeline_mode=pl.Buffered(1),
                )
            ]
            + (sums if earlier else []),
            out_specs=(
                *sums,
                row_block(MODEL_WIDTH),
                row_block(MODEL_WIDTH),
                row_block(FF),
                row_block(FF),
                row_block(FF),
            ),
            scratch_shapes=[
                pltpu.VMEM((2, 2, rows, MODEL_WIDTH), bf16),
                pltpu.VMEM((2, 2, tokens, MODEL_WIDTH), bf16),
                pltpu.SemaphoreType.DMA((2, 4)),
            ],
        ),
        compiler_params=pltpu.CompilerParams(
            dimension_semantics=("arbitrary",), vmem_limit_bytes=VMEM_LIMIT
        ),
        cost_estimate=pl.CostEstimate(
            flops=2 * macs, bytes_accessed=moved, transcendentals=total * FF
        ),
        name="experts",
    )(place, *acts, *dys, weights, *earlier)


def weight_grad_kernel(x_ref, gdy_ref, h_ref, dg_ref, du_ref, out_ref):
    shape = (out_ref.shape[0], out_ref.shape[3], FF)
    x = x_ref[...]
    first = ((0,), (0,))
    out_ref[:, 0, 0] = dot(x, dg_ref[...], first).astype(bf16).reshape(shape)
    out_ref[:, 0, 1] = dot(x, du_ref[...], first).astype(bf16).reshape(shape)
    out_ref[:, 0, 2] = dot(gdy_ref[...], h_ref[...], first).astype(bf16).reshape(shape)


def weight_grads(x, gdy, hidden, dgate, dup, z, local):
    total = x.shape[0]
    wide = 384
    per = MODEL_WIDTH // 2 // wide
    full = pl.BlockSpec((total, FF), lambda i: (0, 0))
    column = pl.BlockSpec((total, wide), lambda i: (0, i))
    return pl.pallas_call(
        weight_grad_kernel,
        out_shape=jax.ShapeDtypeStruct((z, 2, 3, local, FF), bf16),
        grid=(MODEL_WIDTH // wide,),
        in_specs=[column, column, full, full, full],
        out_specs=pl.BlockSpec(
            (wide // local, 1, 3, local, FF), lambda i: (lax.rem(i, per), lax.div(i, per), 0, 0, 0)
        ),
        compiler_params=pltpu.CompilerParams(
            dimension_semantics=("arbitrary",), vmem_limit_bytes=VMEM_LIMIT
        ),
        cost_estimate=pl.CostEstimate(
            flops=6 * total * MODEL_WIDTH * FF,
            bytes_accessed=2 * (total * (2 * MODEL_WIDTH + 3 * FF) + 3 * MODEL_WIDTH * FF),
            transcendentals=0,
        ),
        name="weight_grads",
    )(x, gdy, hidden, dgate, dup)


SCORE = math.log2(math.e) / math.sqrt(HEAD_SIZE)
STRIP = 256


def roll_half(x):
    return pltpu.roll(x, HEAD_SIZE // 2, 1)


def causal(strip):
    shape = ((strip + 1) * STRIP, STRIP)
    key = lax.broadcasted_iota(jnp.int32, shape, 0)
    return key <= lax.broadcasted_iota(jnp.int32, shape, 1) + strip * STRIP


def attend_kernel(place, q_ref, ko_ref, vo_ref, kr_ref, vr_ref, cos_ref, sin_ref, rot_ref, mix_ref, log_ref):
    q = q_ref[...]
    rot_ref[...] = (q * cos_ref[...] + roll_half(q) * sin_ref[...]).astype(bf16)
    last = ((1,), (1,))
    first = ((0,), (0,))
    for r in range(q_ref.shape[0] // STRIP):
        rows = pl.ds(r * STRIP, STRIP)
        seen = (r + 1) * STRIP
        q = rot_ref[rows, :]
        far = jnp.where(place[0] > 0, dot(kr_ref[...], q, last), mask_fill)
        near = jnp.where(causal(r), dot(ko_ref[:seen, :], q, last), mask_fill)
        peak = jnp.maximum(
            jnp.max(far, axis=0, keepdims=True), jnp.max(near, axis=0, keepdims=True)
        )
        peak = peak * SCORE
        far = jnp.exp2(far * SCORE - peak)
        near = jnp.exp2(near * SCORE - peak)
        total = jnp.sum(far, axis=0, keepdims=True) + jnp.sum(near, axis=0, keepdims=True)
        out = dot(vr_ref[...], far.astype(bf16), first)
        out = out + dot(vo_ref[:seen, :], near.astype(bf16), first)
        mix_ref[rows, :] = (out / total).T.astype(bf16)
        log_ref[0, :, rows] = peak + jnp.log2(total)


def attention_specs(tokens):
    head = pl.BlockSpec((tokens, HEAD_SIZE), lambda h, place: (0, h))
    key = pl.BlockSpec((tokens, HEAD_SIZE), lambda h, place: (0, h // GROUP))
    value = pl.BlockSpec((tokens, HEAD_SIZE), lambda h, place: (0, KEY_VALUE_HEADS + h // GROUP))
    table = pl.BlockSpec((tokens, HEAD_SIZE), lambda h, place: (0, 0))
    log = pl.BlockSpec((1, 1, tokens), lambda h, place: (h, 0, 0))
    return head, key, value, table, log


def attention(context, qkv, near, far, cosine, sine):
    tokens = qkv.shape[0]
    head, key, value, table, log = attention_specs(tokens)
    pairs = 2 * tokens * tokens * QUERY_HEADS
    return pl.pallas_call(
        attend_kernel,
        out_shape=(
            jax.ShapeDtypeStruct((tokens, Q_WIDTH), bf16),
            jax.ShapeDtypeStruct((tokens, Q_WIDTH), bf16),
            jax.ShapeDtypeStruct((QUERY_HEADS, 1, tokens), f32),
        ),
        grid_spec=pltpu.PrefetchScalarGridSpec(
            num_scalar_prefetch=1,
            grid=(QUERY_HEADS,),
            in_specs=[head, key, value, key, value, table, table],
            out_specs=(head, head, log),
        ),
        compiler_params=pltpu.CompilerParams(
            dimension_semantics=("arbitrary",), vmem_limit_bytes=VMEM_LIMIT
        ),
        cost_estimate=pl.CostEstimate(
            flops=4 * pairs * HEAD_SIZE, bytes_accessed=tokens * Q_WIDTH * 10, transcendentals=pairs
        ),
        name="attention",
    )(context, qkv, near, near, far, far, cosine, sine)


def attend_back_kernel(
    place, q_ref, dout_ref, ko_ref, vo_ref, kr_ref, vr_ref, log_ref, cos_ref, sin_ref,
    dq_ref, dko_ref, dvo_ref, dkr_ref, dvr_ref,
):
    last = ((1,), (1,))
    first = ((0,), (0,))
    scale = 1.0 / math.sqrt(HEAD_SIZE)

    @pl.when(lax.rem(pl.program_id(0), GROUP) == 0)
    def _():
        for ref in (dko_ref, dvo_ref, dkr_ref, dvr_ref):
            ref[...] = jnp.zeros_like(ref)

    for r in range(q_ref.shape[0] // STRIP):
        rows = pl.ds(r * STRIP, STRIP)
        seen = (r + 1) * STRIP
        q = q_ref[rows, :]
        dout = dout_ref[rows, :]
        logs = log_ref[0, :, rows]
        far = jnp.where(place[0] > 0, dot(kr_ref[...], q, last), mask_fill)
        near = jnp.where(causal(r), dot(ko_ref[:seen, :], q, last), mask_fill)
        far = jnp.exp2(far * SCORE - logs)
        near = jnp.exp2(near * SCORE - logs)
        dvr_ref[...] += dot(far.astype(bf16), dout)
        dvo_ref[:seen, :] += dot(near.astype(bf16), dout)
        dfar = dot(vr_ref[...], dout, last)
        dnear = dot(vo_ref[:seen, :], dout, last)
        inner = jnp.sum(far * dfar, axis=0, keepdims=True)
        inner = inner + jnp.sum(near * dnear, axis=0, keepdims=True)
        dfar = (far * (dfar - inner)).astype(bf16)
        dnear = (near * (dnear - inner)).astype(bf16)
        dkr_ref[...] += dot(dfar, q) * scale
        dko_ref[:seen, :] += dot(dnear, q) * scale
        dq = dot(kr_ref[...], dfar, first) + dot(ko_ref[:seen, :], dnear, first)
        dq = dq.T * scale
        dq_ref[rows, :] = (dq * cos_ref[rows, :] - roll_half(dq) * sin_ref[rows, :]).astype(bf16)


def attention_back(context, query, dmixed, near, far, logs, cosine, sine):
    tokens = query.shape[0]
    head, key, value, table, log = attention_specs(tokens)
    pairs = 2 * tokens * tokens * QUERY_HEADS
    side = jax.ShapeDtypeStruct((tokens, KV_WIDTH), f32)
    return pl.pallas_call(
        attend_back_kernel,
        out_shape=(jax.ShapeDtypeStruct((tokens, Q_WIDTH), bf16), side, side, side, side),
        grid_spec=pltpu.PrefetchScalarGridSpec(
            num_scalar_prefetch=1,
            grid=(QUERY_HEADS,),
            in_specs=[head, head, key, value, key, value, log, table, table],
            out_specs=(head, key, key, key, key),
        ),
        compiler_params=pltpu.CompilerParams(
            dimension_semantics=("arbitrary",), vmem_limit_bytes=VMEM_LIMIT
        ),
        cost_estimate=pl.CostEstimate(
            flops=10 * pairs * HEAD_SIZE, bytes_accessed=tokens * Q_WIDTH * 8, transcendentals=pairs
        ),
        name="attention_back",
    )(context, query, dmixed, near, near, far, far, logs, cosine, sine)


def reduce_dense(grad, context, expert):
    count = lax.axis_size("expert")
    z = lax.axis_size("dp")
    n = grad.shape[1]
    r = grad.shape[0] // (2 * z * count)
    grad = grad.astype(bf16).reshape(2, z, count, r, n)
    theirs = swap(lax.dynamic_index_in_dim(grad, 1 - context, 0, keepdims=False))
    mine = lax.dynamic_index_in_dim(grad, context, 0, keepdims=False)

    def part(k):
        at = expert ^ k
        a = lax.dynamic_index_in_dim(mine, at, 1, keepdims=False)
        b = lax.dynamic_index_in_dim(theirs, at, 1, keepdims=False)
        return a.astype(f32) + b.astype(f32)

    total = part(0)
    for k in range(1, count):
        total = total + flip(part(k).astype(bf16), k).astype(f32)
    share = lax.psum_scatter(total.astype(bf16), "dp", scatter_dimension=0, tiled=False)
    blocks = jnp.stack([share] + [flip(share, k) for k in range(1, count)])
    pieces = [lax.dynamic_index_in_dim(blocks, expert ^ e, 0, keepdims=False) for e in range(count)]
    return jnp.concatenate(pieces, axis=0).astype(f32)


def reduce_blocks(own, other):
    count = own.shape[0]
    came = swap(other)
    parts = [own[k].astype(f32) + came[k].astype(f32) for k in range(count)]
    total = parts[0]
    for k in range(1, count):
        total = total + flip(parts[k].astype(bf16), k).astype(f32)
    return total


def local(
    hidden_in,
    out_grad,
    routes,
    attn_gain,
    w_query,
    key_projection,
    value_projection,
    w_out,
    ffn_gain,
    w_router,
    w_gate,
    w_up,
    w_down,
):
    expert = lax.axis_index("expert")
    context = lax.axis_index("context")
    count = lax.axis_size("expert")
    z = lax.axis_size("dp")
    tokens = hidden_in.shape[1]
    experts_all = EXP_DEV * count
    per_core = EXP_DEV // 2
    capacity = tokens * TOP * 5 // (4 * experts_all)
    rows = w_query.shape[0]
    piece = rows // count

    def quarter(parts):
        cut = [
            lax.dynamic_slice_in_dim(p, expert * piece, piece, axis=0).astype(bf16) for p in parts
        ]
        return jnp.concatenate(cut, axis=1)

    pad = jnp.zeros((rows, SMALL - experts_all - 2), f32)
    first_pack = quarter(
        [w_query, key_projection, value_projection, w_router, attn_gain[:, None], ffn_gain[:, None], pad]
    )
    second_pack = quarter([w_out])
    first_z = lax.all_gather(first_pack, "dp", axis=0, tiled=False)
    second_z = lax.all_gather(second_pack, "dp", axis=0, tiled=False)
    own_one, other_one = spread(first_z)
    own_two, other_two = spread(after(second_z, own_one[-1]))
    packed = assemble(own_one, other_one, context, expert)
    out_w = assemble(own_two, other_two, context, expert)
    qkv_w = packed[:, : Q_WIDTH + 2 * KV_WIDTH]
    router_w = packed[:, Q_WIDTH + 2 * KV_WIDTH :][:, :experts_all]
    small = packed[:, Q_WIDTH + 2 * KV_WIDTH :].T
    gain_one = small[experts_all].astype(f32)
    gain_two = small[experts_all + 1].astype(f32)

    def chunk(j):
        picked = slice(j, None, per_core)
        return jnp.stack(
            [
                w_gate[picked].astype(bf16),
                w_up[picked].astype(bf16),
                jnp.swapaxes(w_down[picked], 1, 2).astype(bf16),
            ],
            axis=1,
        )

    gathered = []
    for j in range(per_core):
        sent = after(chunk(j), second_z)
        gathered.append(lax.all_gather(sent, ("context", "dp"), axis=0, tiled=False))

    dy_half = after(out_grad[0], own_two[-1])
    dys_own, dys_other = spread(dy_half)

    route_t = routes[0].T
    expert_ids = jnp.arange(experts_all, dtype=jnp.int32)
    named = jnp.any(route_t[:, None, :] == expert_ids[None, :, None], axis=0)
    earlier = (
        jnp.arange(tokens, dtype=jnp.int32)[:, None] < jnp.arange(tokens, dtype=jnp.int32)[None, :]
    )
    ranks = dot(named.astype(bf16), earlier.astype(bf16))
    slot_code = jnp.where(named & (ranks < capacity), ranks, -1.0)

    inputs_f = hidden_in[0].astype(f32)
    scale_one, norm_one = norm_parts(inputs_f)
    act_one = (norm_one * gain_one).astype(bf16)
    qkv = dot(act_one, qkv_w)
    cosine, sine = rope_tables(context * tokens, tokens, HEAD_SIZE)
    cos_wide = jnp.concatenate([cosine, cosine], axis=1)
    sin_wide = jnp.concatenate([-sine, sine], axis=1)
    key = rotate(
        qkv[:, Q_WIDTH : Q_WIDTH + KV_WIDTH].reshape(tokens, KEY_VALUE_HEADS, HEAD_SIZE),
        cosine,
        sine,
    ).astype(bf16)
    value = qkv[:, Q_WIDTH + KV_WIDTH :].astype(bf16)
    near = jnp.concatenate([key.reshape(tokens, KV_WIDTH), value], axis=1)
    far = lax.ppermute(near, "context", [(0, 1)])
    where = context[None].astype(jnp.int32)
    query, mixed, logs = attention(where, qkv, near, far, cos_wide, sin_wide)
    resid_one = inputs_f + dot(mixed, out_w)
    scale_two, norm_two = norm_parts(resid_one)
    act_two = (norm_two * gain_two).astype(bf16)

    logits = dot(router_w, act_two, ((0,), (1,)))
    shown = jnp.where(named, logits, mask_fill)
    exped = jnp.where(named, jnp.exp(shown - jnp.max(shown, axis=0, keepdims=True)), 0.0)
    gates = exped / jnp.sum(exped, axis=0, keepdims=True)
    gates_high = gates.astype(bf16)
    gates_low = (gates - gates_high.astype(f32)).astype(bf16)
    meta = jnp.concatenate([gates_high, gates_low, slot_code.astype(bf16)], axis=1)
    acts_own, acts_other = spread(jnp.concatenate([act_two, meta], axis=0))

    sums, shares = (), []
    place = jnp.stack([expert * EXP_DEV + context * per_core, context]).astype(jnp.int32)
    step = jnp.array([1, 0], jnp.int32)
    for j in range(per_core):
        *sums, x, gdy, hidden, dgate, dup = run_expert(
            acts_own + acts_other, dys_own + dys_other, gathered[j], place, capacity, sums
        )
        grads = weight_grads(x, gdy, hidden, dgate, dup, z, rows)
        place = after(place + step, grads)
        shares.append(lax.psum_scatter(grads, "dp", scatter_dimension=0, tiled=False))
    y_own, y_other, d_own, d_other = sums
    dact = reduce_blocks(d_own, d_other)
    y_other = after(y_other, dact)
    block_out = (resid_one + reduce_blocks(y_own, y_other)).astype(bf16)[None]

    dy = out_grad[0].astype(f32)
    dgates = dact[tokens:, :tokens] + dact[tokens:, tokens : 2 * tokens]
    dlogits = (gates * (dgates - jnp.sum(gates * dgates, axis=0, keepdims=True))).astype(bf16)
    dact_two = dact[:tokens] + dot(dlogits, router_w, ((0,), (1,)))
    grad_router = dot(act_two, dlogits, ((0,), (1,)))
    grad_gain_two = jnp.sum(dact_two * norm_two, axis=0)
    dn2 = dact_two * gain_two
    dresid = dy + scale_two * (dn2 - norm_two * jnp.mean(dn2 * norm_two, axis=-1, keepdims=True))
    dresid_b = dresid.astype(bf16)
    grad_out = reduce_dense(dot(mixed, dresid_b, ((0,), (0,))), context, expert)
    dmixed = dot(dresid_b, out_w, ((1,), (1,))).astype(bf16)

    dquery, dkey_near, dvalue_near, dkey_far, dvalue_far = attention_back(
        where, query, dmixed, near, far, logs, cos_wide, sin_wide
    )
    sent = jnp.concatenate([dkey_far, dvalue_far], axis=1).astype(bf16)
    came = lax.ppermute(sent, "context", [(1, 0)]).astype(f32)
    dkey_r = (dkey_near + came[:, :KV_WIDTH]).reshape(tokens, KEY_VALUE_HEADS, HEAD_SIZE)
    dkey = rotate(dkey_r, cosine, -sine).astype(bf16).reshape(tokens, KV_WIDTH)
    dvalue = dvalue_near + came[:, KV_WIDTH:]
    dqkv = jnp.concatenate([dquery, dkey, dvalue.astype(bf16)], axis=1)
    dact_one = dot(dqkv, qkv_w, ((1,), (1,)))
    grad_qkv = dot(act_one, dqkv, ((0,), (0,)))
    grad_gain_one = jnp.sum(dact_one * norm_one, axis=0)
    dn1 = dact_one * gain_one
    grad_in = dresid + scale_one * (dn1 - norm_one * jnp.mean(dn1 * norm_one, axis=-1, keepdims=True))
    grad_small = jnp.concatenate(
        [
            grad_router,
            grad_gain_one[:, None],
            grad_gain_two[:, None],
            jnp.zeros((MODEL_WIDTH, SMALL - experts_all - 2), f32),
        ],
        axis=1,
    )
    first = reduce_dense(jnp.concatenate([grad_qkv, grad_small], axis=1), context, expert)
    kv_at = Q_WIDTH + KV_WIDTH
    small_at = kv_at + KV_WIDTH

    finals = []
    for share in shares:
        keep = lax.dynamic_index_in_dim(share, context, 0, keepdims=False)
        came = swap(lax.dynamic_index_in_dim(share, 1 - context, 0, keepdims=False))
        finals.append((jnp.where(context == 0, keep, came), jnp.where(context == 0, came, keep)))
    stacked = jnp.stack([f[c] for c in range(2) for f in finals])
    stacked = stacked.astype(f32)
    return (
        block_out,
        grad_in[None],
        first[:, small_at + experts_all],
        first[:, :Q_WIDTH],
        first[:, Q_WIDTH:kv_at],
        first[:, kv_at:small_at],
        grad_out,
        first[:, small_at + experts_all + 1],
        first[:, small_at : small_at + experts_all],
        stacked[:, 0],
        stacked[:, 1],
        jnp.swapaxes(stacked[:, 2], 1, 2),
    )


def solution(mesh):
    tokens_at = P(("expert", "dp"), "context", None)
    vector = P(("context", "dp"))
    matrix = P(("context", "dp"), None)
    wide = P("expert", ("context", "dp"), None)
    down = P("expert", None, ("context", "dp"))
    return jax.shard_map(
        local,
        mesh=mesh,
        in_specs=(
            tokens_at,
            tokens_at,
            tokens_at,
            vector,
            matrix,
            matrix,
            matrix,
            matrix,
            vector,
            matrix,
            wide,
            wide,
            down,
        ),
        out_specs=(
            tokens_at,
            tokens_at,
            vector,
            matrix,
            matrix,
            matrix,
            matrix,
            vector,
            matrix,
            wide,
            wide,
            down,
        ),
        check_vma=False,
    )
```

```python
import functools
import math

import jax
import jax.numpy as jnp
from jax import lax
from jax.experimental import pallas as pl
from jax.experimental.pallas import tpu as pltpu
from jax.sharding import PartitionSpec as P

MODEL_WIDTH = 1536
QUERY_HEADS = 12
KEY_VALUE_HEADS = 2
HEAD_SIZE = 128
FF = 768
TOP = 4
EXP_DEV = 4
GROUP = QUERY_HEADS // KEY_VALUE_HEADS
Q_WIDTH = QUERY_HEADS * HEAD_SIZE
KV_WIDTH = KEY_VALUE_HEADS * HEAD_SIZE
SMALL = 128

norm_eps = 1e-06
rope_base = 1000000.0
mask_fill = -1e30
bf16 = jnp.bfloat16
f32 = jnp.float32
VMEM_LIMIT = 60 * 1024 * 1024


COST_SCALE = 1


def cost(flops, bytes_accessed, transcendentals):
    return pl.CostEstimate(
        flops=flops // COST_SCALE,
        bytes_accessed=bytes_accessed // COST_SCALE,
        transcendentals=transcendentals // COST_SCALE,
    )


def dot(a, b, dims=((1,), (0,))):
    return lax.dot_general(a, b, (dims, ((), ())), preferred_element_type=f32)


def after(value, *others):
    return lax.optimization_barrier((value,) + others)[0]


def tie(*values):
    return lax.optimization_barrier(values)


def flip(value, step):
    count = lax.axis_size("expert")
    return lax.ppermute(value, "expert", [(i, i ^ step) for i in range(count)])


def swap(value):
    return lax.ppermute(value, "context", [(0, 1), (1, 0)])


def rope_tables(start_pos, length, head_dim):
    half_dim = head_dim // 2
    freqs = rope_base ** (-(2.0 * jnp.arange(half_dim, dtype=f32)) / head_dim)
    places = (start_pos + jnp.arange(length, dtype=jnp.int32)).astype(f32)
    angles = places[:, None] * freqs[None, :]
    return (jnp.cos(angles), jnp.sin(angles))


def rotate(heads, cosine, sine):
    half_dim = heads.shape[-1] // 2
    a = heads[..., :half_dim]
    b = heads[..., half_dim:]
    c = cosine[:, None, :]
    s = sine[:, None, :]
    return jnp.concatenate([a * c - b * s, b * c + a * s], axis=-1)


def norm_parts(values):
    scale = lax.rsqrt(jnp.mean(values * values, axis=-1, keepdims=True) + norm_eps)
    return scale, values * scale


def assemble(own, other, context, expert):
    count = len(own)
    z, r, n = own[0].shape
    if r % 16 != 0:
        blocks = jnp.stack([jnp.stack(own), jnp.stack(other)])
        order = jnp.arange(count) ^ expert
        blocks = jnp.take(blocks, order, axis=1)
        blocks = jnp.take(blocks, jnp.arange(2) ^ context, axis=0)
        return jnp.transpose(blocks, (0, 2, 1, 3, 4)).reshape(2 * z * count * r, n)

    def kernel(place, *refs):
        sources, out, sems = refs[: 2 * count], refs[2 * count], refs[2 * count + 1]
        copies = []
        for k in range(count):
            for half in range(2):
                at = place[0] if half == 0 else 1 - place[0]
                copies.append(
                    pltpu.make_async_copy(
                        sources[half * count + k],
                        out.at[at, :, jnp.bitwise_xor(place[1], k)],
                        sems.at[half * count + k],
                    )
                )
        for copy in copies:
            copy.start()
        for copy in copies:
            copy.wait()

    size = 2 * z * count * r * n * 2
    shape = (2, z, count, r, n)
    out = pl.pallas_call(
        kernel,
        out_shape=jax.ShapeDtypeStruct(shape, bf16),
        grid_spec=pltpu.PrefetchScalarGridSpec(
            num_scalar_prefetch=1,
            grid=(1,),
            in_specs=[pl.BlockSpec(memory_space=pl.ANY)] * (2 * count),
            out_specs=pl.BlockSpec(shape, lambda i, place: (0, 0, 0, 0, 0)),
            scratch_shapes=[pltpu.SemaphoreType.DMA((2 * count,))],
        ),
        compiler_params=pltpu.CompilerParams(vmem_limit_bytes=VMEM_LIMIT),
        cost_estimate=cost(flops=0, bytes_accessed=2 * size, transcendentals=0),
        name="assemble",
    )(jnp.stack([context, expert]).astype(jnp.int32), *own, *other)
    return out.reshape(2 * z * count * r, n)


def halves_of(size):
    return size // 2 if size < 32 else size // 32 * 16


def fourth_block(one, two, *later):
    cut = halves_of(one.shape[0])
    first, second = flip(after(one[:cut], *later), 2), flip(after(two[cut:], *later), 1)
    return jnp.concatenate([first, second], axis=0)


def gather_blocks(block):
    count = lax.axis_size("expert")
    if count != 4:
        return [block] + [flip(block, k) for k in range(1, count)]
    one, two = flip(block, 1), flip(block, 2)
    return [block, one, two, fourth_block(one, two)]


def spread(block):
    own = gather_blocks(block)
    return own, [swap(b) for b in own]


def scatter_blocks(parts, before=(), between=(), finish=()):
    count = lax.axis_size("expert")
    if count != 4:
        came = [flip(after(parts[k], *before), k) for k in range(1, count)]
        return add_all(parts[0], came), came, came
    cut = halves_of(parts[0].shape[0])
    top, bottom = [p[:cut] for p in parts], [p[cut:] for p in parts]
    top_sent = after(jnp.stack([top[1], top[3]]), *before)
    bottom_sent = after(jnp.stack([bottom[2], bottom[3]]), *before)
    top_came, bottom_came = flip(top_sent, 1), flip(bottom_sent, 2)
    top_next = add_all(top[2], [top_came[1]]).astype(bf16)
    bottom_next = add_all(bottom[1], [bottom_came[1]]).astype(bf16)
    top_last = after(flip(after(top_next, *between), 2), *finish)
    bottom_last = flip(after(bottom_next, *between), 1)
    total = jnp.concatenate(
        [
            add_all(top[0], [top_came[0], top_last]),
            add_all(bottom[0], [bottom_came[0], bottom_last]),
        ],
        axis=0,
    )
    return total, [top_came, bottom_came], [top_last, bottom_last]


GELU_C = math.sqrt(2.0 / math.pi)


def expert_kernel(count, tokens, capacity, place, *refs):
    acts, dys = refs[: 2 * count], refs[2 * count : 4 * count]
    w_ref, refs = refs[4 * count], refs[4 * count + 1 :]
    earlier, refs = refs[: len(refs) - 12], refs[len(refs) - 12 :]
    y_refs, d_refs, (x_ref, gdy_ref, h_ref, dg_ref, du_ref, abuf, dbuf, sems) = refs[:2], refs[2:4], refs[4:]
    step = pl.program_id(0)
    slot = lax.rem(step, 2)

    def copies(k, at):
        out = []
        for s in range(2):
            out.append(pltpu.make_async_copy(acts[s * count + k], abuf.at[at, s], sems.at[at, s]))
            out.append(pltpu.make_async_copy(dys[s * count + k], dbuf.at[at, s], sems.at[at, 2 + s]))
        return out

    @pl.when(step == 0)
    def _():
        for c in copies(0, 0):
            c.start()

    for k in range(1, count):

        @pl.when(step == k - 1)
        def _(k=k):
            for c in copies(k, k % 2):
                c.start()

    for k in range(count):

        @pl.when(step == k)
        def _(k=k):
            for c in copies(k, k % 2):
                c.wait()

    row = place[0]
    extra = abuf.shape[2] - tokens
    row_ids = lax.broadcasted_iota(jnp.int32, (extra, 3 * tokens), 0)
    slot_ids = lax.broadcasted_iota(jnp.int32, (capacity, tokens), 0).astype(f32)
    hits = []
    gate_cols = []
    for s in range(2):
        meta = abuf[slot, s, tokens:, :].astype(f32)
        line = jnp.sum(jnp.where(row_ids == row, meta, 0.0), axis=0, keepdims=True)
        gate_line = line[:, :tokens] + line[:, tokens : 2 * tokens]
        hit = slot_ids == line[:, 2 * tokens :]
        hits.append(hit)
        gate_col = jnp.sum(jnp.where(hit, gate_line, 0.0), axis=1, keepdims=True)
        gate_cols.append(gate_col)
        one = jnp.where(hit, 1.0, 0.0).astype(bf16)
        at = pl.ds(s * capacity, capacity)
        x_ref[at, :] = dot(one, abuf[slot, s, :tokens, :]).astype(bf16)
        gdy_ref[at, :] = dot(one, dbuf[slot, s]).astype(bf16)
    gate_col = jnp.concatenate(gate_cols, axis=0)
    wide = w_ref.shape[0] * w_ref.shape[3]
    w_gate = w_ref[:, 0, 0].reshape(wide, FF)
    w_up = w_ref[:, 0, 1].reshape(wide, FF)
    w_down = w_ref[:, 0, 2].reshape(wide, FF)
    x = x_ref[...]
    dy = gdy_ref[...]
    gate_h = dot(x, w_gate)
    up_h = dot(x, w_up)
    back = dot(dy, w_down)
    square = gate_h * gate_h
    tanh = jnp.tanh(GELU_C * gate_h * (1.0 + 0.044715 * square))
    half = 0.5 * (1.0 + tanh)
    gelu = gate_h * half
    slope = half + 0.5 * gate_h * (1.0 - tanh * tanh) * (GELU_C * (1.0 + 3 * 0.044715 * square))
    hidden = (gelu * up_h).astype(bf16)
    dgate_col = jnp.sum(hidden.astype(f32) * back, axis=1, keepdims=True)
    dhidden = back * gate_col
    dgate_h = (dhidden * up_h * slope).astype(bf16)
    dup_h = (dhidden * gelu).astype(bf16)
    h_ref[...] = hidden
    dg_ref[...] = dgate_h
    du_ref[...] = dup_h
    gdy_ref[...] = (dy.astype(f32) * gate_col).astype(bf16)
    result = (dot(hidden, w_down, ((1,), (1,))) * gate_col).astype(bf16)
    dx = (dot(dgate_h, w_gate, ((1,), (1,))) + dot(dup_h, w_up, ((1,), (1,)))).astype(bf16)
    for s in range(2):
        one = jnp.where(hits[s], 1.0, 0.0).astype(bf16)
        rows = slice(s * capacity, (s + 1) * capacity)
        y = dot(one, result[rows], ((0,), (0,)))
        d = dot(one, dx[rows], ((0,), (0,)))
        line = jnp.sum(jnp.where(hits[s], dgate_col[rows], 0.0), axis=0, keepdims=True)
        high = line.astype(bf16).astype(f32)
        line = jnp.concatenate([high, line - high, jnp.zeros_like(high)], axis=1)
        line = jnp.where(row_ids == row, line, 0.0)
        if earlier:
            y = y + earlier[s][0].astype(f32)
            d = d + earlier[2 + s][0, :tokens].astype(f32)
            line = line + earlier[2 + s][0, tokens:].astype(f32)
        y_refs[s][0] = y.astype(bf16)
        d_refs[s][0, :tokens] = d.astype(bf16)
        d_refs[s][0, tokens:] = line.astype(bf16)


def run_expert(acts, dys, weights, place, capacity, earlier=()):
    count = len(acts) // 2
    tokens = dys[0].shape[0]
    rows = acts[0].shape[0]
    cz, _, _, local, _ = weights.shape
    slots = 2 * capacity
    total = count * slots

    def row_block(width):
        return pl.BlockSpec((slots, width), lambda i, place: (i, 0))

    macs = total * (9 * MODEL_WIDTH * FF - 3 * MODEL_WIDTH * FF + 4 * tokens * MODEL_WIDTH)
    moved = 2 * (
        4 * count * (rows + tokens) * MODEL_WIDTH + total * (2 * MODEL_WIDTH + 3 * FF) + 3 * MODEL_WIDTH * FF
    )
    sums = [pl.BlockSpec((1, n, MODEL_WIDTH), lambda i, place: (i, 0, 0)) for n in (tokens, tokens, rows, rows)]
    return pl.pallas_call(
        functools.partial(expert_kernel, count, tokens, capacity),
        out_shape=(
            jax.ShapeDtypeStruct((count, tokens, MODEL_WIDTH), bf16),
            jax.ShapeDtypeStruct((count, tokens, MODEL_WIDTH), bf16),
            jax.ShapeDtypeStruct((count, rows, MODEL_WIDTH), bf16),
            jax.ShapeDtypeStruct((count, rows, MODEL_WIDTH), bf16),
            jax.ShapeDtypeStruct((total, MODEL_WIDTH), bf16),
            jax.ShapeDtypeStruct((total, MODEL_WIDTH), bf16),
            jax.ShapeDtypeStruct((total, FF), bf16),
            jax.ShapeDtypeStruct((total, FF), bf16),
            jax.ShapeDtypeStruct((total, FF), bf16),
        ),
        grid_spec=pltpu.PrefetchScalarGridSpec(
            num_scalar_prefetch=1,
            grid=(count,),
            in_specs=[pl.BlockSpec(memory_space=pl.ANY)] * (4 * count)
            + [
                pl.BlockSpec(
                    (cz, 1, 3, local, FF),
                    lambda i, place: (0, place[1], 0, 0, 0),
                    pipeline_mode=pl.Buffered(1),
                )
            ]
            + (sums if earlier else []),
            out_specs=(
                *sums,
                row_block(MODEL_WIDTH),
                row_block(MODEL_WIDTH),
                row_block(FF),
                row_block(FF),
                row_block(FF),
            ),
            scratch_shapes=[
                pltpu.VMEM((2, 2, rows, MODEL_WIDTH), bf16),
                pltpu.VMEM((2, 2, tokens, MODEL_WIDTH), bf16),
                pltpu.SemaphoreType.DMA((2, 4)),
            ],
        ),
        compiler_params=pltpu.CompilerParams(
            dimension_semantics=("arbitrary",), vmem_limit_bytes=VMEM_LIMIT
        ),
        cost_estimate=cost(
            flops=2 * macs, bytes_accessed=moved, transcendentals=total * FF
        ),
        name="experts",
    )(place, *acts, *dys, weights, *earlier)


def weight_grad_kernel(x_ref, gdy_ref, h_ref, dg_ref, du_ref, out_ref):
    shape = (out_ref.shape[0], out_ref.shape[3], FF)
    x = x_ref[...]
    first = ((0,), (0,))
    out_ref[:, 0, 0] = dot(x, dg_ref[...], first).astype(bf16).reshape(shape)
    out_ref[:, 0, 1] = dot(x, du_ref[...], first).astype(bf16).reshape(shape)
    out_ref[:, 0, 2] = dot(gdy_ref[...], h_ref[...], first).astype(bf16).reshape(shape)


def weight_grads(x, gdy, hidden, dgate, dup, z, local):
    total = x.shape[0]
    wide = 384
    per = MODEL_WIDTH // 2 // wide
    full = pl.BlockSpec((total, FF), lambda i: (0, 0))
    column = pl.BlockSpec((total, wide), lambda i: (0, i))
    return pl.pallas_call(
        weight_grad_kernel,
        out_shape=jax.ShapeDtypeStruct((z, 2, 3, local, FF), bf16),
        grid=(MODEL_WIDTH // wide,),
        in_specs=[column, column, full, full, full],
        out_specs=pl.BlockSpec(
            (wide // local, 1, 3, local, FF), lambda i: (lax.rem(i, per), lax.div(i, per), 0, 0, 0)
        ),
        compiler_params=pltpu.CompilerParams(
            dimension_semantics=("arbitrary",), vmem_limit_bytes=VMEM_LIMIT
        ),
        cost_estimate=cost(
            flops=6 * total * MODEL_WIDTH * FF,
            bytes_accessed=2 * (total * (2 * MODEL_WIDTH + 3 * FF) + 3 * MODEL_WIDTH * FF),
            transcendentals=0,
        ),
        name="weight_grads",
    )(x, gdy, hidden, dgate, dup)


SCORE = math.log2(math.e) / math.sqrt(HEAD_SIZE)
STRIP = 256


def roll_half(x):
    return pltpu.roll(x, HEAD_SIZE // 2, 1)


def causal(strip):
    shape = ((strip + 1) * STRIP, STRIP)
    key = lax.broadcasted_iota(jnp.int32, shape, 0)
    return key <= lax.broadcasted_iota(jnp.int32, shape, 1) + strip * STRIP


def attend_kernel(place, q_ref, ko_ref, vo_ref, kr_ref, vr_ref, cos_ref, sin_ref, rot_ref, mix_ref, log_ref):
    q = q_ref[...]
    rot_ref[...] = (q * cos_ref[...] + roll_half(q) * sin_ref[...]).astype(bf16)
    last = ((1,), (1,))
    first = ((0,), (0,))
    for r in range(q_ref.shape[0] // STRIP):
        rows = pl.ds(r * STRIP, STRIP)
        seen = (r + 1) * STRIP
        q = rot_ref[rows, :]
        far = jnp.where(place[0] > 0, dot(kr_ref[...], q, last), mask_fill)
        near = jnp.where(causal(r), dot(ko_ref[:seen, :], q, last), mask_fill)
        peak = jnp.maximum(
            jnp.max(far, axis=0, keepdims=True), jnp.max(near, axis=0, keepdims=True)
        )
        peak = peak * SCORE
        far = jnp.exp2(far * SCORE - peak)
        near = jnp.exp2(near * SCORE - peak)
        total = jnp.sum(far, axis=0, keepdims=True) + jnp.sum(near, axis=0, keepdims=True)
        out = dot(vr_ref[...], far.astype(bf16), first)
        out = out + dot(vo_ref[:seen, :], near.astype(bf16), first)
        mix_ref[rows, :] = (out / total).T.astype(bf16)
        log_ref[0, :, rows] = peak + jnp.log2(total)


def key_value_kernel(x_ref, cos_ref, sin_ref, out_ref):
    for h in range(KEY_VALUE_HEADS):
        at = pl.ds(h * HEAD_SIZE, HEAD_SIZE)
        x = x_ref[:, at]
        out_ref[:, at] = (x * cos_ref[...] + roll_half(x) * sin_ref[...]).astype(bf16)
    out_ref[:, KV_WIDTH:] = x_ref[:, KV_WIDTH:].astype(bf16)


def key_value(qkv, cosine, sine):
    tokens = qkv.shape[0]
    table = pl.BlockSpec((tokens, HEAD_SIZE), lambda i: (0, 0))
    return pl.pallas_call(
        key_value_kernel,
        out_shape=jax.ShapeDtypeStruct((tokens, 2 * KV_WIDTH), bf16),
        grid=(1,),
        in_specs=[
            pl.BlockSpec((tokens, 2 * KV_WIDTH), lambda i: (0, Q_WIDTH // (2 * KV_WIDTH))),
            table,
            table,
        ],
        out_specs=pl.BlockSpec((tokens, 2 * KV_WIDTH), lambda i: (0, 0)),
        cost_estimate=cost(
            flops=tokens * KV_WIDTH * 4, bytes_accessed=tokens * KV_WIDTH * 14, transcendentals=0
        ),
        name="key_value",
    )(qkv, cosine, sine)


def key_value_back_kernel(near_ref, came_ref, cos_ref, sin_ref, out_ref):
    for h in range(KEY_VALUE_HEADS):
        at = pl.ds(h * HEAD_SIZE, HEAD_SIZE)
        x = near_ref[:, at] + came_ref[:, at].astype(f32)
        out_ref[:, at] = (x * cos_ref[...] - roll_half(x) * sin_ref[...]).astype(bf16)
    out_ref[:, KV_WIDTH:] = (
        near_ref[:, KV_WIDTH:] + came_ref[:, KV_WIDTH:].astype(f32)
    ).astype(bf16)


def key_value_back(near, came, cosine, sine):
    tokens = near.shape[0]
    return pl.pallas_call(
        key_value_back_kernel,
        out_shape=jax.ShapeDtypeStruct((tokens, 2 * KV_WIDTH), bf16),
        cost_estimate=cost(
            flops=tokens * KV_WIDTH * 6, bytes_accessed=tokens * KV_WIDTH * 18, transcendentals=0
        ),
        name="key_value_back",
    )(near, came, cosine, sine)


def attention_specs(tokens):
    head = pl.BlockSpec((tokens, HEAD_SIZE), lambda h, place: (0, h))
    key = pl.BlockSpec((tokens, HEAD_SIZE), lambda h, place: (0, h // GROUP))
    value = pl.BlockSpec((tokens, HEAD_SIZE), lambda h, place: (0, KEY_VALUE_HEADS + h // GROUP))
    table = pl.BlockSpec((tokens, HEAD_SIZE), lambda h, place: (0, 0))
    log = pl.BlockSpec((1, 1, tokens), lambda h, place: (h, 0, 0))
    return head, key, value, table, log


def attention(context, qkv, near, far, cosine, sine):
    tokens = qkv.shape[0]
    head, key, value, table, log = attention_specs(tokens)
    pairs = 2 * tokens * tokens * QUERY_HEADS
    return pl.pallas_call(
        attend_kernel,
        out_shape=(
            jax.ShapeDtypeStruct((tokens, Q_WIDTH), bf16),
            jax.ShapeDtypeStruct((tokens, Q_WIDTH), bf16),
            jax.ShapeDtypeStruct((QUERY_HEADS, 1, tokens), f32),
        ),
        grid_spec=pltpu.PrefetchScalarGridSpec(
            num_scalar_prefetch=1,
            grid=(QUERY_HEADS,),
            in_specs=[head, key, value, key, value, table, table],
            out_specs=(head, head, log),
        ),
        compiler_params=pltpu.CompilerParams(
            dimension_semantics=("arbitrary",), vmem_limit_bytes=VMEM_LIMIT
        ),
        cost_estimate=cost(
            flops=4 * pairs * HEAD_SIZE, bytes_accessed=tokens * Q_WIDTH * 10, transcendentals=pairs
        ),
        name="attention",
    )(context, qkv, near, near, far, far, cosine, sine)


def attend_back_kernel(
    place, q_ref, dout_ref, ko_ref, vo_ref, kr_ref, vr_ref, log_ref, cos_ref, sin_ref,
    dq_ref, near_ref, far_ref, dko_ref, dvo_ref, dkr_ref, dvr_ref,
):
    last = ((1,), (1,))
    first = ((0,), (0,))
    scale = 1.0 / math.sqrt(HEAD_SIZE)
    head = pl.program_id(0)

    @pl.when(lax.rem(head, GROUP) == 0)
    def _():
        for ref in (dko_ref, dvo_ref, dkr_ref, dvr_ref):
            ref[...] = jnp.zeros_like(ref)

    for r in range(q_ref.shape[0] // STRIP):
        rows = pl.ds(r * STRIP, STRIP)
        seen = (r + 1) * STRIP
        q = q_ref[rows, :]
        dout = dout_ref[rows, :]
        logs = log_ref[0, :, rows]
        far = jnp.where(place[0] > 0, dot(kr_ref[...], q, last), mask_fill)
        near = jnp.where(causal(r), dot(ko_ref[:seen, :], q, last), mask_fill)
        far = jnp.exp2(far * SCORE - logs)
        near = jnp.exp2(near * SCORE - logs)
        dvr_ref[...] += dot(far.astype(bf16), dout)
        dvo_ref[:seen, :] += dot(near.astype(bf16), dout)
        dfar = dot(vr_ref[...], dout, last)
        dnear = dot(vo_ref[:seen, :], dout, last)
        inner = jnp.sum(far * dfar, axis=0, keepdims=True)
        inner = inner + jnp.sum(near * dnear, axis=0, keepdims=True)
        dfar = (far * (dfar - inner)).astype(bf16)
        dnear = (near * (dnear - inner)).astype(bf16)
        dkr_ref[...] += dot(dfar, q)
        dko_ref[:seen, :] += dot(dnear, q)
        dq = dot(kr_ref[...], dfar, first) + dot(ko_ref[:seen, :], dnear, first)
        dq = dq.T * scale
        dq_ref[rows, :] = (dq * cos_ref[rows, :] - roll_half(dq) * sin_ref[rows, :]).astype(bf16)

    for h in range(KEY_VALUE_HEADS):

        @pl.when(head == (h + 1) * GROUP - 1)
        def _(h=h):
            key = pl.ds(h * HEAD_SIZE, HEAD_SIZE)
            value = pl.ds(KV_WIDTH + h * HEAD_SIZE, HEAD_SIZE)
            near_ref[:, key] = dko_ref[...] * scale
            near_ref[:, value] = dvo_ref[...]
            far_ref[:, key] = (dkr_ref[...] * scale).astype(bf16)
            far_ref[:, value] = dvr_ref[...].astype(bf16)


def attention_back(context, query, dmixed, near, far, logs, cosine, sine):
    tokens = query.shape[0]
    head, key, value, table, log = attention_specs(tokens)
    pairs = 2 * tokens * tokens * QUERY_HEADS
    side = pl.BlockSpec((tokens, 2 * KV_WIDTH), lambda h, place: (0, 0))
    return pl.pallas_call(
        attend_back_kernel,
        out_shape=(
            jax.ShapeDtypeStruct((tokens, Q_WIDTH), bf16),
            jax.ShapeDtypeStruct((tokens, 2 * KV_WIDTH), f32),
            jax.ShapeDtypeStruct((tokens, 2 * KV_WIDTH), bf16),
        ),
        grid_spec=pltpu.PrefetchScalarGridSpec(
            num_scalar_prefetch=1,
            grid=(QUERY_HEADS,),
            in_specs=[head, head, key, value, key, value, log, table, table],
            out_specs=(head, side, side),
            scratch_shapes=[pltpu.VMEM((tokens, HEAD_SIZE), f32)] * 4,
        ),
        compiler_params=pltpu.CompilerParams(
            dimension_semantics=("arbitrary",), vmem_limit_bytes=VMEM_LIMIT
        ),
        cost_estimate=cost(
            flops=10 * pairs * HEAD_SIZE, bytes_accessed=tokens * Q_WIDTH * 8, transcendentals=pairs
        ),
        name="attention_back",
    )(context, query, dmixed, near, near, far, far, logs, cosine, sine)


def swap_halves(grad, context):
    z = lax.axis_size("dp")
    count = lax.axis_size("expert")
    r = grad.shape[0] // (2 * z * count)
    grad = grad.astype(bf16).reshape(2, z, count, r, grad.shape[1])
    theirs = swap(lax.dynamic_index_in_dim(grad, 1 - context, 0, keepdims=False))
    return lax.dynamic_index_in_dim(grad, context, 0, keepdims=False), theirs


def dense_parts(halves, expert):
    out = []
    for k in range(lax.axis_size("expert")):
        sums = []
        for pair in halves:
            a, b = (lax.dynamic_index_in_dim(p, expert ^ k, 1, keepdims=False) for p in pair)
            sums.append(a.astype(f32) + b.astype(f32))
        out.append(jnp.concatenate(sums, axis=-1).astype(bf16))
    return out


def line_step(grads, step, came):
    z = lax.axis_size("dp")
    me = lax.axis_index("dp")

    def part(at, arrived):
        own = lax.dynamic_index_in_dim(grads, jnp.clip(at, 0, z - 1), 0, keepdims=False)
        return own if arrived is None else add_all(own, [arrived]).astype(bf16)

    up = part(z - step + me, came[0])
    down = part(step + me - z, came[1])
    return (
        lax.ppermute(up, "dp", [(i, i + 1) for i in range(step)]),
        lax.ppermute(down, "dp", [(i, i - 1) for i in range(z - step, z)]),
    )


def add_all(own, came):
    total = own.astype(f32)
    for c in came:
        total = total + c.astype(f32)
    return total


def finish_dense(total, expert):
    count = lax.axis_size("expert")
    share = lax.psum_scatter(total, "dp", scatter_dimension=0, tiled=False)
    blocks = jnp.stack([share] + [flip(share, k) for k in range(1, count)])
    pieces = [lax.dynamic_index_in_dim(blocks, expert ^ e, 0, keepdims=False) for e in range(count)]
    return jnp.concatenate(pieces, axis=0).astype(f32), share


def block_parts(own, other):
    came = swap(other)
    return [(own[i].astype(f32) + came[i].astype(f32)).astype(bf16) for i in range(own.shape[0])]


def local(
    hidden_in,
    out_grad,
    routes,
    attn_gain,
    w_query,
    key_projection,
    value_projection,
    w_out,
    ffn_gain,
    w_router,
    w_gate,
    w_up,
    w_down,
):
    expert = lax.axis_index("expert")
    context = lax.axis_index("context")
    count = lax.axis_size("expert")
    z = lax.axis_size("dp")
    tokens = hidden_in.shape[1]
    experts_all = EXP_DEV * count
    per_core = EXP_DEV // 2
    capacity = tokens * TOP * 5 // (4 * experts_all)
    rows = w_query.shape[0]
    piece = rows // count

    def quarter(parts):
        cut = [
            lax.dynamic_slice_in_dim(p, expert * piece, piece, axis=0).astype(bf16) for p in parts
        ]
        return jnp.concatenate(cut, axis=1)

    pad = jnp.zeros((rows, SMALL - experts_all - 2), f32)
    pack = quarter(
        [
            w_query,
            key_projection,
            value_projection,
            w_router,
            attn_gain[:, None],
            ffn_gain[:, None],
            pad,
            w_out,
        ]
    )
    dense_z = lax.all_gather(pack, "dp", axis=0, tiled=False)
    cut = Q_WIDTH + 2 * KV_WIDTH + SMALL
    own_one, other_one = spread(dense_z[..., :cut])
    dy_half = after(out_grad[0], *own_one[1:])
    dy_first = [flip(dy_half, k) for k in ((1, 2) if count == 4 else range(1, count))]
    own_two, other_two = spread(after(dense_z[..., cut:], *dy_first))
    if count == 4:
        dys_own = [dy_half, *dy_first, fourth_block(*dy_first, *own_two[1:])]
    else:
        dys_own = [dy_half, *dy_first]
    dys_other = [swap(b) for b in dys_own]
    packed = assemble(own_one, other_one, context, expert)
    qkv_w = packed[:, : Q_WIDTH + 2 * KV_WIDTH]
    router_w = packed[:, Q_WIDTH + 2 * KV_WIDTH :][:, :experts_all]
    small = packed[:, Q_WIDTH + 2 * KV_WIDTH :].T
    gain_one = small[experts_all].astype(f32)
    gain_two = small[experts_all + 1].astype(f32)

    def chunk(j):
        parts = []
        for at in range(j, EXP_DEV, per_core):
            parts += [w_gate[at], w_up[at], w_down[at].T]
        return jnp.concatenate([p.astype(bf16) for p in parts], axis=0)

    gathered = []
    for j in range(per_core):
        sent = after(chunk(j), dense_z)
        came = lax.all_gather(sent, ("context", "dp"), axis=0, tiled=False)
        gathered.append(came.reshape(2 * z, 2, 3, rows, FF))

    route_t = routes[0].T
    expert_ids = jnp.arange(experts_all, dtype=jnp.int32)
    named = jnp.any(route_t[:, None, :] == expert_ids[None, :, None], axis=0)
    earlier = (
        jnp.arange(tokens, dtype=jnp.int32)[:, None] < jnp.arange(tokens, dtype=jnp.int32)[None, :]
    )
    ranks = dot(named.astype(bf16), earlier.astype(bf16))
    slot_code = jnp.where(named & (ranks < capacity), ranks, -1.0)

    inputs_f = hidden_in[0].astype(f32)
    scale_one, norm_one = norm_parts(inputs_f)
    act_one = (norm_one * gain_one).astype(bf16)
    qkv = dot(act_one, qkv_w)
    cosine, sine = rope_tables(context * tokens, tokens, HEAD_SIZE)
    cos_wide = jnp.concatenate([cosine, cosine], axis=1)
    sin_wide = jnp.concatenate([-sine, sine], axis=1)
    near = key_value(qkv, cos_wide, sin_wide)
    far = lax.ppermute(near, "context", [(0, 1)])
    where = context[None].astype(jnp.int32)
    query, mixed, logs = attention(where, qkv, near, far, cos_wide, sin_wide)
    out_w = assemble(own_two, other_two, context, expert)
    resid_one = inputs_f + dot(mixed, out_w)
    scale_two, norm_two = norm_parts(resid_one)
    act_two = (norm_two * gain_two).astype(bf16)

    logits = dot(router_w, act_two, ((0,), (1,)))
    shown = jnp.where(named, logits, mask_fill)
    exped = jnp.where(named, jnp.exp(shown - jnp.max(shown, axis=0, keepdims=True)), 0.0)
    gates = exped / jnp.sum(exped, axis=0, keepdims=True)
    gates_high = gates.astype(bf16)
    gates_low = (gates - gates_high.astype(f32)).astype(bf16)
    meta = jnp.concatenate([gates_high, gates_low, slot_code.astype(bf16)], axis=1)
    payload = jnp.concatenate([act_two, meta], axis=0)
    acts_own, acts_other = spread(after(payload, *dys_own[1:]))

    place = jnp.stack([expert * EXP_DEV + context * per_core, context]).astype(jnp.int32)
    step = jnp.array([1, 0], jnp.int32)
    sums, shares = (), []
    for j in range(per_core):
        *sums, x, gdy, hidden, dgate, dup = run_expert(
            acts_own + acts_other, dys_own + dys_other, gathered[j], place, capacity, sums
        )
        if j == per_core - 1:
            d_parts = block_parts(sums[2], sums[3])
            x = after(x, d_parts[-1])
        grads = weight_grads(x, gdy, hidden, dgate, dup, z, rows)
        place, grads = tie(place + step, grads)
        if j == per_core - 1:
            dact, came, last = scatter_blocks(d_parts, (), (), [shares[-1], grads])
            grads, shares[-1] = tie(grads, shares[-1])
        shares.append(lax.psum_scatter(grads, "dp", scatter_dimension=0, tiled=False))
    y_parts = block_parts(sums[0], after(sums[1], *came))
    y_sum, y_came, _ = scatter_blocks(y_parts, last)

    dy = out_grad[0].astype(f32)
    dgates = dact[tokens:, :tokens] + dact[tokens:, tokens : 2 * tokens]
    dlogits = (gates * (dgates - jnp.sum(gates * dgates, axis=0, keepdims=True))).astype(bf16)
    dact_two = dact[:tokens] + dot(dlogits, router_w, ((0,), (1,)))
    grad_router = dot(act_two, dlogits, ((0,), (1,)))
    grad_gain_two = jnp.sum(dact_two * norm_two, axis=0)
    dn2 = dact_two * gain_two
    dresid = dy + scale_two * (dn2 - norm_two * jnp.mean(dn2 * norm_two, axis=-1, keepdims=True))
    dresid_b = dresid.astype(bf16)
    dmixed = dot(dresid_b, out_w, ((1,), (1,))).astype(bf16)
    out_halves = swap_halves(dot(mixed, after(dresid_b, dmixed), ((0,), (0,))), context)
    out_total, out_first, out_came = scatter_blocks(dense_parts([out_halves], expert))

    dquery, near_grad, far_grad = attention_back(
        where, query, dmixed, near, far, logs, cos_wide, sin_wide
    )
    came = lax.ppermute(after(far_grad, *y_came), "context", [(1, 0)])
    grad_query = dot(act_one, dquery, ((0,), (0,))).astype(bf16)
    dkv = key_value_back(near_grad, came, cos_wide, sin_wide)
    grad_kv = dot(act_one, dkv, ((0,), (0,))).astype(bf16)
    dact_one = dot(dquery, qkv_w[:, :Q_WIDTH], ((1,), (1,)))
    dact_one = dact_one + dot(after(dkv, grad_kv), qkv_w[:, Q_WIDTH:], ((1,), (1,)))
    grad_gain_one = jnp.sum(dact_one * norm_one, axis=0)
    dn1 = dact_one * gain_one
    grad_in = dresid + scale_one * (dn1 - norm_one * jnp.mean(dn1 * norm_one, axis=-1, keepdims=True))
    grad_small = jnp.concatenate(
        [
            grad_router,
            grad_gain_one[:, None],
            grad_gain_two[:, None],
            jnp.zeros((MODEL_WIDTH, SMALL - experts_all - 2), f32),
        ],
        axis=1,
    )
    block_out = (resid_one + y_sum).astype(bf16)[None]
    out_total, shares[-1] = tie(out_total.astype(bf16), shares[-1])
    grad_out, out_share = finish_dense(out_total, expert)
    halves = [swap_halves(grad, context) for grad in (grad_query, grad_kv)]
    first_total, _, _ = scatter_blocks(dense_parts(halves, expert), out_came)
    small_total, _, _ = scatter_blocks(dense_parts([swap_halves(grad_small, context)], expert))
    first_total = jnp.concatenate([first_total, small_total], axis=-1).astype(bf16)
    first_total, out_share = tie(first_total, out_share)
    first, _ = finish_dense(first_total, expert)
    kv_at = Q_WIDTH + KV_WIDTH
    small_at = kv_at + KV_WIDTH

    finals = []
    for share in shares:
        keep = lax.dynamic_index_in_dim(share, context, 0, keepdims=False)
        came = swap(lax.dynamic_index_in_dim(share, 1 - context, 0, keepdims=False))
        finals.append((jnp.where(context == 0, keep, came), jnp.where(context == 0, came, keep)))
    stacked = jnp.stack([f[c] for c in range(2) for f in finals])
    stacked = stacked.astype(f32)
    return (
        block_out,
        grad_in[None],
        first[:, small_at + experts_all],
        first[:, :Q_WIDTH],
        first[:, Q_WIDTH:kv_at],
        first[:, kv_at:small_at],
        grad_out,
        first[:, small_at + experts_all + 1],
        first[:, small_at : small_at + experts_all],
        stacked[:, 0],
        stacked[:, 1],
        jnp.swapaxes(stacked[:, 2], 1, 2),
    )


def solution(mesh):
    tokens_at = P(("expert", "dp"), "context", None)
    vector = P(("context", "dp"))
    matrix = P(("context", "dp"), None)
    wide = P("expert", ("context", "dp"), None)
    down = P("expert", None, ("context", "dp"))
    return jax.shard_map(
        local,
        mesh=mesh,
        in_specs=(
            tokens_at,
            tokens_at,
            tokens_at,
            vector,
            matrix,
            matrix,
            matrix,
            matrix,
            vector,
            matrix,
            wide,
            wide,
            down,
        ),
        out_specs=(
            tokens_at,
            tokens_at,
            vector,
            matrix,
            matrix,
            matrix,
            matrix,
            vector,
            matrix,
            wide,
            wide,
            down,
        ),
        check_vma=False,
    )
```

```python
import functools
import math

import jax
import jax.numpy as jnp
from jax import lax
from jax.experimental import pallas as pl
from jax.experimental.pallas import tpu as pltpu
from jax.sharding import PartitionSpec as P

MODEL_WIDTH = 1536
QUERY_HEADS = 12
KEY_VALUE_HEADS = 2
HEAD_SIZE = 128
FF = 768
TOP = 4
EXP_DEV = 4
GROUP = QUERY_HEADS // KEY_VALUE_HEADS
Q_WIDTH = QUERY_HEADS * HEAD_SIZE
KV_WIDTH = KEY_VALUE_HEADS * HEAD_SIZE
SMALL = 128

norm_eps = 1e-06
rope_base = 1000000.0
mask_fill = -1e30
bf16 = jnp.bfloat16
f32 = jnp.float32
VMEM_LIMIT = 60 * 1024 * 1024


COST_SCALE = 1


def cost(flops, bytes_accessed, transcendentals):
    return pl.CostEstimate(
        flops=flops // COST_SCALE,
        bytes_accessed=bytes_accessed // COST_SCALE,
        transcendentals=transcendentals // COST_SCALE,
    )


def dot(a, b, dims=((1,), (0,))):
    return lax.dot_general(a, b, (dims, ((), ())), preferred_element_type=f32)


def after(value, *others):
    return lax.optimization_barrier((value,) + others)[0]


def tie(*values):
    return lax.optimization_barrier(values)


def flip(value, step):
    count = lax.axis_size("expert")
    return lax.ppermute(value, "expert", [(i, i ^ step) for i in range(count)])


def swap(value):
    return lax.ppermute(value, "context", [(0, 1), (1, 0)])


def rope_tables(start_pos, length, head_dim):
    half_dim = head_dim // 2
    freqs = rope_base ** (-(2.0 * jnp.arange(half_dim, dtype=f32)) / head_dim)
    places = (start_pos + jnp.arange(length, dtype=jnp.int32)).astype(f32)
    angles = places[:, None] * freqs[None, :]
    return (jnp.cos(angles), jnp.sin(angles))


def rotate(heads, cosine, sine):
    half_dim = heads.shape[-1] // 2
    a = heads[..., :half_dim]
    b = heads[..., half_dim:]
    c = cosine[:, None, :]
    s = sine[:, None, :]
    return jnp.concatenate([a * c - b * s, b * c + a * s], axis=-1)


def norm_parts(values):
    scale = lax.rsqrt(jnp.mean(values * values, axis=-1, keepdims=True) + norm_eps)
    return scale, values * scale


def assemble(own, other, context, expert):
    count = len(own)
    z, r, n = own[0].shape
    if r % 16 != 0:
        blocks = jnp.stack([jnp.stack(own), jnp.stack(other)])
        order = jnp.arange(count) ^ expert
        blocks = jnp.take(blocks, order, axis=1)
        blocks = jnp.take(blocks, jnp.arange(2) ^ context, axis=0)
        return jnp.transpose(blocks, (0, 2, 1, 3, 4)).reshape(2 * z * count * r, n)

    def kernel(place, *refs):
        sources, out, sems = refs[: 2 * count], refs[2 * count], refs[2 * count + 1]
        copies = []
        for k in range(count):
            for half in range(2):
                at = place[0] if half == 0 else 1 - place[0]
                copies.append(
                    pltpu.make_async_copy(
                        sources[half * count + k],
                        out.at[at, :, jnp.bitwise_xor(place[1], k)],
                        sems.at[half * count + k],
                    )
                )
        for copy in copies:
            copy.start()
        for copy in copies:
            copy.wait()

    size = 2 * z * count * r * n * 2
    shape = (2, z, count, r, n)
    out = pl.pallas_call(
        kernel,
        out_shape=jax.ShapeDtypeStruct(shape, bf16),
        grid_spec=pltpu.PrefetchScalarGridSpec(
            num_scalar_prefetch=1,
            grid=(1,),
            in_specs=[pl.BlockSpec(memory_space=pl.ANY)] * (2 * count),
            out_specs=pl.BlockSpec(shape, lambda i, place: (0, 0, 0, 0, 0)),
            scratch_shapes=[pltpu.SemaphoreType.DMA((2 * count,))],
        ),
        compiler_params=pltpu.CompilerParams(vmem_limit_bytes=VMEM_LIMIT),
        cost_estimate=cost(flops=0, bytes_accessed=2 * size, transcendentals=0),
        name="assemble",
    )(jnp.stack([context, expert]).astype(jnp.int32), *own, *other)
    return out.reshape(2 * z * count * r, n)


def halves_of(size):
    return size // 2 if size < 32 else size // 32 * 16


def fourth_block(one, two):
    cut = halves_of(one.shape[0])
    return jnp.concatenate([flip(one[:cut], 2), flip(two[cut:], 1)], axis=0)


def gather_first(block):
    count = lax.axis_size("expert")
    return [flip(block, k) for k in ((1, 2) if count == 4 else range(1, count))]


def gather_second(came):
    return [fourth_block(*came)] if lax.axis_size("expert") == 4 else []


def gather_blocks(block):
    came = gather_first(block)
    return [block, *came, *gather_second(came)]


def spread(block):
    own = gather_blocks(block)
    return own, [swap(b) for b in own]


def scatter_first(parts):
    count = lax.axis_size("expert")
    if count != 4:
        return [flip(parts[k], k) for k in range(1, count)]
    cut = halves_of(parts[0].shape[0])
    top = jnp.stack([parts[1][:cut], parts[3][:cut]])
    bottom = jnp.stack([parts[2][cut:], parts[3][cut:]])
    return [flip(top, 1), flip(bottom, 2)]


def scatter_second(parts, came):
    if lax.axis_size("expert") != 4:
        return []
    cut = halves_of(parts[0].shape[0])
    top = add_all(parts[2][:cut], [came[0][1]]).astype(bf16)
    bottom = add_all(parts[1][cut:], [came[1][1]]).astype(bf16)
    return [flip(top, 2), flip(bottom, 1)]


def scatter_total(parts, came, last):
    if lax.axis_size("expert") != 4:
        return add_all(parts[0], came)
    cut = halves_of(parts[0].shape[0])
    top = add_all(parts[0][:cut], [came[0][0], last[0]])
    bottom = add_all(parts[0][cut:], [came[1][0], last[1]])
    return jnp.concatenate([top, bottom], axis=0)


def tie_lists(*lists):
    flat = iter(tie(*(v for values in lists for v in values)))
    return [[next(flat) for _ in values] for values in lists]


GELU_C = math.sqrt(2.0 / math.pi)


def expert_kernel(count, tokens, capacity, place, *refs):
    acts, dys = refs[: 2 * count], refs[2 * count : 4 * count]
    w_ref, refs = refs[4 * count], refs[4 * count + 1 :]
    earlier, refs = refs[: len(refs) - 12], refs[len(refs) - 12 :]
    y_refs, d_refs, (x_ref, gdy_ref, h_ref, dg_ref, du_ref, abuf, dbuf, sems) = refs[:2], refs[2:4], refs[4:]
    step = pl.program_id(0)
    slot = lax.rem(step, 2)

    def copies(k, at):
        out = []
        for s in range(2):
            out.append(pltpu.make_async_copy(acts[s * count + k], abuf.at[at, s], sems.at[at, s]))
            out.append(pltpu.make_async_copy(dys[s * count + k], dbuf.at[at, s], sems.at[at, 2 + s]))
        return out

    @pl.when(step == 0)
    def _():
        for c in copies(0, 0):
            c.start()

    for k in range(1, count):

        @pl.when(step == k - 1)
        def _(k=k):
            for c in copies(k, k % 2):
                c.start()

    for k in range(count):

        @pl.when(step == k)
        def _(k=k):
            for c in copies(k, k % 2):
                c.wait()

    row = place[0]
    extra = abuf.shape[2] - tokens
    row_ids = lax.broadcasted_iota(jnp.int32, (extra, 3 * tokens), 0)
    slot_ids = lax.broadcasted_iota(jnp.int32, (capacity, tokens), 0).astype(f32)
    hits = []
    gate_cols = []
    for s in range(2):
        meta = abuf[slot, s, tokens:, :].astype(f32)
        line = jnp.sum(jnp.where(row_ids == row, meta, 0.0), axis=0, keepdims=True)
        gate_line = line[:, :tokens] + line[:, tokens : 2 * tokens]
        hit = slot_ids == line[:, 2 * tokens :]
        hits.append(hit)
        gate_col = jnp.sum(jnp.where(hit, gate_line, 0.0), axis=1, keepdims=True)
        gate_cols.append(gate_col)
        one = jnp.where(hit, 1.0, 0.0).astype(bf16)
        at = pl.ds(s * capacity, capacity)
        x_ref[at, :] = dot(one, abuf[slot, s, :tokens, :]).astype(bf16)
        gdy_ref[at, :] = dot(one, dbuf[slot, s]).astype(bf16)
    gate_col = jnp.concatenate(gate_cols, axis=0)
    wide = w_ref.shape[0] * w_ref.shape[3]
    w_gate = w_ref[:, 0, 0].reshape(wide, FF)
    w_up = w_ref[:, 0, 1].reshape(wide, FF)
    w_down = w_ref[:, 0, 2].reshape(wide, FF)
    x = x_ref[...]
    dy = gdy_ref[...]
    gate_h = dot(x, w_gate)
    up_h = dot(x, w_up)
    back = dot(dy, w_down)
    square = gate_h * gate_h
    tanh = jnp.tanh(GELU_C * gate_h * (1.0 + 0.044715 * square))
    half = 0.5 * (1.0 + tanh)
    gelu = gate_h * half
    slope = half + 0.5 * gate_h * (1.0 - tanh * tanh) * (GELU_C * (1.0 + 3 * 0.044715 * square))
    hidden = (gelu * up_h).astype(bf16)
    dgate_col = jnp.sum(hidden.astype(f32) * back, axis=1, keepdims=True)
    dhidden = back * gate_col
    dgate_h = (dhidden * up_h * slope).astype(bf16)
    dup_h = (dhidden * gelu).astype(bf16)
    h_ref[...] = hidden
    dg_ref[...] = dgate_h
    du_ref[...] = dup_h
    gdy_ref[...] = (dy.astype(f32) * gate_col).astype(bf16)
    result = (dot(hidden, w_down, ((1,), (1,))) * gate_col).astype(bf16)
    dx = (dot(dgate_h, w_gate, ((1,), (1,))) + dot(dup_h, w_up, ((1,), (1,)))).astype(bf16)
    for s in range(2):
        one = jnp.where(hits[s], 1.0, 0.0).astype(bf16)
        rows = slice(s * capacity, (s + 1) * capacity)
        y = dot(one, result[rows], ((0,), (0,)))
        d = dot(one, dx[rows], ((0,), (0,)))
        line = jnp.sum(jnp.where(hits[s], dgate_col[rows], 0.0), axis=0, keepdims=True)
        high = line.astype(bf16).astype(f32)
        line = jnp.concatenate([high, line - high, jnp.zeros_like(high)], axis=1)
        line = jnp.where(row_ids == row, line, 0.0)
        if earlier:
            y = y + earlier[s][0].astype(f32)
            d = d + earlier[2 + s][0, :tokens].astype(f32)
            line = line + earlier[2 + s][0, tokens:].astype(f32)
        y_refs[s][0] = y.astype(bf16)
        d_refs[s][0, :tokens] = d.astype(bf16)
        d_refs[s][0, tokens:] = line.astype(bf16)


def run_expert(acts, dys, weights, place, capacity, earlier=()):
    count = len(acts) // 2
    tokens = dys[0].shape[0]
    rows = acts[0].shape[0]
    cz, _, _, local, _ = weights.shape
    slots = 2 * capacity
    total = count * slots

    def row_block(width):
        return pl.BlockSpec((slots, width), lambda i, place: (i, 0))

    macs = total * (9 * MODEL_WIDTH * FF - 3 * MODEL_WIDTH * FF + 4 * tokens * MODEL_WIDTH)
    moved = 2 * (
        4 * count * (rows + tokens) * MODEL_WIDTH + total * (2 * MODEL_WIDTH + 3 * FF) + 3 * MODEL_WIDTH * FF
    )
    sums = [pl.BlockSpec((1, n, MODEL_WIDTH), lambda i, place: (i, 0, 0)) for n in (tokens, tokens, rows, rows)]
    return pl.pallas_call(
        functools.partial(expert_kernel, count, tokens, capacity),
        out_shape=(
            jax.ShapeDtypeStruct((count, tokens, MODEL_WIDTH), bf16),
            jax.ShapeDtypeStruct((count, tokens, MODEL_WIDTH), bf16),
            jax.ShapeDtypeStruct((count, rows, MODEL_WIDTH), bf16),
            jax.ShapeDtypeStruct((count, rows, MODEL_WIDTH), bf16),
            jax.ShapeDtypeStruct((total, MODEL_WIDTH), bf16),
            jax.ShapeDtypeStruct((total, MODEL_WIDTH), bf16),
            jax.ShapeDtypeStruct((total, FF), bf16),
            jax.ShapeDtypeStruct((total, FF), bf16),
            jax.ShapeDtypeStruct((total, FF), bf16),
        ),
        grid_spec=pltpu.PrefetchScalarGridSpec(
            num_scalar_prefetch=1,
            grid=(count,),
            in_specs=[pl.BlockSpec(memory_space=pl.ANY)] * (4 * count)
            + [
                pl.BlockSpec(
                    (cz, 1, 3, local, FF),
                    lambda i, place: (0, place[1], 0, 0, 0),
                    pipeline_mode=pl.Buffered(1),
                )
            ]
            + (sums if earlier else []),
            out_specs=(
                *sums,
                row_block(MODEL_WIDTH),
                row_block(MODEL_WIDTH),
                row_block(FF),
                row_block(FF),
                row_block(FF),
            ),
            scratch_shapes=[
                pltpu.VMEM((2, 2, rows, MODEL_WIDTH), bf16),
                pltpu.VMEM((2, 2, tokens, MODEL_WIDTH), bf16),
                pltpu.SemaphoreType.DMA((2, 4)),
            ],
        ),
        compiler_params=pltpu.CompilerParams(
            dimension_semantics=("arbitrary",), vmem_limit_bytes=VMEM_LIMIT
        ),
        cost_estimate=cost(
            flops=2 * macs, bytes_accessed=moved, transcendentals=total * FF
        ),
        name="experts",
    )(place, *acts, *dys, weights, *earlier)


def weight_grad_kernel(per, x_ref, gdy_ref, h_ref, dg_ref, du_ref, *out_refs):
    first = ((0,), (0,))

    def write(out_ref):
        shape = (out_ref.shape[0], out_ref.shape[2], FF)
        x = x_ref[...]
        out_ref[:, 0] = dot(x, dg_ref[...], first).astype(bf16).reshape(shape)
        out_ref[:, 1] = dot(x, du_ref[...], first).astype(bf16).reshape(shape)
        out_ref[:, 2] = dot(gdy_ref[...], h_ref[...], first).astype(bf16).reshape(shape)

    if len(out_refs) == 1:
        write(out_refs[0].at[:, 0])
    else:
        for c, out_ref in enumerate(out_refs):
            pl.when(lax.div(pl.program_id(0), per) == c)(functools.partial(write, out_ref))


def weight_grads(x, gdy, hidden, dgate, dup, z, local, split):
    total = x.shape[0]
    wide = 384
    per = MODEL_WIDTH // 2 // wide
    full = pl.BlockSpec((total, FF), lambda i: (0, 0))
    column = pl.BlockSpec((total, wide), lambda i: (0, i))
    block = wide // local
    if split:
        shapes = [jax.ShapeDtypeStruct((z, 3, local, FF), bf16)] * 2
        specs = [
            pl.BlockSpec((block, 3, local, FF), lambda i: (jnp.minimum(i, per - 1), 0, 0, 0)),
            pl.BlockSpec((block, 3, local, FF), lambda i: (jnp.maximum(i - per, 0), 0, 0, 0)),
        ]
    else:
        shapes = [jax.ShapeDtypeStruct((z, 2, 3, local, FF), bf16)]
        specs = [
            pl.BlockSpec(
                (block, 1, 3, local, FF), lambda i: (lax.rem(i, per), lax.div(i, per), 0, 0, 0)
            )
        ]
    return pl.pallas_call(
        functools.partial(weight_grad_kernel, per),
        out_shape=shapes,
        grid=(MODEL_WIDTH // wide,),
        in_specs=[column, column, full, full, full],
        out_specs=specs,
        compiler_params=pltpu.CompilerParams(
            dimension_semantics=("arbitrary",), vmem_limit_bytes=VMEM_LIMIT
        ),
        cost_estimate=cost(
            flops=6 * total * MODEL_WIDTH * FF,
            bytes_accessed=2 * (total * (2 * MODEL_WIDTH + 3 * FF) + 3 * MODEL_WIDTH * FF),
            transcendentals=0,
        ),
        name="weight_grads",
    )(x, gdy, hidden, dgate, dup)


SCORE = math.log2(math.e) / math.sqrt(HEAD_SIZE)
STRIP = 256


def roll_half(x):
    return pltpu.roll(x, HEAD_SIZE // 2, 1)


def causal(strip):
    shape = ((strip + 1) * STRIP, STRIP)
    key = lax.broadcasted_iota(jnp.int32, shape, 0)
    return key <= lax.broadcasted_iota(jnp.int32, shape, 1) + strip * STRIP


def attend_kernel(place, q_ref, ko_ref, vo_ref, kr_ref, vr_ref, cos_ref, sin_ref, rot_ref, mix_ref, log_ref):
    q = q_ref[...]
    rot_ref[...] = (q * cos_ref[...] + roll_half(q) * sin_ref[...]).astype(bf16)
    last = ((1,), (1,))
    first = ((0,), (0,))
    for r in range(q_ref.shape[0] // STRIP):
        rows = pl.ds(r * STRIP, STRIP)
        seen = (r + 1) * STRIP
        q = rot_ref[rows, :]
        far = jnp.where(place[0] > 0, dot(kr_ref[...], q, last), mask_fill)
        near = jnp.where(causal(r), dot(ko_ref[:seen, :], q, last), mask_fill)
        peak = jnp.maximum(
            jnp.max(far, axis=0, keepdims=True), jnp.max(near, axis=0, keepdims=True)
        )
        peak = peak * SCORE
        far = jnp.exp2(far * SCORE - peak)
        near = jnp.exp2(near * SCORE - peak)
        total = jnp.sum(far, axis=0, keepdims=True) + jnp.sum(near, axis=0, keepdims=True)
        out = dot(vr_ref[...], far.astype(bf16), first)
        out = out + dot(vo_ref[:seen, :], near.astype(bf16), first)
        mix_ref[rows, :] = (out / total).T.astype(bf16)
        log_ref[0, :, rows] = peak + jnp.log2(total)


def key_value_kernel(x_ref, cos_ref, sin_ref, out_ref):
    for h in range(KEY_VALUE_HEADS):
        at = pl.ds(h * HEAD_SIZE, HEAD_SIZE)
        x = x_ref[:, at]
        out_ref[:, at] = (x * cos_ref[...] + roll_half(x) * sin_ref[...]).astype(bf16)
    out_ref[:, KV_WIDTH:] = x_ref[:, KV_WIDTH:].astype(bf16)


def key_value(qkv, cosine, sine):
    tokens = qkv.shape[0]
    table = pl.BlockSpec((tokens, HEAD_SIZE), lambda i: (0, 0))
    return pl.pallas_call(
        key_value_kernel,
        out_shape=jax.ShapeDtypeStruct((tokens, 2 * KV_WIDTH), bf16),
        grid=(1,),
        in_specs=[
            pl.BlockSpec((tokens, 2 * KV_WIDTH), lambda i: (0, Q_WIDTH // (2 * KV_WIDTH))),
            table,
            table,
        ],
        out_specs=pl.BlockSpec((tokens, 2 * KV_WIDTH), lambda i: (0, 0)),
        cost_estimate=cost(
            flops=tokens * KV_WIDTH * 4, bytes_accessed=tokens * KV_WIDTH * 14, transcendentals=0
        ),
        name="key_value",
    )(qkv, cosine, sine)


def key_value_back_kernel(near_ref, came_ref, cos_ref, sin_ref, out_ref):
    for h in range(KEY_VALUE_HEADS):
        at = pl.ds(h * HEAD_SIZE, HEAD_SIZE)
        x = near_ref[:, at] + came_ref[:, at].astype(f32)
        out_ref[:, at] = (x * cos_ref[...] - roll_half(x) * sin_ref[...]).astype(bf16)
    out_ref[:, KV_WIDTH:] = (
        near_ref[:, KV_WIDTH:] + came_ref[:, KV_WIDTH:].astype(f32)
    ).astype(bf16)


def key_value_back(near, came, cosine, sine):
    tokens = near.shape[0]
    return pl.pallas_call(
        key_value_back_kernel,
        out_shape=jax.ShapeDtypeStruct((tokens, 2 * KV_WIDTH), bf16),
        cost_estimate=cost(
            flops=tokens * KV_WIDTH * 6, bytes_accessed=tokens * KV_WIDTH * 18, transcendentals=0
        ),
        name="key_value_back",
    )(near, came, cosine, sine)


def attention_specs(tokens):
    head = pl.BlockSpec((tokens, HEAD_SIZE), lambda h, place: (0, h))
    key = pl.BlockSpec((tokens, HEAD_SIZE), lambda h, place: (0, h // GROUP))
    value = pl.BlockSpec((tokens, HEAD_SIZE), lambda h, place: (0, KEY_VALUE_HEADS + h // GROUP))
    table = pl.BlockSpec((tokens, HEAD_SIZE), lambda h, place: (0, 0))
    log = pl.BlockSpec((1, 1, tokens), lambda h, place: (h, 0, 0))
    return head, key, value, table, log


def attention(context, qkv, near, far, cosine, sine):
    tokens = qkv.shape[0]
    head, key, value, table, log = attention_specs(tokens)
    pairs = 2 * tokens * tokens * QUERY_HEADS
    return pl.pallas_call(
        attend_kernel,
        out_shape=(
            jax.ShapeDtypeStruct((tokens, Q_WIDTH), bf16),
            jax.ShapeDtypeStruct((tokens, Q_WIDTH), bf16),
            jax.ShapeDtypeStruct((QUERY_HEADS, 1, tokens), f32),
        ),
        grid_spec=pltpu.PrefetchScalarGridSpec(
            num_scalar_prefetch=1,
            grid=(QUERY_HEADS,),
            in_specs=[head, key, value, key, value, table, table],
            out_specs=(head, head, log),
        ),
        compiler_params=pltpu.CompilerParams(
            dimension_semantics=("arbitrary",), vmem_limit_bytes=VMEM_LIMIT
        ),
        cost_estimate=cost(
            flops=4 * pairs * HEAD_SIZE, bytes_accessed=tokens * Q_WIDTH * 10, transcendentals=pairs
        ),
        name="attention",
    )(context, qkv, near, near, far, far, cosine, sine)


def attend_back_kernel(
    place, q_ref, dout_ref, ko_ref, vo_ref, kr_ref, vr_ref, log_ref, cos_ref, sin_ref,
    dq_ref, near_ref, far_ref, dko_ref, dvo_ref, dkr_ref, dvr_ref,
):
    last = ((1,), (1,))
    first = ((0,), (0,))
    scale = 1.0 / math.sqrt(HEAD_SIZE)
    head = pl.program_id(0)

    @pl.when(lax.rem(head, GROUP) == 0)
    def _():
        for ref in (dko_ref, dvo_ref, dkr_ref, dvr_ref):
            ref[...] = jnp.zeros_like(ref)

    for r in range(q_ref.shape[0] // STRIP):
        rows = pl.ds(r * STRIP, STRIP)
        seen = (r + 1) * STRIP
        q = q_ref[rows, :]
        dout = dout_ref[rows, :]
        logs = log_ref[0, :, rows]
        far = jnp.where(place[0] > 0, dot(kr_ref[...], q, last), mask_fill)
        near = jnp.where(causal(r), dot(ko_ref[:seen, :], q, last), mask_fill)
        far = jnp.exp2(far * SCORE - logs)
        near = jnp.exp2(near * SCORE - logs)
        dvr_ref[...] += dot(far.astype(bf16), dout)
        dvo_ref[:seen, :] += dot(near.astype(bf16), dout)
        dfar = dot(vr_ref[...], dout, last)
        dnear = dot(vo_ref[:seen, :], dout, last)
        inner = jnp.sum(far * dfar, axis=0, keepdims=True)
        inner = inner + jnp.sum(near * dnear, axis=0, keepdims=True)
        dfar = (far * (dfar - inner)).astype(bf16)
        dnear = (near * (dnear - inner)).astype(bf16)
        dkr_ref[...] += dot(dfar, q)
        dko_ref[:seen, :] += dot(dnear, q)
        dq = dot(kr_ref[...], dfar, first) + dot(ko_ref[:seen, :], dnear, first)
        dq = dq.T * scale
        dq_ref[rows, :] = (dq * cos_ref[rows, :] - roll_half(dq) * sin_ref[rows, :]).astype(bf16)

    for h in range(KEY_VALUE_HEADS):

        @pl.when(head == (h + 1) * GROUP - 1)
        def _(h=h):
            key = pl.ds(h * HEAD_SIZE, HEAD_SIZE)
            value = pl.ds(KV_WIDTH + h * HEAD_SIZE, HEAD_SIZE)
            near_ref[:, key] = dko_ref[...] * scale
            near_ref[:, value] = dvo_ref[...]
            far_ref[:, key] = (dkr_ref[...] * scale).astype(bf16)
            far_ref[:, value] = dvr_ref[...].astype(bf16)


def attention_back(context, query, dmixed, near, far, logs, cosine, sine):
    tokens = query.shape[0]
    head, key, value, table, log = attention_specs(tokens)
    pairs = 2 * tokens * tokens * QUERY_HEADS
    side = pl.BlockSpec((tokens, 2 * KV_WIDTH), lambda h, place: (0, 0))
    return pl.pallas_call(
        attend_back_kernel,
        out_shape=(
            jax.ShapeDtypeStruct((tokens, Q_WIDTH), bf16),
            jax.ShapeDtypeStruct((tokens, 2 * KV_WIDTH), f32),
            jax.ShapeDtypeStruct((tokens, 2 * KV_WIDTH), bf16),
        ),
        grid_spec=pltpu.PrefetchScalarGridSpec(
            num_scalar_prefetch=1,
            grid=(QUERY_HEADS,),
            in_specs=[head, head, key, value, key, value, log, table, table],
            out_specs=(head, side, side),
            scratch_shapes=[pltpu.VMEM((tokens, HEAD_SIZE), f32)] * 4,
        ),
        compiler_params=pltpu.CompilerParams(
            dimension_semantics=("arbitrary",), vmem_limit_bytes=VMEM_LIMIT
        ),
        cost_estimate=cost(
            flops=10 * pairs * HEAD_SIZE, bytes_accessed=tokens * Q_WIDTH * 8, transcendentals=pairs
        ),
        name="attention_back",
    )(context, query, dmixed, near, near, far, far, logs, cosine, sine)


def swap_halves(grad, context):
    z = lax.axis_size("dp")
    count = lax.axis_size("expert")
    r = grad.shape[0] // (2 * z * count)
    grad = grad.astype(bf16).reshape(2, z, count, r, grad.shape[1])
    theirs = swap(lax.dynamic_index_in_dim(grad, 1 - context, 0, keepdims=False))
    return lax.dynamic_index_in_dim(grad, context, 0, keepdims=False), theirs


def dense_parts(halves, expert):
    out = []
    for k in range(lax.axis_size("expert")):
        sums = []
        for pair in halves:
            a, b = (lax.dynamic_index_in_dim(p, expert ^ k, 1, keepdims=False) for p in pair)
            sums.append(a.astype(f32) + b.astype(f32))
        out.append(jnp.concatenate(sums, axis=-1).astype(bf16))
    return out


def add_all(own, came):
    total = own.astype(f32)
    for c in came:
        total = total + c.astype(f32)
    return total


def finish_dense(total, expert):
    count = lax.axis_size("expert")
    share = lax.psum_scatter(total, "dp", scatter_dimension=0, tiled=False)
    blocks = jnp.stack([share] + [flip(share, k) for k in range(1, count)])
    pieces = [lax.dynamic_index_in_dim(blocks, expert ^ e, 0, keepdims=False) for e in range(count)]
    return jnp.concatenate(pieces, axis=0).astype(f32), share


def block_parts(own, other):
    came = swap(other)
    return [(own[i].astype(f32) + came[i].astype(f32)).astype(bf16) for i in range(own.shape[0])]


def local(
    hidden_in,
    out_grad,
    routes,
    attn_gain,
    w_query,
    key_projection,
    value_projection,
    w_out,
    ffn_gain,
    w_router,
    w_gate,
    w_up,
    w_down,
):
    expert = lax.axis_index("expert")
    context = lax.axis_index("context")
    count = lax.axis_size("expert")
    z = lax.axis_size("dp")
    tokens = hidden_in.shape[1]
    experts_all = EXP_DEV * count
    per_core = EXP_DEV // 2
    capacity = tokens * TOP * 5 // (4 * experts_all)
    rows = w_query.shape[0]
    piece = rows // count

    def chunk(j):
        parts = []
        for at in range(j, EXP_DEV, per_core):
            parts += [w_gate[at], w_up[at], w_down[at].T]
        return jnp.concatenate([p.astype(bf16) for p in parts], axis=0)

    chunks = [chunk(j) for j in range(per_core)]

    def quarter(parts):
        cut = [
            lax.dynamic_slice_in_dim(p, expert * piece, piece, axis=0).astype(bf16) for p in parts
        ]
        return jnp.concatenate(cut, axis=1)

    pad = jnp.zeros((rows, SMALL - experts_all - 2), f32)
    first_pack = quarter(
        [
            w_query,
            key_projection,
            value_projection,
            w_router,
            attn_gain[:, None],
            ffn_gain[:, None],
            pad,
        ]
    )
    second_both = lax.all_gather(quarter([w_out]), ("context", "dp"), axis=0, tiled=False)
    second_both = second_both.reshape(2, z, piece, MODEL_WIDTH)
    first_pack, chunks[0] = tie(first_pack, chunks[0])
    first_z = lax.all_gather(first_pack, "dp", axis=0, tiled=False)
    own_one, other_one = spread(first_z)
    gathered = [lax.all_gather(chunks[0], ("context", "dp"), axis=0, tiled=False)]
    for sent in chunks[1:]:
        sent = after(sent, first_z)
        gathered.append(lax.all_gather(sent, ("context", "dp"), axis=0, tiled=False))
    gathered = [came.reshape(2 * z, 2, 3, rows, FF) for came in gathered]
    second_z = lax.dynamic_index_in_dim(second_both, context, 0, keepdims=False)
    second_other = lax.dynamic_index_in_dim(second_both, 1 - context, 0, keepdims=False)
    second_came = gather_first(after(second_z, *own_one[1:3]))
    packed = assemble(own_one, other_one, context, expert)
    qkv_w = packed[:, : Q_WIDTH + 2 * KV_WIDTH]
    router_w = packed[:, Q_WIDTH + 2 * KV_WIDTH :][:, :experts_all]
    small = packed[:, Q_WIDTH + 2 * KV_WIDTH :].T
    gain_one = small[experts_all].astype(f32)
    gain_two = small[experts_all + 1].astype(f32)

    route_t = routes[0].T
    expert_ids = jnp.arange(experts_all, dtype=jnp.int32)
    named = jnp.any(route_t[:, None, :] == expert_ids[None, :, None], axis=0)
    earlier = (
        jnp.arange(tokens, dtype=jnp.int32)[:, None] < jnp.arange(tokens, dtype=jnp.int32)[None, :]
    )
    ranks = dot(named.astype(bf16), earlier.astype(bf16))
    slot_code = jnp.where(named & (ranks < capacity), ranks, -1.0)

    inputs_f = hidden_in[0].astype(f32)
    scale_one, norm_one = norm_parts(inputs_f)
    act_one = (norm_one * gain_one).astype(bf16)
    qkv = dot(act_one, qkv_w)
    (qkv,), second_came = tie_lists((qkv,), second_came)
    own_two = [second_z, *second_came, *gather_second(second_came)]
    other_two = [second_other] + [swap(b) for b in own_two[1:]]
    dy_half = after(out_grad[0], *own_two[1:])
    dy_came = gather_first(dy_half)
    cosine, sine = rope_tables(context * tokens, tokens, HEAD_SIZE)
    cos_wide = jnp.concatenate([cosine, cosine], axis=1)
    sin_wide = jnp.concatenate([-sine, sine], axis=1)
    near = key_value(qkv, cos_wide, sin_wide)
    far = lax.ppermute(near, "context", [(0, 1)])
    where = context[None].astype(jnp.int32)
    query, mixed, logs = attention(where, qkv, near, far, cos_wide, sin_wide)
    (mixed,), dy_came = tie_lists((mixed,), dy_came)
    dys_own = [dy_half, *dy_came, *gather_second(dy_came)]
    dys_other = [swap(b) for b in dys_own]
    out_w = assemble(own_two, other_two, context, expert)
    resid_one = inputs_f + dot(mixed, out_w)
    scale_two, norm_two = norm_parts(resid_one)
    act_two = (norm_two * gain_two).astype(bf16)

    logits = dot(router_w, act_two, ((0,), (1,)))
    shown = jnp.where(named, logits, mask_fill)
    exped = jnp.where(named, jnp.exp(shown - jnp.max(shown, axis=0, keepdims=True)), 0.0)
    gates = exped / jnp.sum(exped, axis=0, keepdims=True)
    gates_high = gates.astype(bf16)
    gates_low = (gates - gates_high.astype(f32)).astype(bf16)
    meta = jnp.concatenate([gates_high, gates_low, slot_code.astype(bf16)], axis=1)
    payload = jnp.concatenate([act_two, meta], axis=0)
    acts_own, acts_other = spread(after(payload, *dys_own[1:]))

    place = jnp.stack([expert * EXP_DEV + context * per_core, context]).astype(jnp.int32)
    step = jnp.array([1, 0], jnp.int32)
    sums, shares = (), []
    for j in range(per_core):
        *sums, x, gdy, hidden, dgate, dup = run_expert(
            acts_own + acts_other, dys_own + dys_other, gathered[j], place, capacity, sums
        )
        if j == per_core - 1:
            d_parts = block_parts(sums[2], sums[3])
            (x, y_other), d_parts = tie_lists((x, sums[1]), d_parts)
            d_came = scatter_first(d_parts)
        grads = weight_grads(x, gdy, hidden, dgate, dup, z, rows, True)
        (place,), grads = tie_lists((place + step,), grads)
        if j == per_core - 1:
            y_parts = block_parts(sums[0], y_other)
            d_came, grads = tie_lists(d_came, grads)
            d_last = scatter_second(d_parts, d_came)
            d_last, y_parts, shares[-1] = tie_lists(d_last, y_parts, shares[-1])
        shares.append([lax.psum_scatter(g, "dp", scatter_dimension=0, tiled=False) for g in grads])
    dact = scatter_total(d_parts, d_came, d_last)
    y_came = scatter_first(y_parts)

    dy = out_grad[0].astype(f32)
    dgates = dact[tokens:, :tokens] + dact[tokens:, tokens : 2 * tokens]
    dlogits = (gates * (dgates - jnp.sum(gates * dgates, axis=0, keepdims=True))).astype(bf16)
    dact_two = dact[:tokens] + dot(dlogits, router_w, ((0,), (1,)))
    grad_router = dot(dlogits, act_two)
    grad_gain_two = jnp.sum(dact_two * norm_two, axis=0)
    dn2 = dact_two * gain_two
    dresid = dy + scale_two * (dn2 - norm_two * jnp.mean(dn2 * norm_two, axis=-1, keepdims=True))
    dresid_b = dresid.astype(bf16)
    dmixed = dot(dresid_b, out_w, ((1,), (1,))).astype(bf16)
    out_halves = swap_halves(dot(mixed, after(dresid_b, dmixed), ((0,), (0,))), context)

    dquery, near_grad, far_grad = attention_back(
        where, query, dmixed, near, far, logs, cos_wide, sin_wide
    )
    (far_grad,), y_came = tie_lists((far_grad,), y_came)
    came = lax.ppermute(far_grad, "context", [(1, 0)])
    grad_query = dot(act_one, dquery, ((0,), (0,))).astype(bf16)
    dkv = key_value_back(near_grad, came, cos_wide, sin_wide)
    grad_kv = dot(act_one, dkv, ((0,), (0,))).astype(bf16)
    dact_one = dot(dquery, qkv_w[:, :Q_WIDTH], ((1,), (1,)))
    dact_one = dact_one + dot(dkv, qkv_w[:, Q_WIDTH:], ((1,), (1,)))
    grad_gain_one = jnp.sum(dact_one * norm_one, axis=0)
    small = jnp.concatenate(
        [
            grad_router,
            grad_gain_one[None],
            grad_gain_two[None],
            jnp.zeros((SMALL - experts_all - 2, MODEL_WIDTH), f32),
        ],
        axis=0,
    )
    halves = [swap_halves(grad, context) for grad in (grad_query, grad_kv, small.T)]
    first_parts = dense_parts(halves, expert)
    first_came = scatter_first(first_parts)
    out_parts = dense_parts([out_halves], expert)
    out_came = scatter_first(out_parts)
    out_total = scatter_total(out_parts, out_came, scatter_second(out_parts, out_came))

    dn1 = dact_one * gain_one
    grad_in = dresid + scale_one * (dn1 - norm_one * jnp.mean(dn1 * norm_one, axis=-1, keepdims=True))
    y_came, first_came = tie_lists(y_came, first_came)
    first_total = scatter_total(first_parts, first_came, scatter_second(first_parts, first_came))
    y_sum = scatter_total(y_parts, y_came, scatter_second(y_parts, y_came))
    block_out = (resid_one + y_sum).astype(bf16)[None]
    out_total, shares[-1][-1] = tie(out_total.astype(bf16), shares[-1][-1])
    grad_out, out_share = finish_dense(out_total, expert)
    first, _ = finish_dense(first_total.astype(bf16), expert)
    kv_at = Q_WIDTH + KV_WIDTH
    small_at = kv_at + KV_WIDTH

    finals = []
    for pair in shares:
        low, high = pair if len(pair) == 2 else (pair[0][0], pair[0][1])
        keep = jnp.where(context == 0, low, high)
        came = swap(jnp.where(context == 0, high, low))
        finals.append((jnp.where(context == 0, keep, came), jnp.where(context == 0, came, keep)))
    stacked = jnp.stack([f[c] for c in range(2) for f in finals])
    stacked = stacked.astype(f32)
    return (
        block_out,
        grad_in[None],
        first[:, small_at + experts_all],
        first[:, :Q_WIDTH],
        first[:, Q_WIDTH:kv_at],
        first[:, kv_at:small_at],
        grad_out,
        first[:, small_at + experts_all + 1],
        first[:, small_at : small_at + experts_all],
        stacked[:, 0],
        stacked[:, 1],
        jnp.swapaxes(stacked[:, 2], 1, 2),
    )


def solution(mesh):
    tokens_at = P(("expert", "dp"), "context", None)
    vector = P(("context", "dp"))
    matrix = P(("context", "dp"), None)
    wide = P("expert", ("context", "dp"), None)
    down = P("expert", None, ("context", "dp"))
    return jax.shard_map(
        local,
        mesh=mesh,
        in_specs=(
            tokens_at,
            tokens_at,
            tokens_at,
            vector,
            matrix,
            matrix,
            matrix,
            matrix,
            vector,
            matrix,
            wide,
            wide,
            down,
        ),
        out_specs=(
            tokens_at,
            tokens_at,
            vector,
            matrix,
            matrix,
            matrix,
            matrix,
            vector,
            matrix,
            wide,
            wide,
            down,
        ),
        check_vma=False,
    )
```

```python
import functools
import math

import jax
import jax.numpy as jnp
from jax import lax
from jax.experimental import pallas as pl
from jax.experimental.pallas import tpu as pltpu
from jax.sharding import PartitionSpec as P

MODEL_WIDTH = 1536
QUERY_HEADS = 12
KEY_VALUE_HEADS = 2
HEAD_SIZE = 128
FF = 768
TOP = 4
EXP_DEV = 4
GROUP = QUERY_HEADS // KEY_VALUE_HEADS
Q_WIDTH = QUERY_HEADS * HEAD_SIZE
KV_WIDTH = KEY_VALUE_HEADS * HEAD_SIZE
SMALL = 128

norm_eps = 1e-06
rope_base = 1000000.0
mask_fill = -1e30
bf16 = jnp.bfloat16
f32 = jnp.float32
VMEM_LIMIT = 60 * 1024 * 1024


COST_SCALE = 1


def cost(flops, bytes_accessed, transcendentals):
    return pl.CostEstimate(
        flops=flops // COST_SCALE,
        bytes_accessed=bytes_accessed // COST_SCALE,
        transcendentals=transcendentals // COST_SCALE,
    )


def dot(a, b, dims=((1,), (0,))):
    return lax.dot_general(a, b, (dims, ((), ())), preferred_element_type=f32)


def after(value, *others):
    return lax.optimization_barrier((value,) + others)[0]


def tie(*values):
    return lax.optimization_barrier(values)


def flip(value, step):
    count = lax.axis_size("expert")
    return lax.ppermute(value, "expert", [(i, i ^ step) for i in range(count)])


def swap(value):
    return lax.ppermute(value, "context", [(0, 1), (1, 0)])


def rope_tables(start_pos, length, head_dim):
    half_dim = head_dim // 2
    freqs = rope_base ** (-(2.0 * jnp.arange(half_dim, dtype=f32)) / head_dim)
    places = (start_pos + jnp.arange(length, dtype=jnp.int32)).astype(f32)
    angles = places[:, None] * freqs[None, :]
    return (jnp.cos(angles), jnp.sin(angles))


def rotate(heads, cosine, sine):
    half_dim = heads.shape[-1] // 2
    a = heads[..., :half_dim]
    b = heads[..., half_dim:]
    c = cosine[:, None, :]
    s = sine[:, None, :]
    return jnp.concatenate([a * c - b * s, b * c + a * s], axis=-1)


def norm_parts(values):
    scale = lax.rsqrt(jnp.mean(values * values, axis=-1, keepdims=True) + norm_eps)
    return scale, values * scale


def assemble(own, other, context, expert):
    count = len(own)
    z, r, n = own[0].shape
    if r % 16 != 0:
        blocks = jnp.stack([jnp.stack(own), jnp.stack(other)])
        order = jnp.arange(count) ^ expert
        blocks = jnp.take(blocks, order, axis=1)
        blocks = jnp.take(blocks, jnp.arange(2) ^ context, axis=0)
        return jnp.transpose(blocks, (0, 2, 1, 3, 4)).reshape(2 * z * count * r, n)

    def kernel(place, *refs):
        sources, out, sems = refs[: 2 * count], refs[2 * count], refs[2 * count + 1]
        copies = []
        for k in range(count):
            for half in range(2):
                at = place[0] if half == 0 else 1 - place[0]
                copies.append(
                    pltpu.make_async_copy(
                        sources[half * count + k],
                        out.at[at, :, jnp.bitwise_xor(place[1], k)],
                        sems.at[half * count + k],
                    )
                )
        for copy in copies:
            copy.start()
        for copy in copies:
            copy.wait()

    size = 2 * z * count * r * n * 2
    shape = (2, z, count, r, n)
    out = pl.pallas_call(
        kernel,
        out_shape=jax.ShapeDtypeStruct(shape, bf16),
        grid_spec=pltpu.PrefetchScalarGridSpec(
            num_scalar_prefetch=1,
            grid=(1,),
            in_specs=[pl.BlockSpec(memory_space=pl.ANY)] * (2 * count),
            out_specs=pl.BlockSpec(shape, lambda i, place: (0, 0, 0, 0, 0)),
            scratch_shapes=[pltpu.SemaphoreType.DMA((2 * count,))],
        ),
        compiler_params=pltpu.CompilerParams(vmem_limit_bytes=VMEM_LIMIT),
        cost_estimate=cost(flops=0, bytes_accessed=2 * size, transcendentals=0),
        name="assemble",
    )(jnp.stack([context, expert]).astype(jnp.int32), *own, *other)
    return out.reshape(2 * z * count * r, n)


def fourth_block(one, two):
    cut = one.shape[0] // 2
    return jnp.concatenate([flip(one[:cut], 2), flip(two[cut:], 1)], axis=0)


def gather_first(block):
    count = lax.axis_size("expert")
    return [flip(block, k) for k in ((1, 2) if count == 4 else range(1, count))]


def gather_second(came):
    return [fourth_block(*came)] if lax.axis_size("expert") == 4 else []


def gather_blocks(block):
    came = gather_first(block)
    return [block, *came, *gather_second(came)]


def spread(block):
    own = gather_blocks(block)
    return own, [swap(b) for b in own]


def fold_kernel(dense, pairs, place, *refs):
    k, half = pl.program_id(0), pl.program_id(1)
    odd, far = lax.rem(k, 2) == 1, k >= 2
    top, bottom, keep_top, keep_bottom = refs[2 * pairs :]

    def write(out):
        begin = 0
        for own, came in zip(refs[: 2 * pairs : 2], refs[1 : 2 * pairs : 2]):
            lanes = pl.ds(begin, own.shape[-1])
            begin += own.shape[-1]
            if dense:
                out[0, :, :, lanes] = own[0, :, 0] + came[:, 0]
            else:
                out[0, :, lanes] = own[0] + came[0]

    for here, out in (
        ((half == 0) & odd, top),
        ((half == 1) & far, bottom),
        ((half == 0) & jnp.logical_not(odd), keep_top),
        ((half == 1) & jnp.logical_not(far), keep_bottom),
    ):
        pl.when(here)(functools.partial(write, out))


def fold(dense, pairs, place):
    if dense:
        z, _, r, _ = pairs[0][1].shape
        size, rest = z // 2, (r, sum(came.shape[-1] for _, came in pairs))
    else:
        size, rest = pairs[0][0].shape[1] // 2, pairs[0][0].shape[2:]
    specs = []
    for own, came in pairs:
        n = own.shape[-1]
        if dense:
            specs += [
                pl.BlockSpec(
                    (1, size, 1, r, n), lambda k, h, place: (place[0], h, place[1] ^ k, 0, 0)
                ),
                pl.BlockSpec((size, 1, r, n), lambda k, h, place: (h, place[1] ^ k, 0, 0)),
            ]
        else:
            specs += [pl.BlockSpec((1, size, n), lambda k, h, place: (k, h, 0))] * 2
    tail = (0,) * (1 + len(rest))

    def out(at):
        return pl.BlockSpec((1, size, *rest), lambda k, h, place: (at(k), *tail))

    elements = 2 * size * math.prod(rest)
    return list(
        pl.pallas_call(
            functools.partial(fold_kernel, dense, len(pairs)),
            out_shape=[jax.ShapeDtypeStruct((2, size, *rest), bf16)] * 4,
            grid_spec=pltpu.PrefetchScalarGridSpec(
                num_scalar_prefetch=1,
                grid=(4, 2),
                in_specs=specs,
                out_specs=[
                    out(lambda k: lax.div(k, 2)),
                    out(lambda k: jnp.maximum(k - 2, 0)),
                    out(lambda k: lax.div(k, 2)),
                    out(lambda k: jnp.minimum(k, 1)),
                ],
            ),
            compiler_params=pltpu.CompilerParams(
                dimension_semantics=("arbitrary", "arbitrary"), vmem_limit_bytes=VMEM_LIMIT
            ),
            cost_estimate=cost(flops=4 * elements, bytes_accessed=24 * elements, transcendentals=0),
            name="fold",
        )(place, *(v for pair in pairs for v in pair))
    )


def fold_half_kernel(own_ref, came_ref, out_ref):
    out_ref[...] = own_ref[...] + came_ref[...]


def fold_half(own, came, block, half):
    spec = pl.BlockSpec((1, *came.shape[1:]), lambda i: (i, 0, 0))
    return pl.pallas_call(
        fold_half_kernel,
        out_shape=jax.ShapeDtypeStruct(came.shape, bf16),
        grid=(2,),
        in_specs=[pl.BlockSpec((1, *came.shape[1:]), lambda i: (block(i), half, 0)), spec],
        out_specs=spec,
        compiler_params=pltpu.CompilerParams(dimension_semantics=("arbitrary",)),
        cost_estimate=cost(flops=came.size, bytes_accessed=6 * came.size, transcendentals=0),
        name="fold_half",
    )(own, came)


def block_parts(own, other):
    came = swap(other)
    if lax.axis_size("expert") == 4:
        return fold(False, [(own, came)], jnp.zeros((2,), jnp.int32))
    return [(own[i].astype(f32) + came[i].astype(f32)).astype(bf16) for i in range(own.shape[0])]


def swap_halves(grad, context):
    z = lax.axis_size("dp")
    count = lax.axis_size("expert")
    r = grad.shape[0] // (2 * z * count)
    grad = grad.astype(bf16).reshape(2, z, count, r, grad.shape[1])
    return grad, swap(lax.dynamic_index_in_dim(grad, 1 - context, 0, keepdims=False))


def dense_parts(halves, context, expert):
    if lax.axis_size("expert") == 4 and halves[0][0].shape[3] % 16 == 0:
        return fold(True, halves, jnp.stack([context, expert]).astype(jnp.int32))
    out = []
    for k in range(lax.axis_size("expert")):
        sums = []
        for grad, theirs in halves:
            mine = lax.dynamic_index_in_dim(grad, context, 0, keepdims=False)
            a, b = (lax.dynamic_index_in_dim(p, expert ^ k, 1, keepdims=False) for p in (mine, theirs))
            sums.append(a.astype(f32) + b.astype(f32))
        out.append(jnp.concatenate(sums, axis=-1).astype(bf16))
    return out


def scatter_first(parts):
    count = lax.axis_size("expert")
    if count != 4:
        return [flip(parts[k], k) for k in range(1, count)]
    return [flip(parts[0], 1), flip(parts[1], 2)]


def scatter_second(parts, came):
    if lax.axis_size("expert") != 4:
        return []
    top = add_all(parts[2][1], [came[0][1]]).astype(bf16)
    bottom = add_all(parts[3][1], [came[1][1]]).astype(bf16)
    return [flip(top, 2), flip(bottom, 1)]


def scatter_total(parts, came, last):
    if lax.axis_size("expert") != 4:
        return add_all(parts[0], came)
    top = add_all(parts[2][0], [came[0][0], last[0]])
    bottom = add_all(parts[3][0], [came[1][0], last[1]])
    return jnp.concatenate([top, bottom], axis=0)


def tie_lists(*lists):
    flat = iter(tie(*(v for values in lists for v in values)))
    return [[next(flat) for _ in values] for values in lists]


GELU_C = math.sqrt(2.0 / math.pi)


def expert_kernel(count, tokens, capacity, apart, place, *refs):
    acts, dys = refs[: 2 * count], refs[2 * count : 4 * count]
    w_ref, refs = refs[4 * count], refs[4 * count + 1 :]
    sums = 7 if apart else 4
    earlier, refs = refs[: len(refs) - sums - 8], refs[len(refs) - sums - 8 :]
    y_refs, d_refs = refs[:2], refs[2:sums]
    x_ref, gdy_ref, h_ref, dg_ref, du_ref, abuf, dbuf, sems = refs[sums:]
    step = pl.program_id(0)
    slot = lax.rem(step, 2)

    def copies(k, at):
        out = []
        for s in range(2):
            out.append(pltpu.make_async_copy(acts[s * count + k], abuf.at[at, s], sems.at[at, s]))
            out.append(pltpu.make_async_copy(dys[s * count + k], dbuf.at[at, s], sems.at[at, 2 + s]))
        return out

    @pl.when(step == 0)
    def _():
        for c in copies(0, 0):
            c.start()

    for k in range(1, count):

        @pl.when(step == k - 1)
        def _(k=k):
            for c in copies(k, k % 2):
                c.start()

    for k in range(count):

        @pl.when(step == k)
        def _(k=k):
            for c in copies(k, k % 2):
                c.wait()

    row = place[0]
    extra = abuf.shape[2] - tokens
    row_ids = lax.broadcasted_iota(jnp.int32, (extra, 3 * tokens), 0)
    slot_ids = lax.broadcasted_iota(jnp.int32, (capacity, tokens), 0).astype(f32)
    hits = []
    gate_cols = []
    for s in range(2):
        meta = abuf[slot, s, tokens:, :].astype(f32)
        line = jnp.sum(jnp.where(row_ids == row, meta, 0.0), axis=0, keepdims=True)
        gate_line = line[:, :tokens] + line[:, tokens : 2 * tokens]
        hit = slot_ids == line[:, 2 * tokens :]
        hits.append(hit)
        gate_col = jnp.sum(jnp.where(hit, gate_line, 0.0), axis=1, keepdims=True)
        gate_cols.append(gate_col)
        one = jnp.where(hit, 1.0, 0.0).astype(bf16)
        at = pl.ds(s * capacity, capacity)
        x_ref[at, :] = dot(one, abuf[slot, s, :tokens, :]).astype(bf16)
        gdy_ref[at, :] = dot(one, dbuf[slot, s]).astype(bf16)
    gate_col = jnp.concatenate(gate_cols, axis=0)
    wide = w_ref.shape[0] * w_ref.shape[3]
    w_gate = w_ref[:, 0, 0].reshape(wide, FF)
    w_up = w_ref[:, 0, 1].reshape(wide, FF)
    w_down = w_ref[:, 0, 2].reshape(wide, FF)
    x = x_ref[...]
    dy = gdy_ref[...]
    gate_h = dot(x, w_gate)
    up_h = dot(x, w_up)
    back = dot(dy, w_down)
    square = gate_h * gate_h
    tanh = jnp.tanh(GELU_C * gate_h * (1.0 + 0.044715 * square))
    half = 0.5 * (1.0 + tanh)
    gelu = gate_h * half
    slope = half + 0.5 * gate_h * (1.0 - tanh * tanh) * (GELU_C * (1.0 + 3 * 0.044715 * square))
    hidden = (gelu * up_h).astype(bf16)
    dgate_col = jnp.sum(hidden.astype(f32) * back, axis=1, keepdims=True)
    dhidden = back * gate_col
    dgate_h = (dhidden * up_h * slope).astype(bf16)
    dup_h = (dhidden * gelu).astype(bf16)
    h_ref[...] = hidden
    dg_ref[...] = dgate_h
    du_ref[...] = dup_h
    gdy_ref[...] = (dy.astype(f32) * gate_col).astype(bf16)
    result = (dot(hidden, w_down, ((1,), (1,))) * gate_col).astype(bf16)
    dx = (dot(dgate_h, w_gate, ((1,), (1,))) + dot(dup_h, w_up, ((1,), (1,)))).astype(bf16)
    for s in range(2):
        one = jnp.where(hits[s], 1.0, 0.0).astype(bf16)
        rows = slice(s * capacity, (s + 1) * capacity)
        y = dot(one, result[rows], ((0,), (0,)))
        d = dot(one, dx[rows], ((0,), (0,)))
        line = jnp.sum(jnp.where(hits[s], dgate_col[rows], 0.0), axis=0, keepdims=True)
        high = line.astype(bf16).astype(f32)
        line = jnp.concatenate([high, line - high, jnp.zeros_like(high)], axis=1)
        line = jnp.where(row_ids == row, line, 0.0)
        if earlier:
            y = y + earlier[s][0].astype(f32)
            d = d + earlier[2 + s][0, :tokens].astype(f32)
            line = line + earlier[2 + s][0, tokens:].astype(f32)
        y_refs[s][0] = y.astype(bf16)
        d, line = d.astype(bf16), line.astype(bf16)
        if s == 0 or not apart:
            d_refs[s][0, :tokens] = d
            d_refs[s][0, tokens:] = line
            continue
        cut = d_refs[1].shape[1]
        odd, far = lax.rem(step, 2) == 1, step >= 2

        def write_top(ref, d=d):
            ref[0] = d[:cut]

        def write_bottom(ref, d=d, line=line):
            ref[0, : tokens - cut] = d[cut:]
            ref[0, tokens - cut :] = line

        for here, write, ref in zip(
            (odd, far, jnp.logical_not(odd), jnp.logical_not(far)),
            (write_top, write_bottom, write_top, write_bottom),
            d_refs[1:],
        ):
            pl.when(here)(functools.partial(write, ref))


def run_expert(acts, dys, weights, place, capacity, earlier, apart):
    count = len(acts) // 2
    tokens = dys[0].shape[0]
    rows = acts[0].shape[0]
    cz, _, _, local, _ = weights.shape
    slots = 2 * capacity
    total = count * slots
    widths = (MODEL_WIDTH, MODEL_WIDTH, FF, FF, FF)
    macs = total * (6 * MODEL_WIDTH * FF + 4 * tokens * MODEL_WIDTH)
    moved = 2 * (4 * count * (rows + tokens) * MODEL_WIDTH + total * sum(widths) + 3 * MODEL_WIDTH * FF)

    def block(n):
        return pl.BlockSpec((1, n, MODEL_WIDTH), lambda i, place: (i, 0, 0))

    def half(at):
        return pl.BlockSpec((1, rows // 2, MODEL_WIDTH), lambda i, place: (at(i), 0, 0))

    sums = [block(n) for n in (tokens, tokens, rows, rows)]
    shapes = [jax.ShapeDtypeStruct((count, n, MODEL_WIDTH), bf16) for n in (tokens, tokens, rows, rows)]
    outs = list(sums)
    if apart:
        outs[3:] = [
            half(lambda i: lax.div(i, 2)),
            half(lambda i: jnp.maximum(i - 2, 0)),
            half(lambda i: lax.div(i, 2)),
            half(lambda i: jnp.minimum(i, 1)),
        ]
        shapes[3:] = [jax.ShapeDtypeStruct((2, rows // 2, MODEL_WIDTH), bf16)] * 4
    return pl.pallas_call(
        functools.partial(expert_kernel, count, tokens, capacity, apart),
        out_shape=(*shapes, *(jax.ShapeDtypeStruct((total, n), bf16) for n in widths)),
        grid_spec=pltpu.PrefetchScalarGridSpec(
            num_scalar_prefetch=1,
            grid=(count,),
            in_specs=[pl.BlockSpec(memory_space=pl.ANY)] * (4 * count)
            + [
                pl.BlockSpec(
                    (cz, 1, 3, local, FF),
                    lambda i, place: (0, place[1], 0, 0, 0),
                    pipeline_mode=pl.Buffered(1),
                )
            ]
            + (sums if earlier else []),
            out_specs=(*outs, *(pl.BlockSpec((slots, n), lambda i, place: (i, 0)) for n in widths)),
            scratch_shapes=[
                pltpu.VMEM((2, 2, rows, MODEL_WIDTH), bf16),
                pltpu.VMEM((2, 2, tokens, MODEL_WIDTH), bf16),
                pltpu.SemaphoreType.DMA((2, 4)),
            ],
        ),
        compiler_params=pltpu.CompilerParams(
            dimension_semantics=("arbitrary",), vmem_limit_bytes=VMEM_LIMIT
        ),
        cost_estimate=cost(
            flops=2 * macs, bytes_accessed=moved, transcendentals=total * FF
        ),
        name="experts",
    )(place, *acts, *dys, weights, *earlier)


def weight_grad_kernel(per, x_ref, gdy_ref, h_ref, dg_ref, du_ref, *out_refs):
    first = ((0,), (0,))

    def write(out_ref):
        shape = (out_ref.shape[0], out_ref.shape[2], FF)
        x = x_ref[...]
        out_ref[:, 0] = dot(x, dg_ref[...], first).astype(bf16).reshape(shape)
        out_ref[:, 1] = dot(x, du_ref[...], first).astype(bf16).reshape(shape)
        out_ref[:, 2] = dot(gdy_ref[...], h_ref[...], first).astype(bf16).reshape(shape)

    if len(out_refs) == 1:
        write(out_refs[0].at[:, 0])
    else:
        for c, out_ref in enumerate(out_refs):
            pl.when(lax.div(pl.program_id(0), per) == c)(functools.partial(write, out_ref))


def weight_grads(x, gdy, hidden, dgate, dup, z, local, split):
    total = x.shape[0]
    wide = 384
    per = MODEL_WIDTH // 2 // wide
    full = pl.BlockSpec((total, FF), lambda i: (0, 0))
    column = pl.BlockSpec((total, wide), lambda i: (0, i))
    block = wide // local
    if split:
        shapes = [jax.ShapeDtypeStruct((z, 3, local, FF), bf16)] * 2
        specs = [
            pl.BlockSpec((block, 3, local, FF), lambda i: (jnp.minimum(i, per - 1), 0, 0, 0)),
            pl.BlockSpec((block, 3, local, FF), lambda i: (jnp.maximum(i - per, 0), 0, 0, 0)),
        ]
    else:
        shapes = [jax.ShapeDtypeStruct((z, 2, 3, local, FF), bf16)]
        specs = [
            pl.BlockSpec(
                (block, 1, 3, local, FF), lambda i: (lax.rem(i, per), lax.div(i, per), 0, 0, 0)
            )
        ]
    return pl.pallas_call(
        functools.partial(weight_grad_kernel, per),
        out_shape=shapes,
        grid=(MODEL_WIDTH // wide,),
        in_specs=[column, column, full, full, full],
        out_specs=specs,
        compiler_params=pltpu.CompilerParams(
            dimension_semantics=("arbitrary",), vmem_limit_bytes=VMEM_LIMIT
        ),
        cost_estimate=cost(
            flops=6 * total * MODEL_WIDTH * FF,
            bytes_accessed=2 * (total * (2 * MODEL_WIDTH + 3 * FF) + 3 * MODEL_WIDTH * FF),
            transcendentals=0,
        ),
        name="weight_grads",
    )(x, gdy, hidden, dgate, dup)


SCORE = math.log2(math.e) / math.sqrt(HEAD_SIZE)
STRIP = 512


def roll_half(x):
    return pltpu.roll(x, HEAD_SIZE // 2, 1)


def masked(scores):
    key = lax.broadcasted_iota(jnp.int32, (STRIP, STRIP), 0)
    seen = key <= lax.broadcasted_iota(jnp.int32, (STRIP, STRIP), 1)
    square = jnp.where(seen, scores[-STRIP:], mask_fill)
    return jnp.concatenate([scores[:-STRIP], square], axis=0) if scores.shape[0] > STRIP else square


def attend_kernel(place, q_ref, ko_ref, vo_ref, kr_ref, vr_ref, cos_ref, sin_ref, rot_ref, mix_ref, log_ref):
    last = ((1,), (1,))
    first = ((0,), (0,))
    for m in range(PAIR):
        lanes = pl.ds(m * HEAD_SIZE, HEAD_SIZE)
        q = q_ref[:, lanes]
        rot_ref[:, lanes] = (q * cos_ref[...] + roll_half(q) * sin_ref[...]).astype(bf16)
    for r in range(q_ref.shape[0] // STRIP):
        rows = pl.ds(r * STRIP, STRIP)
        seen = (r + 1) * STRIP
        for m in range(PAIR):
            lanes = pl.ds(m * HEAD_SIZE, HEAD_SIZE)
            q = rot_ref[rows, lanes]
            far = dot(kr_ref[...], q, last)
            near = masked(dot(ko_ref[:seen, :], q, last))
            far_peak = jnp.where(place[0] > 0, jnp.max(far, axis=0, keepdims=True), mask_fill)
            peak = jnp.maximum(far_peak, jnp.max(near, axis=0, keepdims=True)) * SCORE
            far = jnp.exp2(far * SCORE - jnp.where(place[0] > 0, peak, -mask_fill))
            near = jnp.exp2(near * SCORE - peak)
            total = jnp.sum(far, axis=0, keepdims=True) + jnp.sum(near, axis=0, keepdims=True)
            out = dot(vr_ref[...], far.astype(bf16), first)
            out = out + dot(vo_ref[:seen, :], near.astype(bf16), first)
            mix_ref[rows, lanes] = (out / total).T.astype(bf16)
            log_ref[m, :, rows] = peak + jnp.log2(total)


def key_value_kernel(x_ref, cos_ref, sin_ref, out_ref):
    for h in range(KEY_VALUE_HEADS):
        at = pl.ds(h * HEAD_SIZE, HEAD_SIZE)
        x = x_ref[:, at]
        out_ref[:, at] = (x * cos_ref[...] + roll_half(x) * sin_ref[...]).astype(bf16)
    out_ref[:, KV_WIDTH:] = x_ref[:, KV_WIDTH:].astype(bf16)


def key_value(qkv, cosine, sine):
    tokens = qkv.shape[0]
    table = pl.BlockSpec((tokens, HEAD_SIZE), lambda i: (0, 0))
    return pl.pallas_call(
        key_value_kernel,
        out_shape=jax.ShapeDtypeStruct((tokens, 2 * KV_WIDTH), bf16),
        grid=(1,),
        in_specs=[
            pl.BlockSpec((tokens, 2 * KV_WIDTH), lambda i: (0, Q_WIDTH // (2 * KV_WIDTH))),
            table,
            table,
        ],
        out_specs=pl.BlockSpec((tokens, 2 * KV_WIDTH), lambda i: (0, 0)),
        cost_estimate=cost(
            flops=tokens * KV_WIDTH * 4, bytes_accessed=tokens * KV_WIDTH * 14, transcendentals=0
        ),
        name="key_value",
    )(qkv, cosine, sine)


def key_value_back_kernel(near_ref, came_ref, cos_ref, sin_ref, out_ref):
    for h in range(KEY_VALUE_HEADS):
        at = pl.ds(h * HEAD_SIZE, HEAD_SIZE)
        x = near_ref[:, at] + came_ref[:, at].astype(f32)
        out_ref[:, at] = (x * cos_ref[...] - roll_half(x) * sin_ref[...]).astype(bf16)
    out_ref[:, KV_WIDTH:] = (
        near_ref[:, KV_WIDTH:] + came_ref[:, KV_WIDTH:].astype(f32)
    ).astype(bf16)


def key_value_back(near, came, cosine, sine):
    tokens = near.shape[0]
    return pl.pallas_call(
        key_value_back_kernel,
        out_shape=jax.ShapeDtypeStruct((tokens, 2 * KV_WIDTH), bf16),
        cost_estimate=cost(
            flops=tokens * KV_WIDTH * 6, bytes_accessed=tokens * KV_WIDTH * 18, transcendentals=0
        ),
        name="key_value_back",
    )(near, came, cosine, sine)


PAIR = 6


def attention_specs(tokens):
    head = pl.BlockSpec((tokens, PAIR * HEAD_SIZE), lambda h, place: (0, h))
    key = pl.BlockSpec((tokens, HEAD_SIZE), lambda h, place: (0, h * PAIR // GROUP))
    value = pl.BlockSpec(
        (tokens, HEAD_SIZE), lambda h, place: (0, KEY_VALUE_HEADS + h * PAIR // GROUP)
    )
    table = pl.BlockSpec((tokens, HEAD_SIZE), lambda h, place: (0, 0))
    log = pl.BlockSpec((PAIR, 1, tokens), lambda h, place: (h, 0, 0))
    return head, key, value, table, log


def attention(context, qkv, near, far, cosine, sine):
    tokens = qkv.shape[0]
    head, key, value, table, log = attention_specs(tokens)
    pairs = 2 * tokens * tokens * QUERY_HEADS
    return pl.pallas_call(
        attend_kernel,
        out_shape=(
            jax.ShapeDtypeStruct((tokens, Q_WIDTH), bf16),
            jax.ShapeDtypeStruct((tokens, Q_WIDTH), bf16),
            jax.ShapeDtypeStruct((QUERY_HEADS, 1, tokens), f32),
        ),
        grid_spec=pltpu.PrefetchScalarGridSpec(
            num_scalar_prefetch=1,
            grid=(QUERY_HEADS // PAIR,),
            in_specs=[head, key, value, key, value, table, table],
            out_specs=(head, head, log),
        ),
        compiler_params=pltpu.CompilerParams(
            dimension_semantics=("arbitrary",), vmem_limit_bytes=VMEM_LIMIT
        ),
        cost_estimate=cost(
            flops=4 * pairs * HEAD_SIZE, bytes_accessed=tokens * Q_WIDTH * 10, transcendentals=pairs
        ),
        name="attention",
    )(context, qkv, near, near, far, far, cosine, sine)


def attend_back_kernel(
    place, q_ref, dout_ref, ko_ref, vo_ref, kr_ref, vr_ref, log_ref, cos_ref, sin_ref,
    dq_ref, near_ref, far_ref, dko_ref, dvo_ref, dkr_ref, dvr_ref,
):
    last = ((1,), (1,))
    first = ((0,), (0,))
    scale = 1.0 / math.sqrt(HEAD_SIZE)
    pair = pl.program_id(0)

    @pl.when(lax.rem(pair, GROUP // PAIR) == 0)
    def _():
        for ref in (dko_ref, dvo_ref, dkr_ref, dvr_ref):
            ref[...] = jnp.zeros_like(ref)

    for r in range(q_ref.shape[0] // STRIP):
        rows = pl.ds(r * STRIP, STRIP)
        seen = (r + 1) * STRIP
        dvr = dvo = dkr = dko = 0.0
        for m in range(PAIR):
            lanes = pl.ds(m * HEAD_SIZE, HEAD_SIZE)
            q = q_ref[rows, lanes]
            dout = dout_ref[rows, lanes]
            logs = log_ref[m, :, rows]
            far = dot(kr_ref[...], q, last)
            near = masked(dot(ko_ref[:seen, :], q, last))
            far = jnp.exp2(far * SCORE - jnp.where(place[0] > 0, logs, -mask_fill))
            near = jnp.exp2(near * SCORE - logs)
            dvr = dvr + dot(far.astype(bf16), dout)
            dvo = dvo + dot(near.astype(bf16), dout)
            dfar = dot(vr_ref[...], dout, last)
            dnear = dot(vo_ref[:seen, :], dout, last)
            inner = jnp.sum(far * dfar, axis=0, keepdims=True)
            inner = inner + jnp.sum(near * dnear, axis=0, keepdims=True)
            dfar = (far * (dfar - inner)).astype(bf16)
            dnear = (near * (dnear - inner)).astype(bf16)
            dkr = dkr + dot(dfar, q)
            dko = dko + dot(dnear, q)
            dq = dot(kr_ref[...], dfar, first) + dot(ko_ref[:seen, :], dnear, first)
            dq = dq.T * scale
            dq_ref[rows, lanes] = (dq * cos_ref[rows, :] - roll_half(dq) * sin_ref[rows, :]).astype(bf16)
        dvr_ref[...] += dvr
        dvo_ref[:seen, :] += dvo
        dkr_ref[...] += dkr
        dko_ref[:seen, :] += dko

    for h in range(KEY_VALUE_HEADS):

        @pl.when(pair == (h + 1) * GROUP // PAIR - 1)
        def _(h=h):
            key = pl.ds(h * HEAD_SIZE, HEAD_SIZE)
            value = pl.ds(KV_WIDTH + h * HEAD_SIZE, HEAD_SIZE)
            near_ref[:, key] = dko_ref[...] * scale
            near_ref[:, value] = dvo_ref[...]
            far_ref[:, key] = (dkr_ref[...] * scale).astype(bf16)
            far_ref[:, value] = dvr_ref[...].astype(bf16)


def attention_back(context, query, dmixed, near, far, logs, cosine, sine):
    tokens = query.shape[0]
    head, key, value, table, log = attention_specs(tokens)
    pairs = 2 * tokens * tokens * QUERY_HEADS
    side = pl.BlockSpec((tokens, 2 * KV_WIDTH), lambda h, place: (0, 0))
    return pl.pallas_call(
        attend_back_kernel,
        out_shape=(
            jax.ShapeDtypeStruct((tokens, Q_WIDTH), bf16),
            jax.ShapeDtypeStruct((tokens, 2 * KV_WIDTH), f32),
            jax.ShapeDtypeStruct((tokens, 2 * KV_WIDTH), bf16),
        ),
        grid_spec=pltpu.PrefetchScalarGridSpec(
            num_scalar_prefetch=1,
            grid=(QUERY_HEADS // PAIR,),
            in_specs=[head, head, key, value, key, value, log, table, table],
            out_specs=(head, side, side),
            scratch_shapes=[pltpu.VMEM((tokens, HEAD_SIZE), f32)] * 4,
        ),
        compiler_params=pltpu.CompilerParams(
            dimension_semantics=("arbitrary",), vmem_limit_bytes=VMEM_LIMIT
        ),
        cost_estimate=cost(
            flops=10 * pairs * HEAD_SIZE, bytes_accessed=tokens * Q_WIDTH * 8, transcendentals=pairs
        ),
        name="attention_back",
    )(context, query, dmixed, near, near, far, far, logs, cosine, sine)


def add_all(own, came):
    total = own.astype(f32)
    for c in came:
        total = total + c.astype(f32)
    return total


def finish_dense(total, expert):
    count = lax.axis_size("expert")
    share = lax.psum_scatter(total, "dp", scatter_dimension=0, tiled=False)
    blocks = jnp.stack([share] + [flip(share, k) for k in range(1, count)])
    pieces = [lax.dynamic_index_in_dim(blocks, expert ^ e, 0, keepdims=False) for e in range(count)]
    return jnp.concatenate(pieces, axis=0).astype(f32), share


def local(
    hidden_in,
    out_grad,
    routes,
    attn_gain,
    w_query,
    key_projection,
    value_projection,
    w_out,
    ffn_gain,
    w_router,
    w_gate,
    w_up,
    w_down,
):
    expert = lax.axis_index("expert")
    context = lax.axis_index("context")
    count = lax.axis_size("expert")
    z = lax.axis_size("dp")
    tokens = hidden_in.shape[1]
    experts_all = EXP_DEV * count
    per_core = EXP_DEV // 2
    capacity = tokens * TOP * 5 // (4 * experts_all)
    rows = w_query.shape[0]
    piece = rows // count

    def chunk(j):
        parts = []
        for at in range(j, EXP_DEV, per_core):
            parts += [w_gate[at], w_up[at], w_down[at].T]
        return jnp.concatenate([p.astype(bf16) for p in parts], axis=0)

    chunks = [chunk(j) for j in range(per_core)]

    def quarter(parts):
        cut = [
            lax.dynamic_slice_in_dim(p, expert * piece, piece, axis=0).astype(bf16) for p in parts
        ]
        return jnp.concatenate(cut, axis=1)

    pad = jnp.zeros((rows, SMALL - experts_all - 2), f32)
    first_pack = quarter(
        [
            w_query,
            key_projection,
            value_projection,
            w_router,
            attn_gain[:, None],
            ffn_gain[:, None],
            pad,
        ]
    )
    second_both = lax.all_gather(quarter([w_out]), ("context", "dp"), axis=0, tiled=False)
    second_both = second_both.reshape(2, z, piece, MODEL_WIDTH)
    first_pack, chunks[0] = tie(first_pack, chunks[0])
    first_z = lax.all_gather(first_pack, "dp", axis=0, tiled=False)
    own_one, other_one = spread(first_z)
    gathered = [lax.all_gather(chunks[0], ("context", "dp"), axis=0, tiled=False)]
    for sent in chunks[1:]:
        sent = after(sent, first_z)
        gathered.append(lax.all_gather(sent, ("context", "dp"), axis=0, tiled=False))
    gathered = [came.reshape(2 * z, 2, 3, rows, FF) for came in gathered]
    second_z = lax.dynamic_index_in_dim(second_both, context, 0, keepdims=False)
    second_other = lax.dynamic_index_in_dim(second_both, 1 - context, 0, keepdims=False)
    second_came = gather_first(after(second_z, *own_one[1:3]))
    packed = assemble(own_one, other_one, context, expert)
    qkv_w = packed[:, : Q_WIDTH + 2 * KV_WIDTH]
    router_w = packed[:, Q_WIDTH + 2 * KV_WIDTH :][:, :experts_all]
    small = packed[:, Q_WIDTH + 2 * KV_WIDTH :].T
    gain_one = small[experts_all].astype(f32)
    gain_two = small[experts_all + 1].astype(f32)

    route_t = routes[0].T
    expert_ids = jnp.arange(experts_all, dtype=jnp.int32)
    named = jnp.any(route_t[:, None, :] == expert_ids[None, :, None], axis=0)
    earlier = (
        jnp.arange(tokens, dtype=jnp.int32)[:, None] < jnp.arange(tokens, dtype=jnp.int32)[None, :]
    )
    ranks = dot(named.astype(bf16), earlier.astype(bf16))
    slot_code = jnp.where(named & (ranks < capacity), ranks, -1.0)

    inputs_f = hidden_in[0].astype(f32)
    scale_one, norm_one = norm_parts(inputs_f)
    act_one = (norm_one * gain_one).astype(bf16)
    qkv = dot(act_one, qkv_w)
    (qkv,), second_came = tie_lists((qkv,), second_came)
    own_two = [second_z, *second_came, *gather_second(second_came)]
    other_two = [second_other] + [swap(b) for b in own_two[1:]]
    dy_half = after(out_grad[0], *own_two[1:])
    dy_came = gather_first(dy_half)
    cosine, sine = rope_tables(context * tokens, tokens, HEAD_SIZE)
    cos_wide = jnp.concatenate([cosine, cosine], axis=1)
    sin_wide = jnp.concatenate([-sine, sine], axis=1)
    near = key_value(qkv, cos_wide, sin_wide)
    far = lax.ppermute(near, "context", [(0, 1)])
    where = context[None].astype(jnp.int32)
    query, mixed, logs = attention(where, qkv, near, far, cos_wide, sin_wide)
    (mixed,), dy_came = tie_lists((mixed,), dy_came)
    dys_own = [dy_half, *dy_came, *gather_second(dy_came)]
    dys_other = [swap(b) for b in dys_own]
    out_w = assemble(own_two, other_two, context, expert)
    resid_one = inputs_f + dot(mixed, out_w)
    scale_two, norm_two = norm_parts(resid_one)
    act_two = (norm_two * gain_two).astype(bf16)

    logits = dot(router_w, act_two, ((0,), (1,)))
    shown = jnp.where(named, logits, mask_fill)
    exped = jnp.where(named, jnp.exp(shown - jnp.max(shown, axis=0, keepdims=True)), 0.0)
    gates = exped / jnp.sum(exped, axis=0, keepdims=True)
    gates_high = gates.astype(bf16)
    gates_low = (gates - gates_high.astype(f32)).astype(bf16)
    meta = jnp.concatenate([gates_high, gates_low, slot_code.astype(bf16)], axis=1)
    meta = jnp.pad(meta, ((0, -experts_all % 32), (0, 0)))
    payload = jnp.concatenate([act_two, meta], axis=0)
    acts_own, acts_other = spread(after(payload, *dys_own[1:]))

    place = jnp.stack([expert * EXP_DEV + context * per_core, context]).astype(jnp.int32)
    step = jnp.array([1, 0], jnp.int32)
    sums, shares = (), []
    for j in range(per_core):
        final = j == per_core - 1
        *sums, x, gdy, hidden, dgate, dup = run_expert(
            acts_own + acts_other,
            dys_own + dys_other,
            gathered[j],
            place,
            capacity,
            sums,
            final and count == 4,
        )
        if final and count == 4:
            y_own, y_other, d_own, *d_apart = sums
            top = fold_half(d_own, swap(d_apart[0]), lambda i: 2 * i + 1, 0)
            bottom = fold_half(d_own, swap(d_apart[1]), lambda i: i + 2, 1)
            d_came = scatter_first([top, bottom])
            (x, y_other, *d_apart[2:]), (top, bottom) = tie_lists(
                (x, y_other, *d_apart[2:]), (top, bottom)
            )
            keep_top = fold_half(d_own, swap(d_apart[2]), lambda i: 2 * i, 0)
            keep_bottom = fold_half(d_own, swap(d_apart[3]), lambda i: i, 1)
            d_parts = [top, bottom, keep_top, keep_bottom]
        elif final:
            y_own, y_other, d_own, d_other = sums
            d_parts = block_parts(d_own, d_other)
            d_came = scatter_first(d_parts)
        grads = weight_grads(x, gdy, hidden, dgate, dup, z, rows, False)
        (place,), grads = tie_lists((place + step,), grads)
        if final:
            d_came, grads = tie_lists(d_came, grads)
            d_last = scatter_second(d_parts, d_came)
            y_parts = block_parts(y_own, y_other)
            d_last, y_parts, shares[-1] = tie_lists(d_last, y_parts, shares[-1])
        shares.append([lax.psum_scatter(g, "dp", scatter_dimension=0, tiled=False) for g in grads])
    dact = scatter_total(d_parts, d_came, d_last)
    y_came = scatter_first(y_parts)

    dy = out_grad[0].astype(f32)
    dgates = dact[tokens : tokens + experts_all, : 2 * tokens]
    dgates = dgates[:, :tokens] + dgates[:, tokens:]
    dlogits = (gates * (dgates - jnp.sum(gates * dgates, axis=0, keepdims=True))).astype(bf16)
    dact_two = dact[:tokens] + dot(dlogits, router_w, ((0,), (1,)))
    grad_gain_two = jnp.sum(dact_two * norm_two, axis=0)
    dn2 = dact_two * gain_two
    dresid = dy + scale_two * (dn2 - norm_two * jnp.mean(dn2 * norm_two, axis=-1, keepdims=True))
    dresid_b = dresid.astype(bf16)
    dmixed = dot(dresid_b, out_w, ((1,), (1,))).astype(bf16)

    dquery, near_grad, far_grad = attention_back(
        where, query, dmixed, near, far, logs, cos_wide, sin_wide
    )
    (far_grad,), y_came = tie_lists((far_grad,), y_came)
    came = lax.ppermute(far_grad, "context", [(1, 0)])
    grad_query = dot(act_one, dquery, ((0,), (0,))).astype(bf16)
    dkv = key_value_back(near_grad, came, cos_wide, sin_wide)
    grad_kv = dot(act_one, dkv, ((0,), (0,))).astype(bf16)
    halves = [swap_halves(grad, context) for grad in (grad_query, grad_kv)]
    first_parts = dense_parts(halves, context, expert)
    first_came = scatter_first(first_parts)

    first_parts, (dquery, dkv, dlogits, dresid_b), shares[0] = tie_lists(
        first_parts, (dquery, dkv, dlogits, dresid_b), shares[0]
    )
    out_halves = swap_halves(dot(mixed, dresid_b, ((0,), (0,))), context)
    dact_one = dot(dquery, qkv_w[:, :Q_WIDTH], ((1,), (1,)))
    dact_one = dact_one + dot(dkv, qkv_w[:, Q_WIDTH:], ((1,), (1,)))
    grad_gain_one = jnp.sum(dact_one * norm_one, axis=0)
    dn1 = dact_one * gain_one
    grad_in = dresid + scale_one * (dn1 - norm_one * jnp.mean(dn1 * norm_one, axis=-1, keepdims=True))
    small = jnp.concatenate(
        [
            dot(dlogits, act_two),
            grad_gain_one[None],
            grad_gain_two[None],
            jnp.zeros((SMALL - experts_all - 2, MODEL_WIDTH), f32),
        ],
        axis=0,
    )
    small = swap_halves(small.T, context)
    (out_theirs, small_theirs), first_came = tie_lists((out_halves[1], small[1]), first_came)
    first_last = scatter_second(first_parts, first_came)
    out_halves = [(out_halves[0], out_theirs), (small[0], small_theirs)]
    out_parts = dense_parts(out_halves, context, expert)
    out_came = scatter_first(out_parts)
    first_total = scatter_total(first_parts, first_came, first_last)
    (first_total,), shares[-1], out_parts = tie_lists(
        (first_total.astype(bf16),), shares[-1], out_parts
    )
    first, first_share = finish_dense(first_total, expert)
    out_total = scatter_total(out_parts, out_came, scatter_second(out_parts, out_came))
    (out_total, first_share, grad_in), y_came = tie_lists(
        (out_total.astype(bf16), first_share, grad_in), y_came
    )
    last, out_share = finish_dense(out_total, expert)
    y_last = scatter_second(y_parts, y_came)
    y_last, (out_share,) = tie_lists(y_last, (out_share,))
    y_sum = scatter_total(y_parts, y_came, y_last)
    block_out = (resid_one + y_sum).astype(bf16)[None]
    kv_at = Q_WIDTH + KV_WIDTH

    finals = []
    for pair in shares:
        low, high = pair if len(pair) == 2 else (pair[0][0], pair[0][1])
        keep = jnp.where(context == 0, low, high)
        came = swap(jnp.where(context == 0, high, low))
        finals.append((jnp.where(context == 0, keep, came), jnp.where(context == 0, came, keep)))
    stacked = jnp.stack([f[c] for c in range(2) for f in finals])
    stacked = stacked.astype(f32)
    return (
        block_out,
        grad_in[None],
        last[:, MODEL_WIDTH + experts_all],
        first[:, :Q_WIDTH],
        first[:, Q_WIDTH:kv_at],
        first[:, kv_at:],
        last[:, :MODEL_WIDTH],
        last[:, MODEL_WIDTH + experts_all + 1],
        last[:, MODEL_WIDTH : MODEL_WIDTH + experts_all],
        stacked[:, 0],
        stacked[:, 1],
        jnp.swapaxes(stacked[:, 2], 1, 2),
    )


def solution(mesh):
    tokens_at = P(("expert", "dp"), "context", None)
    vector = P(("context", "dp"))
    matrix = P(("context", "dp"), None)
    wide = P("expert", ("context", "dp"), None)
    down = P("expert", None, ("context", "dp"))
    return jax.shard_map(
        local,
        mesh=mesh,
        in_specs=(
            tokens_at,
            tokens_at,
            tokens_at,
            vector,
            matrix,
            matrix,
            matrix,
            matrix,
            vector,
            matrix,
            wide,
            wide,
            down,
        ),
        out_specs=(
            tokens_at,
            tokens_at,
            vector,
            matrix,
            matrix,
            matrix,
            matrix,
            vector,
            matrix,
            wide,
            wide,
            down,
        ),
        check_vma=False,
    )
```

```python
import functools
import math

import jax
import jax.numpy as jnp
from jax import lax
from jax.experimental import pallas as pl
from jax.experimental.pallas import tpu as pltpu
from jax.sharding import PartitionSpec as P

MODEL_WIDTH = 1536
QUERY_HEADS = 12
KEY_VALUE_HEADS = 2
HEAD_SIZE = 128
FF = 768
TOP = 4
EXP_DEV = 4
GROUP = QUERY_HEADS // KEY_VALUE_HEADS
Q_WIDTH = QUERY_HEADS * HEAD_SIZE
KV_WIDTH = KEY_VALUE_HEADS * HEAD_SIZE
SMALL = 128

norm_eps = 1e-06
rope_base = 1000000.0
mask_fill = -1e30
bf16 = jnp.bfloat16
f32 = jnp.float32
VMEM_LIMIT = 60 * 1024 * 1024


COST_SCALE = 1


def cost(flops, bytes_accessed, transcendentals):
    return pl.CostEstimate(
        flops=flops // COST_SCALE,
        bytes_accessed=bytes_accessed // COST_SCALE,
        transcendentals=transcendentals // COST_SCALE,
    )


def dot(a, b, dims=((1,), (0,))):
    return lax.dot_general(a, b, (dims, ((), ())), preferred_element_type=f32)


def after(value, *others):
    return lax.optimization_barrier((value,) + others)[0]


def tie(*values):
    return lax.optimization_barrier(values)


def flip(value, step):
    count = lax.axis_size("expert")
    return lax.ppermute(value, "expert", [(i, i ^ step) for i in range(count)])


def swap(value):
    return lax.ppermute(value, "context", [(0, 1), (1, 0)])


def rope_tables(start_pos, length, head_dim):
    half_dim = head_dim // 2
    freqs = rope_base ** (-(2.0 * jnp.arange(half_dim, dtype=f32)) / head_dim)
    places = (start_pos + jnp.arange(length, dtype=jnp.int32)).astype(f32)
    angles = places[:, None] * freqs[None, :]
    return (jnp.cos(angles), jnp.sin(angles))


def rotate(heads, cosine, sine):
    half_dim = heads.shape[-1] // 2
    a = heads[..., :half_dim]
    b = heads[..., half_dim:]
    c = cosine[:, None, :]
    s = sine[:, None, :]
    return jnp.concatenate([a * c - b * s, b * c + a * s], axis=-1)


def norm_parts(values):
    scale = lax.rsqrt(jnp.mean(values * values, axis=-1, keepdims=True) + norm_eps)
    return scale, values * scale


def assemble(own, other, context, expert):
    count = len(own)
    z, r, n = own[0].shape
    if r % 16 != 0:
        blocks = jnp.stack([jnp.stack(own), jnp.stack(other)])
        order = jnp.arange(count) ^ expert
        blocks = jnp.take(blocks, order, axis=1)
        blocks = jnp.take(blocks, jnp.arange(2) ^ context, axis=0)
        return jnp.transpose(blocks, (0, 2, 1, 3, 4)).reshape(2 * z * count * r, n)

    def kernel(place, *refs):
        sources, out, sems = refs[: 2 * count], refs[2 * count], refs[2 * count + 1]
        copies = []
        for k in range(count):
            for half in range(2):
                at = place[0] if half == 0 else 1 - place[0]
                copies.append(
                    pltpu.make_async_copy(
                        sources[half * count + k],
                        out.at[at, :, jnp.bitwise_xor(place[1], k)],
                        sems.at[half * count + k],
                    )
                )
        for copy in copies:
            copy.start()
        for copy in copies:
            copy.wait()

    size = 2 * z * count * r * n * 2
    shape = (2, z, count, r, n)
    out = pl.pallas_call(
        kernel,
        out_shape=jax.ShapeDtypeStruct(shape, bf16),
        grid_spec=pltpu.PrefetchScalarGridSpec(
            num_scalar_prefetch=1,
            grid=(1,),
            in_specs=[pl.BlockSpec(memory_space=pl.ANY)] * (2 * count),
            out_specs=pl.BlockSpec(shape, lambda i, place: (0, 0, 0, 0, 0)),
            scratch_shapes=[pltpu.SemaphoreType.DMA((2 * count,))],
        ),
        compiler_params=pltpu.CompilerParams(vmem_limit_bytes=VMEM_LIMIT),
        cost_estimate=cost(flops=0, bytes_accessed=2 * size, transcendentals=0),
        name="assemble",
    )(jnp.stack([context, expert]).astype(jnp.int32), *own, *other)
    return out.reshape(2 * z * count * r, n)


def fourth_block(one, two):
    cut = one.shape[0] // 2
    return jnp.concatenate([flip(one[:cut], 2), flip(two[cut:], 1)], axis=0)


def gather_first(block):
    count = lax.axis_size("expert")
    return [flip(block, k) for k in ((1, 2) if count == 4 else range(1, count))]


def gather_second(came):
    return [fourth_block(*came)] if lax.axis_size("expert") == 4 else []


def gather_blocks(block):
    came = gather_first(block)
    return [block, *came, *gather_second(came)]


def spread(block):
    own = gather_blocks(block)
    return own, [swap(b) for b in own]


def fold_kernel(dense, pairs, place, *refs):
    k, half = pl.program_id(0), pl.program_id(1)
    odd, far = lax.rem(k, 2) == 1, k >= 2
    top, bottom, keep_top, keep_bottom = refs[2 * pairs :]

    def write(out):
        begin = 0
        for own, came in zip(refs[: 2 * pairs : 2], refs[1 : 2 * pairs : 2]):
            lanes = pl.ds(begin, own.shape[-1])
            begin += own.shape[-1]
            if dense:
                out[0, :, :, lanes] = own[0, :, 0] + came[:, 0]
            else:
                out[0, :, lanes] = own[0] + came[0]

    for here, out in (
        ((half == 0) & odd, top),
        ((half == 1) & far, bottom),
        ((half == 0) & jnp.logical_not(odd), keep_top),
        ((half == 1) & jnp.logical_not(far), keep_bottom),
    ):
        pl.when(here)(functools.partial(write, out))


def fold(dense, pairs, place):
    if dense:
        z, _, r, _ = pairs[0][1].shape
        size, rest = z // 2, (r, sum(came.shape[-1] for _, came in pairs))
    else:
        size, rest = pairs[0][0].shape[1] // 2, pairs[0][0].shape[2:]
    specs = []
    for own, came in pairs:
        n = own.shape[-1]
        if dense:
            specs += [
                pl.BlockSpec(
                    (1, size, 1, r, n), lambda k, h, place: (place[0], h, place[1] ^ k, 0, 0)
                ),
                pl.BlockSpec((size, 1, r, n), lambda k, h, place: (h, place[1] ^ k, 0, 0)),
            ]
        else:
            specs += [pl.BlockSpec((1, size, n), lambda k, h, place: (k, h, 0))] * 2
    tail = (0,) * (1 + len(rest))

    def out(at):
        return pl.BlockSpec((1, size, *rest), lambda k, h, place: (at(k), *tail))

    elements = 2 * size * math.prod(rest)
    return list(
        pl.pallas_call(
            functools.partial(fold_kernel, dense, len(pairs)),
            out_shape=[jax.ShapeDtypeStruct((2, size, *rest), bf16)] * 4,
            grid_spec=pltpu.PrefetchScalarGridSpec(
                num_scalar_prefetch=1,
                grid=(4, 2),
                in_specs=specs,
                out_specs=[
                    out(lambda k: lax.div(k, 2)),
                    out(lambda k: jnp.maximum(k - 2, 0)),
                    out(lambda k: lax.div(k, 2)),
                    out(lambda k: jnp.minimum(k, 1)),
                ],
            ),
            compiler_params=pltpu.CompilerParams(
                dimension_semantics=("arbitrary", "arbitrary"), vmem_limit_bytes=VMEM_LIMIT
            ),
            cost_estimate=cost(flops=4 * elements, bytes_accessed=24 * elements, transcendentals=0),
            name="fold",
        )(place, *(v for pair in pairs for v in pair))
    )


def fold_half_kernel(own_ref, came_ref, out_ref):
    out_ref[...] = own_ref[...] + came_ref[...]


def fold_half(own, came, block, half):
    spec = pl.BlockSpec((1, *came.shape[1:]), lambda i: (i, 0, 0))
    return pl.pallas_call(
        fold_half_kernel,
        out_shape=jax.ShapeDtypeStruct(came.shape, bf16),
        grid=(2,),
        in_specs=[pl.BlockSpec((1, *came.shape[1:]), lambda i: (block(i), half, 0)), spec],
        out_specs=spec,
        compiler_params=pltpu.CompilerParams(dimension_semantics=("arbitrary",)),
        cost_estimate=cost(flops=came.size, bytes_accessed=6 * came.size, transcendentals=0),
        name="fold_half",
    )(own, came)


def block_parts(own, other):
    came = swap(other)
    if lax.axis_size("expert") == 4:
        return fold(False, [(own, came)], jnp.zeros((2,), jnp.int32))
    return [(own[i].astype(f32) + came[i].astype(f32)).astype(bf16) for i in range(own.shape[0])]


def swap_halves(grad, context):
    z = lax.axis_size("dp")
    count = lax.axis_size("expert")
    r = grad.shape[0] // (2 * z * count)
    grad = grad.astype(bf16).reshape(2, z, count, r, grad.shape[1])
    return grad, swap(lax.dynamic_index_in_dim(grad, 1 - context, 0, keepdims=False))


def dense_parts(halves, context, expert):
    if lax.axis_size("expert") == 4 and halves[0][0].shape[3] % 16 == 0:
        return fold(True, halves, jnp.stack([context, expert]).astype(jnp.int32))
    out = []
    for k in range(lax.axis_size("expert")):
        sums = []
        for grad, theirs in halves:
            mine = lax.dynamic_index_in_dim(grad, context, 0, keepdims=False)
            a, b = (lax.dynamic_index_in_dim(p, expert ^ k, 1, keepdims=False) for p in (mine, theirs))
            sums.append(a.astype(f32) + b.astype(f32))
        out.append(jnp.concatenate(sums, axis=-1).astype(bf16))
    return out


def scatter_first(parts):
    count = lax.axis_size("expert")
    if count != 4:
        return [flip(parts[k], k) for k in range(1, count)]
    return [flip(parts[0], 1), flip(parts[1], 2)]


def scatter_second(parts, came):
    if lax.axis_size("expert") != 4:
        return []
    top = add_all(parts[2][1], [came[0][1]]).astype(bf16)
    bottom = add_all(parts[3][1], [came[1][1]]).astype(bf16)
    return [flip(top, 2), flip(bottom, 1)]


def scatter_total(parts, came, last):
    if lax.axis_size("expert") != 4:
        return add_all(parts[0], came)
    top = add_all(parts[2][0], [came[0][0], last[0]])
    bottom = add_all(parts[3][0], [came[1][0], last[1]])
    return jnp.concatenate([top, bottom], axis=0)


def tie_lists(*lists):
    flat = iter(tie(*(v for values in lists for v in values)))
    return [[next(flat) for _ in values] for values in lists]


GELU_C = math.sqrt(2.0 / math.pi)


def expert_kernel(count, tokens, capacity, apart, place, *refs):
    acts, dys = refs[: 2 * count], refs[2 * count : 4 * count]
    w_ref, refs = refs[4 * count], refs[4 * count + 1 :]
    sums = 7 if apart else 4
    earlier, refs = refs[: len(refs) - sums - 8], refs[len(refs) - sums - 8 :]
    y_refs, d_refs = refs[:2], refs[2:sums]
    x_ref, gdy_ref, h_ref, dg_ref, du_ref, abuf, dbuf, sems = refs[sums:]
    step = pl.program_id(0)
    slot = lax.rem(step, 2)

    def copies(k, at):
        out = []
        for s in range(2):
            out.append(pltpu.make_async_copy(acts[s * count + k], abuf.at[at, s], sems.at[at, s]))
            out.append(pltpu.make_async_copy(dys[s * count + k], dbuf.at[at, s], sems.at[at, 2 + s]))
        return out

    @pl.when(step == 0)
    def _():
        for c in copies(0, 0):
            c.start()

    for k in range(1, count):

        @pl.when(step == k - 1)
        def _(k=k):
            for c in copies(k, k % 2):
                c.start()

    for k in range(count):

        @pl.when(step == k)
        def _(k=k):
            for c in copies(k, k % 2):
                c.wait()

    row = place[0]
    extra = abuf.shape[2] - tokens
    row_ids = lax.broadcasted_iota(jnp.int32, (extra, 3 * tokens), 0)
    slot_ids = lax.broadcasted_iota(jnp.int32, (capacity, tokens), 0).astype(f32)
    hits = []
    gate_cols = []
    for s in range(2):
        meta = abuf[slot, s, tokens:, :].astype(f32)
        line = jnp.sum(jnp.where(row_ids == row, meta, 0.0), axis=0, keepdims=True)
        gate_line = line[:, :tokens] + line[:, tokens : 2 * tokens]
        hit = slot_ids == line[:, 2 * tokens :]
        hits.append(hit)
        gate_col = jnp.sum(jnp.where(hit, gate_line, 0.0), axis=1, keepdims=True)
        gate_cols.append(gate_col)
        one = jnp.where(hit, 1.0, 0.0).astype(bf16)
        at = pl.ds(s * capacity, capacity)
        x_ref[at, :] = dot(one, abuf[slot, s, :tokens, :]).astype(bf16)
        gdy_ref[at, :] = dot(one, dbuf[slot, s]).astype(bf16)
    gate_col = jnp.concatenate(gate_cols, axis=0)
    wide = w_ref.shape[0] * w_ref.shape[3]
    w_gate = w_ref[:, 0, 0].reshape(wide, FF)
    w_up = w_ref[:, 0, 1].reshape(wide, FF)
    w_down = w_ref[:, 0, 2].reshape(wide, FF)
    x = x_ref[...]
    dy = gdy_ref[...]
    gate_h = dot(x, w_gate)
    up_h = dot(x, w_up)
    back = dot(dy, w_down)
    square = gate_h * gate_h
    tanh = jnp.tanh(GELU_C * gate_h * (1.0 + 0.044715 * square))
    half = 0.5 * (1.0 + tanh)
    gelu = gate_h * half
    slope = half + 0.5 * gate_h * (1.0 - tanh * tanh) * (GELU_C * (1.0 + 3 * 0.044715 * square))
    hidden = (gelu * up_h).astype(bf16)
    dgate_col = jnp.sum(hidden.astype(f32) * back, axis=1, keepdims=True)
    dhidden = back * gate_col
    dgate_h = (dhidden * up_h * slope).astype(bf16)
    dup_h = (dhidden * gelu).astype(bf16)
    h_ref[...] = hidden
    dg_ref[...] = dgate_h
    du_ref[...] = dup_h
    gdy_ref[...] = (dy.astype(f32) * gate_col).astype(bf16)
    result = (dot(hidden, w_down, ((1,), (1,))) * gate_col).astype(bf16)
    dx = (dot(dgate_h, w_gate, ((1,), (1,))) + dot(dup_h, w_up, ((1,), (1,)))).astype(bf16)
    for s in range(2):
        one = jnp.where(hits[s], 1.0, 0.0).astype(bf16)
        rows = slice(s * capacity, (s + 1) * capacity)
        y = dot(one, result[rows], ((0,), (0,)))
        d = dot(one, dx[rows], ((0,), (0,)))
        line = jnp.sum(jnp.where(hits[s], dgate_col[rows], 0.0), axis=0, keepdims=True)
        high = line.astype(bf16).astype(f32)
        line = jnp.concatenate([high, line - high, jnp.zeros_like(high)], axis=1)
        line = jnp.where(row_ids == row, line, 0.0)
        if earlier:
            y = y + earlier[s][0].astype(f32)
            d = d + earlier[2 + s][0, :tokens].astype(f32)
            line = line + earlier[2 + s][0, tokens:].astype(f32)
        y_refs[s][0] = y.astype(bf16)
        d, line = d.astype(bf16), line.astype(bf16)
        if s == 0 or not apart:
            d_refs[s][0, :tokens] = d
            d_refs[s][0, tokens:] = line
            continue
        cut = d_refs[1].shape[1]
        odd, far = lax.rem(step, 2) == 1, step >= 2

        def write_top(ref, d=d):
            ref[0] = d[:cut]

        def write_bottom(ref, d=d, line=line):
            ref[0, : tokens - cut] = d[cut:]
            ref[0, tokens - cut :] = line

        for here, write, ref in zip(
            (odd, far, jnp.logical_not(odd), jnp.logical_not(far)),
            (write_top, write_bottom, write_top, write_bottom),
            d_refs[1:],
        ):
            pl.when(here)(functools.partial(write, ref))


def run_expert(acts, dys, weights, place, capacity, earlier, apart):
    count = len(acts) // 2
    tokens = dys[0].shape[0]
    rows = acts[0].shape[0]
    cz, _, _, local, _ = weights.shape
    slots = 2 * capacity
    total = count * slots
    widths = (MODEL_WIDTH, MODEL_WIDTH, FF, FF, FF)
    macs = total * (6 * MODEL_WIDTH * FF + 4 * tokens * MODEL_WIDTH)
    moved = 2 * (4 * count * (rows + tokens) * MODEL_WIDTH + total * sum(widths) + 3 * MODEL_WIDTH * FF)

    def block(n):
        return pl.BlockSpec((1, n, MODEL_WIDTH), lambda i, place: (i, 0, 0))

    def half(at):
        return pl.BlockSpec((1, rows // 2, MODEL_WIDTH), lambda i, place: (at(i), 0, 0))

    sums = [block(n) for n in (tokens, tokens, rows, rows)]
    shapes = [jax.ShapeDtypeStruct((count, n, MODEL_WIDTH), bf16) for n in (tokens, tokens, rows, rows)]
    outs = list(sums)
    if apart:
        outs[3:] = [
            half(lambda i: lax.div(i, 2)),
            half(lambda i: jnp.maximum(i - 2, 0)),
            half(lambda i: lax.div(i, 2)),
            half(lambda i: jnp.minimum(i, 1)),
        ]
        shapes[3:] = [jax.ShapeDtypeStruct((2, rows // 2, MODEL_WIDTH), bf16)] * 4
    return pl.pallas_call(
        functools.partial(expert_kernel, count, tokens, capacity, apart),
        out_shape=(*shapes, *(jax.ShapeDtypeStruct((total, n), bf16) for n in widths)),
        grid_spec=pltpu.PrefetchScalarGridSpec(
            num_scalar_prefetch=1,
            grid=(count,),
            in_specs=[pl.BlockSpec(memory_space=pl.ANY)] * (4 * count)
            + [
                pl.BlockSpec(
                    (cz, 1, 3, local, FF),
                    lambda i, place: (0, place[1], 0, 0, 0),
                    pipeline_mode=pl.Buffered(1),
                )
            ]
            + (sums if earlier else []),
            out_specs=(*outs, *(pl.BlockSpec((slots, n), lambda i, place: (i, 0)) for n in widths)),
            scratch_shapes=[
                pltpu.VMEM((2, 2, rows, MODEL_WIDTH), bf16),
                pltpu.VMEM((2, 2, tokens, MODEL_WIDTH), bf16),
                pltpu.SemaphoreType.DMA((2, 4)),
            ],
        ),
        compiler_params=pltpu.CompilerParams(
            dimension_semantics=("arbitrary",), vmem_limit_bytes=VMEM_LIMIT
        ),
        cost_estimate=cost(
            flops=2 * macs, bytes_accessed=moved, transcendentals=total * FF
        ),
        name="experts",
    )(place, *acts, *dys, weights, *earlier)


def weight_grad_kernel(per, x_ref, gdy_ref, h_ref, dg_ref, du_ref, *out_refs):
    first = ((0,), (0,))

    def write(out_ref):
        shape = (out_ref.shape[0], out_ref.shape[2], FF)
        x = x_ref[...]
        out_ref[:, 0] = dot(x, dg_ref[...], first).astype(bf16).reshape(shape)
        out_ref[:, 1] = dot(x, du_ref[...], first).astype(bf16).reshape(shape)
        out_ref[:, 2] = dot(gdy_ref[...], h_ref[...], first).astype(bf16).reshape(shape)

    if len(out_refs) == 1:
        write(out_refs[0].at[:, 0])
    else:
        for c, out_ref in enumerate(out_refs):
            pl.when(lax.div(pl.program_id(0), per) == c)(functools.partial(write, out_ref))


def weight_grads(x, gdy, hidden, dgate, dup, z, local, split):
    total = x.shape[0]
    wide = 384
    per = MODEL_WIDTH // 2 // wide
    full = pl.BlockSpec((total, FF), lambda i: (0, 0))
    column = pl.BlockSpec((total, wide), lambda i: (0, i))
    block = wide // local
    if split:
        shapes = [jax.ShapeDtypeStruct((z, 3, local, FF), bf16)] * 2
        specs = [
            pl.BlockSpec((block, 3, local, FF), lambda i: (jnp.minimum(i, per - 1), 0, 0, 0)),
            pl.BlockSpec((block, 3, local, FF), lambda i: (jnp.maximum(i - per, 0), 0, 0, 0)),
        ]
    else:
        shapes = [jax.ShapeDtypeStruct((z, 2, 3, local, FF), bf16)]
        specs = [
            pl.BlockSpec(
                (block, 1, 3, local, FF), lambda i: (lax.rem(i, per), lax.div(i, per), 0, 0, 0)
            )
        ]
    return pl.pallas_call(
        functools.partial(weight_grad_kernel, per),
        out_shape=shapes,
        grid=(MODEL_WIDTH // wide,),
        in_specs=[column, column, full, full, full],
        out_specs=specs,
        compiler_params=pltpu.CompilerParams(
            dimension_semantics=("arbitrary",), vmem_limit_bytes=VMEM_LIMIT
        ),
        cost_estimate=cost(
            flops=6 * total * MODEL_WIDTH * FF,
            bytes_accessed=2 * (total * (2 * MODEL_WIDTH + 3 * FF) + 3 * MODEL_WIDTH * FF),
            transcendentals=0,
        ),
        name="weight_grads",
    )(x, gdy, hidden, dgate, dup)


SCORE = math.log2(math.e) / math.sqrt(HEAD_SIZE)
STRIP = 512


def roll_half(x):
    return pltpu.roll(x, HEAD_SIZE // 2, 1)


def masked(scores):
    key = lax.broadcasted_iota(jnp.int32, (STRIP, STRIP), 0)
    seen = key <= lax.broadcasted_iota(jnp.int32, (STRIP, STRIP), 1)
    square = jnp.where(seen, scores[-STRIP:], mask_fill)
    return jnp.concatenate([scores[:-STRIP], square], axis=0) if scores.shape[0] > STRIP else square


def attend_kernel(place, q_ref, ko_ref, vo_ref, kr_ref, vr_ref, cos_ref, sin_ref, rot_ref, mix_ref, log_ref):
    last = ((1,), (1,))
    first = ((0,), (0,))
    for m in range(PAIR):
        lanes = pl.ds(m * HEAD_SIZE, HEAD_SIZE)
        q = q_ref[:, lanes]
        rot_ref[:, lanes] = (q * cos_ref[...] + roll_half(q) * sin_ref[...]).astype(bf16)
    for r in range(q_ref.shape[0] // STRIP):
        rows = pl.ds(r * STRIP, STRIP)
        seen = (r + 1) * STRIP
        for m in range(PAIR):
            lanes = pl.ds(m * HEAD_SIZE, HEAD_SIZE)
            q = rot_ref[rows, lanes]
            far = dot(kr_ref[...], q, last)
            near = masked(dot(ko_ref[:seen, :], q, last))
            far_peak = jnp.where(place[0] > 0, jnp.max(far, axis=0, keepdims=True), mask_fill)
            peak = jnp.maximum(far_peak, jnp.max(near, axis=0, keepdims=True)) * SCORE
            far = jnp.exp2(far * SCORE - jnp.where(place[0] > 0, peak, -mask_fill))
            near = jnp.exp2(near * SCORE - peak)
            total = jnp.sum(far, axis=0, keepdims=True) + jnp.sum(near, axis=0, keepdims=True)
            out = dot(vr_ref[...], far.astype(bf16), first)
            out = out + dot(vo_ref[:seen, :], near.astype(bf16), first)
            mix_ref[rows, lanes] = (out / total).T.astype(bf16)
            log_ref[m, :, rows] = peak + jnp.log2(total)


def key_value_kernel(x_ref, cos_ref, sin_ref, out_ref):
    for h in range(KEY_VALUE_HEADS):
        at = pl.ds(h * HEAD_SIZE, HEAD_SIZE)
        x = x_ref[:, at]
        out_ref[:, at] = (x * cos_ref[...] + roll_half(x) * sin_ref[...]).astype(bf16)
    out_ref[:, KV_WIDTH:] = x_ref[:, KV_WIDTH:].astype(bf16)


def key_value(qkv, cosine, sine):
    tokens = qkv.shape[0]
    table = pl.BlockSpec((tokens, HEAD_SIZE), lambda i: (0, 0))
    return pl.pallas_call(
        key_value_kernel,
        out_shape=jax.ShapeDtypeStruct((tokens, 2 * KV_WIDTH), bf16),
        grid=(1,),
        in_specs=[
            pl.BlockSpec((tokens, 2 * KV_WIDTH), lambda i: (0, Q_WIDTH // (2 * KV_WIDTH))),
            table,
            table,
        ],
        out_specs=pl.BlockSpec((tokens, 2 * KV_WIDTH), lambda i: (0, 0)),
        cost_estimate=cost(
            flops=tokens * KV_WIDTH * 4, bytes_accessed=tokens * KV_WIDTH * 14, transcendentals=0
        ),
        name="key_value",
    )(qkv, cosine, sine)


def key_value_back_kernel(near_ref, came_ref, cos_ref, sin_ref, out_ref):
    for h in range(KEY_VALUE_HEADS):
        at = pl.ds(h * HEAD_SIZE, HEAD_SIZE)
        x = near_ref[:, at] + came_ref[:, at].astype(f32)
        out_ref[:, at] = (x * cos_ref[...] - roll_half(x) * sin_ref[...]).astype(bf16)
    out_ref[:, KV_WIDTH:] = (
        near_ref[:, KV_WIDTH:] + came_ref[:, KV_WIDTH:].astype(f32)
    ).astype(bf16)


def key_value_back(near, came, cosine, sine):
    tokens = near.shape[0]
    return pl.pallas_call(
        key_value_back_kernel,
        out_shape=jax.ShapeDtypeStruct((tokens, 2 * KV_WIDTH), bf16),
        cost_estimate=cost(
            flops=tokens * KV_WIDTH * 6, bytes_accessed=tokens * KV_WIDTH * 18, transcendentals=0
        ),
        name="key_value_back",
    )(near, came, cosine, sine)


PAIR = 6


def attention_specs(tokens):
    head = pl.BlockSpec((tokens, PAIR * HEAD_SIZE), lambda h, place: (0, h))
    key = pl.BlockSpec((tokens, HEAD_SIZE), lambda h, place: (0, h * PAIR // GROUP))
    value = pl.BlockSpec(
        (tokens, HEAD_SIZE), lambda h, place: (0, KEY_VALUE_HEADS + h * PAIR // GROUP)
    )
    table = pl.BlockSpec((tokens, HEAD_SIZE), lambda h, place: (0, 0))
    log = pl.BlockSpec((PAIR, 1, tokens), lambda h, place: (h, 0, 0))
    return head, key, value, table, log


def attention(context, qkv, near, far, cosine, sine):
    tokens = qkv.shape[0]
    head, key, value, table, log = attention_specs(tokens)
    pairs = 2 * tokens * tokens * QUERY_HEADS
    return pl.pallas_call(
        attend_kernel,
        out_shape=(
            jax.ShapeDtypeStruct((tokens, Q_WIDTH), bf16),
            jax.ShapeDtypeStruct((tokens, Q_WIDTH), bf16),
            jax.ShapeDtypeStruct((QUERY_HEADS, 1, tokens), f32),
        ),
        grid_spec=pltpu.PrefetchScalarGridSpec(
            num_scalar_prefetch=1,
            grid=(QUERY_HEADS // PAIR,),
            in_specs=[head, key, value, key, value, table, table],
            out_specs=(head, head, log),
        ),
        compiler_params=pltpu.CompilerParams(
            dimension_semantics=("arbitrary",), vmem_limit_bytes=VMEM_LIMIT
        ),
        cost_estimate=cost(
            flops=4 * pairs * HEAD_SIZE, bytes_accessed=tokens * Q_WIDTH * 10, transcendentals=pairs
        ),
        name="attention",
    )(context, qkv, near, near, far, far, cosine, sine)


def attend_back_kernel(
    place, q_ref, dout_ref, ko_ref, vo_ref, kr_ref, vr_ref, log_ref, cos_ref, sin_ref,
    dq_ref, near_ref, far_ref, dko_ref, dvo_ref, dkr_ref, dvr_ref,
):
    last = ((1,), (1,))
    first = ((0,), (0,))
    scale = 1.0 / math.sqrt(HEAD_SIZE)
    pair = pl.program_id(0)

    @pl.when(lax.rem(pair, GROUP // PAIR) == 0)
    def _():
        for ref in (dko_ref, dvo_ref, dkr_ref, dvr_ref):
            ref[...] = jnp.zeros_like(ref)

    for r in range(q_ref.shape[0] // STRIP):
        rows = pl.ds(r * STRIP, STRIP)
        seen = (r + 1) * STRIP
        dvr = dvo = dkr = dko = 0.0
        for m in range(PAIR):
            lanes = pl.ds(m * HEAD_SIZE, HEAD_SIZE)
            q = q_ref[rows, lanes]
            dout = dout_ref[rows, lanes]
            logs = log_ref[m, :, rows]
            far = dot(kr_ref[...], q, last)
            near = masked(dot(ko_ref[:seen, :], q, last))
            far = jnp.exp2(far * SCORE - jnp.where(place[0] > 0, logs, -mask_fill))
            near = jnp.exp2(near * SCORE - logs)
            dvr = dvr + dot(far.astype(bf16), dout)
            dvo = dvo + dot(near.astype(bf16), dout)
            dfar = dot(vr_ref[...], dout, last)
            dnear = dot(vo_ref[:seen, :], dout, last)
            inner = jnp.sum(far * dfar, axis=0, keepdims=True)
            inner = inner + jnp.sum(near * dnear, axis=0, keepdims=True)
            dfar = (far * (dfar - inner)).astype(bf16)
            dnear = (near * (dnear - inner)).astype(bf16)
            dkr = dkr + dot(dfar, q)
            dko = dko + dot(dnear, q)
            dq = dot(kr_ref[...], dfar, first) + dot(ko_ref[:seen, :], dnear, first)
            dq = dq.T * scale
            dq_ref[rows, lanes] = (dq * cos_ref[rows, :] - roll_half(dq) * sin_ref[rows, :]).astype(bf16)
        dvr_ref[...] += dvr
        dvo_ref[:seen, :] += dvo
        dkr_ref[...] += dkr
        dko_ref[:seen, :] += dko

    for h in range(KEY_VALUE_HEADS):

        @pl.when(pair == (h + 1) * GROUP // PAIR - 1)
        def _(h=h):
            key = pl.ds(h * HEAD_SIZE, HEAD_SIZE)
            value = pl.ds(KV_WIDTH + h * HEAD_SIZE, HEAD_SIZE)
            near_ref[:, key] = dko_ref[...] * scale
            near_ref[:, value] = dvo_ref[...]
            far_ref[:, key] = (dkr_ref[...] * scale).astype(bf16)
            far_ref[:, value] = dvr_ref[...].astype(bf16)


def attention_back(context, query, dmixed, near, far, logs, cosine, sine):
    tokens = query.shape[0]
    head, key, value, table, log = attention_specs(tokens)
    pairs = 2 * tokens * tokens * QUERY_HEADS
    side = pl.BlockSpec((tokens, 2 * KV_WIDTH), lambda h, place: (0, 0))
    return pl.pallas_call(
        attend_back_kernel,
        out_shape=(
            jax.ShapeDtypeStruct((tokens, Q_WIDTH), bf16),
            jax.ShapeDtypeStruct((tokens, 2 * KV_WIDTH), f32),
            jax.ShapeDtypeStruct((tokens, 2 * KV_WIDTH), bf16),
        ),
        grid_spec=pltpu.PrefetchScalarGridSpec(
            num_scalar_prefetch=1,
            grid=(QUERY_HEADS // PAIR,),
            in_specs=[head, head, key, value, key, value, log, table, table],
            out_specs=(head, side, side),
            scratch_shapes=[pltpu.VMEM((tokens, HEAD_SIZE), f32)] * 4,
        ),
        compiler_params=pltpu.CompilerParams(
            dimension_semantics=("arbitrary",), vmem_limit_bytes=VMEM_LIMIT
        ),
        cost_estimate=cost(
            flops=10 * pairs * HEAD_SIZE, bytes_accessed=tokens * Q_WIDTH * 8, transcendentals=pairs
        ),
        name="attention_back",
    )(context, query, dmixed, near, near, far, far, logs, cosine, sine)


def add_all(own, came):
    total = own.astype(f32)
    for c in came:
        total = total + c.astype(f32)
    return total


def scatter_line(total):
    z = lax.axis_size("dp")
    me = lax.axis_index("dp")
    share = lax.dynamic_index_in_dim(total, me, 0, keepdims=False).astype(f32)
    for s in range(1, z):
        sent = lax.dynamic_index_in_dim(total, lax.rem(me + s, z), 0, keepdims=False)
        came = lax.ppermute(sent, "dp", [(i, (i + s) % z) for i in range(z)])
        share = share + came.astype(f32)
    return share.astype(bf16)


def join_rows(share, expert):
    count = lax.axis_size("expert")
    blocks = jnp.stack([share] + [flip(share, k) for k in range(1, count)])
    pieces = [lax.dynamic_index_in_dim(blocks, expert ^ e, 0, keepdims=False) for e in range(count)]
    return jnp.concatenate(pieces, axis=0).astype(f32)


def local(
    hidden_in,
    out_grad,
    routes,
    attn_gain,
    w_query,
    key_projection,
    value_projection,
    w_out,
    ffn_gain,
    w_router,
    w_gate,
    w_up,
    w_down,
):
    expert = lax.axis_index("expert")
    context = lax.axis_index("context")
    count = lax.axis_size("expert")
    z = lax.axis_size("dp")
    tokens = hidden_in.shape[1]
    experts_all = EXP_DEV * count
    per_core = EXP_DEV // 2
    capacity = tokens * TOP * 5 // (4 * experts_all)
    rows = w_query.shape[0]
    piece = rows // count

    def chunk(j):
        parts = []
        for at in range(j, EXP_DEV, per_core):
            parts += [w_gate[at], w_up[at], w_down[at].T]
        return jnp.concatenate([p.astype(bf16) for p in parts], axis=0)

    chunks = [chunk(j) for j in range(per_core)]

    def quarter(parts):
        cut = [
            lax.dynamic_slice_in_dim(p, expert * piece, piece, axis=0).astype(bf16) for p in parts
        ]
        return jnp.concatenate(cut, axis=1)

    pad = jnp.zeros((rows, SMALL - experts_all - 2), f32)
    first_pack = quarter(
        [
            w_query,
            key_projection,
            value_projection,
            w_router,
            attn_gain[:, None],
            ffn_gain[:, None],
            pad,
        ]
    )
    second_both = lax.all_gather(quarter([w_out]), ("context", "dp"), axis=0, tiled=False)
    second_both = second_both.reshape(2, z, piece, MODEL_WIDTH)
    first_pack, chunks[0] = tie(first_pack, chunks[0])
    first_z = lax.all_gather(first_pack, "dp", axis=0, tiled=False)
    own_one, other_one = spread(first_z)
    gathered = [lax.all_gather(chunks[0], ("context", "dp"), axis=0, tiled=False)]
    for sent in chunks[1:]:
        sent = after(sent, first_z)
        gathered.append(lax.all_gather(sent, ("context", "dp"), axis=0, tiled=False))
    gathered = [came.reshape(2 * z, 2, 3, rows, FF) for came in gathered]
    second_z = lax.dynamic_index_in_dim(second_both, context, 0, keepdims=False)
    second_other = lax.dynamic_index_in_dim(second_both, 1 - context, 0, keepdims=False)
    second_came = gather_first(after(second_z, *own_one[1:3]))
    packed = assemble(own_one, other_one, context, expert)
    qkv_w = packed[:, : Q_WIDTH + 2 * KV_WIDTH]
    router_w = packed[:, Q_WIDTH + 2 * KV_WIDTH :][:, :experts_all]
    small = packed[:, Q_WIDTH + 2 * KV_WIDTH :].T
    gain_one = small[experts_all].astype(f32)
    gain_two = small[experts_all + 1].astype(f32)

    route_t = routes[0].T
    expert_ids = jnp.arange(experts_all, dtype=jnp.int32)
    named = jnp.any(route_t[:, None, :] == expert_ids[None, :, None], axis=0)
    earlier = (
        jnp.arange(tokens, dtype=jnp.int32)[:, None] < jnp.arange(tokens, dtype=jnp.int32)[None, :]
    )
    ranks = dot(named.astype(bf16), earlier.astype(bf16))
    slot_code = jnp.where(named & (ranks < capacity), ranks, -1.0)

    inputs_f = hidden_in[0].astype(f32)
    scale_one, norm_one = norm_parts(inputs_f)
    act_one = (norm_one * gain_one).astype(bf16)
    qkv = dot(act_one, qkv_w)
    (qkv,), second_came = tie_lists((qkv,), second_came)
    own_two = [second_z, *second_came, *gather_second(second_came)]
    other_two = [second_other] + [swap(b) for b in own_two[1:]]
    dy_half = after(out_grad[0], *own_two[1:])
    dy_came = gather_first(dy_half)
    cosine, sine = rope_tables(context * tokens, tokens, HEAD_SIZE)
    cos_wide = jnp.concatenate([cosine, cosine], axis=1)
    sin_wide = jnp.concatenate([-sine, sine], axis=1)
    near = key_value(qkv, cos_wide, sin_wide)
    far = lax.ppermute(near, "context", [(0, 1)])
    where = context[None].astype(jnp.int32)
    query, mixed, logs = attention(where, qkv, near, far, cos_wide, sin_wide)
    (mixed,), dy_came = tie_lists((mixed,), dy_came)
    dys_own = [dy_half, *dy_came, *gather_second(dy_came)]
    dys_other = [swap(b) for b in dys_own]
    out_w = assemble(own_two, other_two, context, expert)
    resid_one = inputs_f + dot(mixed, out_w)
    scale_two, norm_two = norm_parts(resid_one)
    act_two = (norm_two * gain_two).astype(bf16)

    logits = dot(router_w, act_two, ((0,), (1,)))
    shown = jnp.where(named, logits, mask_fill)
    exped = jnp.where(named, jnp.exp(shown - jnp.max(shown, axis=0, keepdims=True)), 0.0)
    gates = exped / jnp.sum(exped, axis=0, keepdims=True)
    gates_high = gates.astype(bf16)
    gates_low = (gates - gates_high.astype(f32)).astype(bf16)
    meta = jnp.concatenate([gates_high, gates_low, slot_code.astype(bf16)], axis=1)
    meta = jnp.pad(meta, ((0, -experts_all % 32), (0, 0)))
    payload = jnp.concatenate([act_two, meta], axis=0)
    acts_own, acts_other = spread(after(payload, *dys_own[1:]))

    place = jnp.stack([expert * EXP_DEV + context * per_core, context]).astype(jnp.int32)
    step = jnp.array([1, 0], jnp.int32)
    sums, shares = (), []
    for j in range(per_core):
        final = j == per_core - 1
        *sums, x, gdy, hidden, dgate, dup = run_expert(
            acts_own + acts_other,
            dys_own + dys_other,
            gathered[j],
            place,
            capacity,
            sums,
            final and count == 4,
        )
        if final and count == 4:
            y_own, y_other, d_own, *d_apart = sums
            top = fold_half(d_own, swap(d_apart[0]), lambda i: 2 * i + 1, 0)
            bottom = fold_half(d_own, swap(d_apart[1]), lambda i: i + 2, 1)
            d_came = scatter_first([top, bottom])
            (x, y_other, *d_apart[2:]), (top, bottom) = tie_lists(
                (x, y_other, *d_apart[2:]), (top, bottom)
            )
            keep_top = fold_half(d_own, swap(d_apart[2]), lambda i: 2 * i, 0)
            keep_bottom = fold_half(d_own, swap(d_apart[3]), lambda i: i, 1)
            d_parts = [top, bottom, keep_top, keep_bottom]
        elif final:
            y_own, y_other, d_own, d_other = sums
            d_parts = block_parts(d_own, d_other)
            d_came = scatter_first(d_parts)
        grads = weight_grads(x, gdy, hidden, dgate, dup, z, rows, False)
        (place,), grads = tie_lists((place + step,), grads)
        if final:
            d_came, grads, d_parts = tie_lists(d_came, grads, d_parts)
            d_last = scatter_second(d_parts, d_came)
            y_parts = block_parts(y_own, y_other)
            d_last, y_parts, shares[-1] = tie_lists(d_last, y_parts, shares[-1])
        shares.append([lax.psum_scatter(g, "dp", scatter_dimension=0, tiled=False) for g in grads])
    dact = scatter_total(d_parts, d_came, d_last)
    y_came = scatter_first(y_parts)

    dy = out_grad[0].astype(f32)
    dgates = dact[tokens : tokens + experts_all, : 2 * tokens]
    dgates = dgates[:, :tokens] + dgates[:, tokens:]
    dlogits = (gates * (dgates - jnp.sum(gates * dgates, axis=0, keepdims=True))).astype(bf16)
    dact_two = dact[:tokens] + dot(dlogits, router_w, ((0,), (1,)))
    grad_gain_two = jnp.sum(dact_two * norm_two, axis=0)
    dn2 = dact_two * gain_two
    dresid = dy + scale_two * (dn2 - norm_two * jnp.mean(dn2 * norm_two, axis=-1, keepdims=True))
    dresid_b = dresid.astype(bf16)
    dmixed = dot(dresid_b, out_w, ((1,), (1,))).astype(bf16)

    dquery, near_grad, far_grad = attention_back(
        where, query, dmixed, near, far, logs, cos_wide, sin_wide
    )
    (far_grad,), y_came = tie_lists((far_grad,), y_came)
    came = lax.ppermute(far_grad, "context", [(1, 0)])
    y_last = scatter_second(y_parts, y_came)
    grad_query = dot(act_one, dquery, ((0,), (0,))).astype(bf16)
    dkv = key_value_back(near_grad, came, cos_wide, sin_wide)
    grad_kv = dot(act_one, dkv, ((0,), (0,))).astype(bf16)
    halves = [swap_halves(grad, context) for grad in (grad_query, grad_kv)]
    first_parts = dense_parts(halves, context, expert)
    first_came = scatter_first(first_parts)

    first_parts, (dquery, dkv, dlogits, dresid_b), y_last, shares[0] = tie_lists(
        first_parts, (dquery, dkv, dlogits, dresid_b), y_last, shares[0]
    )
    y_sum = scatter_total(y_parts, y_came, y_last)
    block_out = (resid_one + y_sum).astype(bf16)[None]
    out_halves = swap_halves(dot(mixed, dresid_b, ((0,), (0,))), context)
    dact_one = dot(dquery, qkv_w[:, :Q_WIDTH], ((1,), (1,)))
    dact_one = dact_one + dot(dkv, qkv_w[:, Q_WIDTH:], ((1,), (1,)))
    grad_gain_one = jnp.sum(dact_one * norm_one, axis=0)
    dn1 = dact_one * gain_one
    grad_in = dresid + scale_one * (dn1 - norm_one * jnp.mean(dn1 * norm_one, axis=-1, keepdims=True))
    small = jnp.concatenate(
        [
            dot(dlogits, act_two),
            grad_gain_one[None],
            grad_gain_two[None],
            jnp.zeros((SMALL - experts_all - 2, MODEL_WIDTH), f32),
        ],
        axis=0,
    )
    small = swap_halves(small.T, context)
    (out_theirs, small_theirs), first_came = tie_lists((out_halves[1], small[1]), first_came)
    first_last = scatter_second(first_parts, first_came)
    out_halves = [(out_halves[0], out_theirs), (small[0], small_theirs)]
    out_parts = dense_parts(out_halves, context, expert)
    out_came = scatter_first(out_parts)
    first_total = scatter_total(first_parts, first_came, first_last)
    (first_total,), shares[-1], out_parts = tie_lists(
        (first_total.astype(bf16),), shares[-1], out_parts
    )
    first_share = lax.psum_scatter(first_total, "dp", scatter_dimension=0, tiled=False)
    out_total = scatter_total(out_parts, out_came, scatter_second(out_parts, out_came))
    out_total, first_share = tie(out_total.astype(bf16), first_share)
    first = join_rows(first_share, expert)
    last = join_rows(scatter_line(out_total), expert)
    kv_at = Q_WIDTH + KV_WIDTH

    finals = []
    for pair in shares:
        low, high = pair if len(pair) == 2 else (pair[0][0], pair[0][1])
        keep = jnp.where(context == 0, low, high)
        came = swap(jnp.where(context == 0, high, low))
        finals.append((jnp.where(context == 0, keep, came), jnp.where(context == 0, came, keep)))
    stacked = jnp.stack([f[c] for c in range(2) for f in finals])
    stacked = stacked.astype(f32)
    return (
        block_out,
        grad_in[None],
        last[:, MODEL_WIDTH + experts_all],
        first[:, :Q_WIDTH],
        first[:, Q_WIDTH:kv_at],
        first[:, kv_at:],
        last[:, :MODEL_WIDTH],
        last[:, MODEL_WIDTH + experts_all + 1],
        last[:, MODEL_WIDTH : MODEL_WIDTH + experts_all],
        stacked[:, 0],
        stacked[:, 1],
        jnp.swapaxes(stacked[:, 2], 1, 2),
    )


def solution(mesh):
    tokens_at = P(("expert", "dp"), "context", None)
    vector = P(("context", "dp"))
    matrix = P(("context", "dp"), None)
    wide = P("expert", ("context", "dp"), None)
    down = P("expert", None, ("context", "dp"))
    return jax.shard_map(
        local,
        mesh=mesh,
        in_specs=(
            tokens_at,
            tokens_at,
            tokens_at,
            vector,
            matrix,
            matrix,
            matrix,
            matrix,
            vector,
            matrix,
            wide,
            wide,
            down,
        ),
        out_specs=(
            tokens_at,
            tokens_at,
            vector,
            matrix,
            matrix,
            matrix,
            matrix,
            vector,
            matrix,
            wide,
            wide,
            down,
        ),
        check_vma=False,
    )
```

```python
import functools
import math

import jax
import jax.numpy as jnp
from jax import lax
from jax.experimental import pallas as pl
from jax.experimental.pallas import tpu as pltpu
from jax.sharding import PartitionSpec as P

MODEL_WIDTH = 1536
QUERY_HEADS = 12
KEY_VALUE_HEADS = 2
HEAD_SIZE = 128
FF = 768
TOP = 4
EXP_DEV = 4
GROUP = QUERY_HEADS // KEY_VALUE_HEADS
Q_WIDTH = QUERY_HEADS * HEAD_SIZE
KV_WIDTH = KEY_VALUE_HEADS * HEAD_SIZE
SMALL = 128

norm_eps = 1e-06
rope_base = 1000000.0
mask_fill = -1e30
bf16 = jnp.bfloat16
f32 = jnp.float32
VMEM_LIMIT = 60 * 1024 * 1024


COST_SCALE = 1


def cost(flops, bytes_accessed, transcendentals):
    return pl.CostEstimate(
        flops=flops // COST_SCALE,
        bytes_accessed=bytes_accessed // COST_SCALE,
        transcendentals=transcendentals // COST_SCALE,
    )


def dot(a, b, dims=((1,), (0,))):
    return lax.dot_general(a, b, (dims, ((), ())), preferred_element_type=f32)


def after(value, *others):
    return lax.optimization_barrier((value,) + others)[0]


def tie(*values):
    return lax.optimization_barrier(values)


def flip(value, step):
    count = lax.axis_size("expert")
    return lax.ppermute(value, "expert", [(i, i ^ step) for i in range(count)])


def swap(value):
    return lax.ppermute(value, "context", [(0, 1), (1, 0)])


def rope_tables(start_pos, length, head_dim):
    half_dim = head_dim // 2
    freqs = rope_base ** (-(2.0 * jnp.arange(half_dim, dtype=f32)) / head_dim)
    places = (start_pos + jnp.arange(length, dtype=jnp.int32)).astype(f32)
    angles = places[:, None] * freqs[None, :]
    return (jnp.cos(angles), jnp.sin(angles))


def rotate(heads, cosine, sine):
    half_dim = heads.shape[-1] // 2
    a = heads[..., :half_dim]
    b = heads[..., half_dim:]
    c = cosine[:, None, :]
    s = sine[:, None, :]
    return jnp.concatenate([a * c - b * s, b * c + a * s], axis=-1)


def norm_parts(values):
    scale = lax.rsqrt(jnp.mean(values * values, axis=-1, keepdims=True) + norm_eps)
    return scale, values * scale


def assemble(own, other, context, expert):
    count = len(own)
    z, r, n = own[0].shape
    if r % 16 != 0:
        blocks = jnp.stack([jnp.stack(own), jnp.stack(other)])
        order = jnp.arange(count) ^ expert
        blocks = jnp.take(blocks, order, axis=1)
        blocks = jnp.take(blocks, jnp.arange(2) ^ context, axis=0)
        return jnp.transpose(blocks, (0, 2, 1, 3, 4)).reshape(2 * z * count * r, n)

    def kernel(place, *refs):
        sources, out, sems = refs[: 2 * count], refs[2 * count], refs[2 * count + 1]
        copies = []
        for k in range(count):
            for half in range(2):
                at = place[0] if half == 0 else 1 - place[0]
                copies.append(
                    pltpu.make_async_copy(
                        sources[half * count + k],
                        out.at[at, :, jnp.bitwise_xor(place[1], k)],
                        sems.at[half * count + k],
                    )
                )
        for copy in copies:
            copy.start()
        for copy in copies:
            copy.wait()

    size = 2 * z * count * r * n * 2
    shape = (2, z, count, r, n)
    out = pl.pallas_call(
        kernel,
        out_shape=jax.ShapeDtypeStruct(shape, bf16),
        grid_spec=pltpu.PrefetchScalarGridSpec(
            num_scalar_prefetch=1,
            grid=(1,),
            in_specs=[pl.BlockSpec(memory_space=pl.ANY)] * (2 * count),
            out_specs=pl.BlockSpec(shape, lambda i, place: (0, 0, 0, 0, 0)),
            scratch_shapes=[pltpu.SemaphoreType.DMA((2 * count,))],
        ),
        compiler_params=pltpu.CompilerParams(vmem_limit_bytes=VMEM_LIMIT),
        cost_estimate=cost(flops=0, bytes_accessed=2 * size, transcendentals=0),
        name="assemble",
    )(jnp.stack([context, expert]).astype(jnp.int32), *own, *other)
    return out.reshape(2 * z * count * r, n)


def fourth_block(one, two):
    cut = one.shape[0] // 2
    return jnp.concatenate([flip(one[:cut], 2), flip(two[cut:], 1)], axis=0)


def gather_first(block):
    count = lax.axis_size("expert")
    return [flip(block, k) for k in ((1, 2) if count == 4 else range(1, count))]


def gather_second(came):
    return [fourth_block(*came)] if lax.axis_size("expert") == 4 else []


def gather_blocks(block):
    came = gather_first(block)
    return [block, *came, *gather_second(came)]


def spread(block):
    own = gather_blocks(block)
    return own, [swap(b) for b in own]


def fold_kernel(dense, pairs, place, *refs):
    k, half = pl.program_id(0), pl.program_id(1)
    odd, far = lax.rem(k, 2) == 1, k >= 2
    top, bottom, keep_top, keep_bottom = refs[2 * pairs :]

    def write(out):
        begin = 0
        for own, came in zip(refs[: 2 * pairs : 2], refs[1 : 2 * pairs : 2]):
            lanes = pl.ds(begin, own.shape[-1])
            begin += own.shape[-1]
            if dense:
                out[0, :, :, lanes] = own[0, :, 0] + came[:, 0]
            else:
                out[0, :, lanes] = own[0] + came[0]

    for here, out in (
        ((half == 0) & odd, top),
        ((half == 1) & far, bottom),
        ((half == 0) & jnp.logical_not(odd), keep_top),
        ((half == 1) & jnp.logical_not(far), keep_bottom),
    ):
        pl.when(here)(functools.partial(write, out))


def fold(dense, pairs, place):
    if dense:
        z, _, r, _ = pairs[0][1].shape
        size, rest = z // 2, (r, sum(came.shape[-1] for _, came in pairs))
    else:
        size, rest = pairs[0][0].shape[1] // 2, pairs[0][0].shape[2:]
    specs = []
    for own, came in pairs:
        n = own.shape[-1]
        if dense:
            specs += [
                pl.BlockSpec(
                    (1, size, 1, r, n), lambda k, h, place: (place[0], h, place[1] ^ k, 0, 0)
                ),
                pl.BlockSpec((size, 1, r, n), lambda k, h, place: (h, place[1] ^ k, 0, 0)),
            ]
        else:
            specs += [pl.BlockSpec((1, size, n), lambda k, h, place: (k, h, 0))] * 2
    tail = (0,) * (1 + len(rest))

    def out(at):
        return pl.BlockSpec((1, size, *rest), lambda k, h, place: (at(k), *tail))

    elements = 2 * size * math.prod(rest)
    return list(
        pl.pallas_call(
            functools.partial(fold_kernel, dense, len(pairs)),
            out_shape=[jax.ShapeDtypeStruct((2, size, *rest), bf16)] * 4,
            grid_spec=pltpu.PrefetchScalarGridSpec(
                num_scalar_prefetch=1,
                grid=(4, 2),
                in_specs=specs,
                out_specs=[
                    out(lambda k: lax.div(k, 2)),
                    out(lambda k: jnp.maximum(k - 2, 0)),
                    out(lambda k: lax.div(k, 2)),
                    out(lambda k: jnp.minimum(k, 1)),
                ],
            ),
            compiler_params=pltpu.CompilerParams(
                dimension_semantics=("arbitrary", "arbitrary"), vmem_limit_bytes=VMEM_LIMIT
            ),
            cost_estimate=cost(flops=4 * elements, bytes_accessed=24 * elements, transcendentals=0),
            name="fold",
        )(place, *(v for pair in pairs for v in pair))
    )


def fold_half_kernel(own_ref, came_ref, out_ref):
    out_ref[...] = own_ref[...] + came_ref[...]


def fold_half(own, came, block, half):
    spec = pl.BlockSpec((1, *came.shape[1:]), lambda i: (i, 0, 0))
    return pl.pallas_call(
        fold_half_kernel,
        out_shape=jax.ShapeDtypeStruct(came.shape, bf16),
        grid=(2,),
        in_specs=[pl.BlockSpec((1, *came.shape[1:]), lambda i: (block(i), half, 0)), spec],
        out_specs=spec,
        compiler_params=pltpu.CompilerParams(dimension_semantics=("arbitrary",)),
        cost_estimate=cost(flops=came.size, bytes_accessed=6 * came.size, transcendentals=0),
        name="fold_half",
    )(own, came)


def block_parts(own, other):
    came = swap(other)
    if lax.axis_size("expert") == 4:
        return fold(False, [(own, came)], jnp.zeros((2,), jnp.int32))
    return [(own[i].astype(f32) + came[i].astype(f32)).astype(bf16) for i in range(own.shape[0])]


def swap_halves(grad, context):
    z = lax.axis_size("dp")
    count = lax.axis_size("expert")
    r = grad.shape[0] // (2 * z * count)
    grad = grad.astype(bf16).reshape(2, z, count, r, grad.shape[1])
    return grad, swap(lax.dynamic_index_in_dim(grad, 1 - context, 0, keepdims=False))


def dense_parts(halves, context, expert):
    if lax.axis_size("expert") == 4 and halves[0][0].shape[3] % 16 == 0:
        return fold(True, halves, jnp.stack([context, expert]).astype(jnp.int32))
    out = []
    for k in range(lax.axis_size("expert")):
        sums = []
        for grad, theirs in halves:
            mine = lax.dynamic_index_in_dim(grad, context, 0, keepdims=False)
            a, b = (lax.dynamic_index_in_dim(p, expert ^ k, 1, keepdims=False) for p in (mine, theirs))
            sums.append(a.astype(f32) + b.astype(f32))
        out.append(jnp.concatenate(sums, axis=-1).astype(bf16))
    return out


def scatter_first(parts):
    count = lax.axis_size("expert")
    if count != 4:
        return [flip(parts[k], k) for k in range(1, count)]
    return [flip(parts[0], 1), flip(parts[1], 2)]


def scatter_second(parts, came):
    if lax.axis_size("expert") != 4:
        return []
    top = add_all(parts[2][1], [came[0][1]]).astype(bf16)
    bottom = add_all(parts[3][1], [came[1][1]]).astype(bf16)
    return [flip(top, 2), flip(bottom, 1)]


def scatter_total(parts, came, last):
    if lax.axis_size("expert") != 4:
        return add_all(parts[0], came)
    top = add_all(parts[2][0], [came[0][0], last[0]])
    bottom = add_all(parts[3][0], [came[1][0], last[1]])
    return jnp.concatenate([top, bottom], axis=0)


def tie_lists(*lists):
    flat = iter(tie(*(v for values in lists for v in values)))
    return [[next(flat) for _ in values] for values in lists]


GELU_C = math.sqrt(2.0 / math.pi)


def expert_kernel(count, tokens, capacity, apart, place, *refs):
    acts, dys = refs[: 2 * count], refs[2 * count : 4 * count]
    w_ref, refs = refs[4 * count], refs[4 * count + 1 :]
    sums = 7 if apart else 4
    earlier, refs = refs[: len(refs) - sums - 10], refs[len(refs) - sums - 10 :]
    y_refs, d_refs = refs[:2], refs[2:sums]
    x_ref, gdy_ref, h_ref, dg_ref, du_ref, abuf, dbuf, wbuf, sems, wsems = refs[sums:]
    step = pl.program_id(0)
    slot = lax.rem(step, 2)

    def copies(k, at):
        out = []
        for s in range(2):
            out.append(pltpu.make_async_copy(acts[s * count + k], abuf.at[at, s], sems.at[at, s]))
            out.append(pltpu.make_async_copy(dys[s * count + k], dbuf.at[at, s], sems.at[at, 2 + s]))
        return out

    def weight_copies():
        return [
            pltpu.make_async_copy(w_ref.at[:, place[1], i], wbuf.at[i], wsems.at[i]) for i in range(3)
        ]

    @pl.when(step == 0)
    def _():
        for c in copies(0, 0) + weight_copies():
            c.start()

    for k in range(1, count):

        @pl.when(step == k - 1)
        def _(k=k):
            for c in copies(k, k % 2):
                c.start()

    for k in range(count):

        @pl.when(step == k)
        def _(k=k):
            for c in copies(k, k % 2):
                c.wait()

    row = place[0]
    extra = abuf.shape[2] - tokens
    row_ids = lax.broadcasted_iota(jnp.int32, (extra, 3 * tokens), 0)
    slot_ids = lax.broadcasted_iota(jnp.int32, (capacity, tokens), 0).astype(f32)
    hits = []
    gate_cols = []
    for s in range(2):
        meta = abuf[slot, s, tokens:, :].astype(f32)
        line = jnp.sum(jnp.where(row_ids == row, meta, 0.0), axis=0, keepdims=True)
        gate_line = line[:, :tokens] + line[:, tokens : 2 * tokens]
        hit = slot_ids == line[:, 2 * tokens :]
        hits.append(hit)
        gate_col = jnp.sum(jnp.where(hit, gate_line, 0.0), axis=1, keepdims=True)
        gate_cols.append(gate_col)
        one = jnp.where(hit, 1.0, 0.0).astype(bf16)
        at = pl.ds(s * capacity, capacity)
        x_ref[at, :] = dot(one, abuf[slot, s, :tokens, :]).astype(bf16)
        gdy_ref[at, :] = dot(one, dbuf[slot, s]).astype(bf16)
    gate_col = jnp.concatenate(gate_cols, axis=0)
    @pl.when(step == 0)
    def _():
        for c in weight_copies():
            c.wait()

    w_gate, w_up, w_down = (wbuf[i].reshape(-1, FF) for i in range(3))
    x = x_ref[...]
    dy = gdy_ref[...]
    gate_h = dot(x, w_gate)
    up_h = dot(x, w_up)
    back = dot(dy, w_down)
    square = gate_h * gate_h
    tanh = jnp.tanh(GELU_C * gate_h * (1.0 + 0.044715 * square))
    half = 0.5 * (1.0 + tanh)
    gelu = gate_h * half
    slope = half + 0.5 * gate_h * (1.0 - tanh * tanh) * (GELU_C * (1.0 + 3 * 0.044715 * square))
    hidden = (gelu * up_h).astype(bf16)
    dgate_col = jnp.sum(hidden.astype(f32) * back, axis=1, keepdims=True)
    dhidden = back * gate_col
    dgate_h = (dhidden * up_h * slope).astype(bf16)
    dup_h = (dhidden * gelu).astype(bf16)
    h_ref[...] = hidden
    dg_ref[...] = dgate_h
    du_ref[...] = dup_h
    gdy_ref[...] = (dy.astype(f32) * gate_col).astype(bf16)
    result = (dot(hidden, w_down, ((1,), (1,))) * gate_col).astype(bf16)
    dx = (dot(dgate_h, w_gate, ((1,), (1,))) + dot(dup_h, w_up, ((1,), (1,)))).astype(bf16)
    for s in range(2):
        one = jnp.where(hits[s], 1.0, 0.0).astype(bf16)
        rows = slice(s * capacity, (s + 1) * capacity)
        y = dot(one, result[rows], ((0,), (0,)))
        d = dot(one, dx[rows], ((0,), (0,)))
        line = jnp.sum(jnp.where(hits[s], dgate_col[rows], 0.0), axis=0, keepdims=True)
        high = line.astype(bf16).astype(f32)
        line = jnp.concatenate([high, line - high, jnp.zeros_like(high)], axis=1)
        line = jnp.where(row_ids == row, line, 0.0)
        if earlier:
            y = y + earlier[s][0].astype(f32)
            d = d + earlier[2 + s][0, :tokens].astype(f32)
            line = line + earlier[2 + s][0, tokens:].astype(f32)
        y_refs[s][0] = y.astype(bf16)
        d, line = d.astype(bf16), line.astype(bf16)
        if s == 0 or not apart:
            d_refs[s][0, :tokens] = d
            d_refs[s][0, tokens:] = line
            continue
        cut = d_refs[1].shape[1]
        odd, far = lax.rem(step, 2) == 1, step >= 2

        def write_top(ref, d=d):
            ref[0] = d[:cut]

        def write_bottom(ref, d=d, line=line):
            ref[0, : tokens - cut] = d[cut:]
            ref[0, tokens - cut :] = line

        for here, write, ref in zip(
            (odd, far, jnp.logical_not(odd), jnp.logical_not(far)),
            (write_top, write_bottom, write_top, write_bottom),
            d_refs[1:],
        ):
            pl.when(here)(functools.partial(write, ref))


def run_expert(acts, dys, weights, place, capacity, earlier, apart):
    count = len(acts) // 2
    tokens = dys[0].shape[0]
    rows = acts[0].shape[0]
    cz, _, _, local, _ = weights.shape
    slots = 2 * capacity
    total = count * slots
    widths = (MODEL_WIDTH, MODEL_WIDTH, FF, FF, FF)
    macs = total * (6 * MODEL_WIDTH * FF + 4 * tokens * MODEL_WIDTH)
    moved = 2 * (4 * count * (rows + tokens) * MODEL_WIDTH + total * sum(widths) + 3 * MODEL_WIDTH * FF)

    def block(n):
        return pl.BlockSpec((1, n, MODEL_WIDTH), lambda i, place: (i, 0, 0))

    def half(at):
        return pl.BlockSpec((1, rows // 2, MODEL_WIDTH), lambda i, place: (at(i), 0, 0))

    sums = [block(n) for n in (tokens, tokens, rows, rows)]
    shapes = [jax.ShapeDtypeStruct((count, n, MODEL_WIDTH), bf16) for n in (tokens, tokens, rows, rows)]
    outs = list(sums)
    if apart:
        outs[3:] = [
            half(lambda i: lax.div(i, 2)),
            half(lambda i: jnp.maximum(i - 2, 0)),
            half(lambda i: lax.div(i, 2)),
            half(lambda i: jnp.minimum(i, 1)),
        ]
        shapes[3:] = [jax.ShapeDtypeStruct((2, rows // 2, MODEL_WIDTH), bf16)] * 4
    return pl.pallas_call(
        functools.partial(expert_kernel, count, tokens, capacity, apart),
        out_shape=(*shapes, *(jax.ShapeDtypeStruct((total, n), bf16) for n in widths)),
        grid_spec=pltpu.PrefetchScalarGridSpec(
            num_scalar_prefetch=1,
            grid=(count,),
            in_specs=[pl.BlockSpec(memory_space=pl.ANY)] * (4 * count)
            + [pl.BlockSpec(memory_space=pl.ANY)]
            + (sums if earlier else []),
            out_specs=(*outs, *(pl.BlockSpec((slots, n), lambda i, place: (i, 0)) for n in widths)),
            scratch_shapes=[
                pltpu.VMEM((2, 2, rows, MODEL_WIDTH), bf16),
                pltpu.VMEM((2, 2, tokens, MODEL_WIDTH), bf16),
                pltpu.VMEM((3, cz, local, FF), bf16),
                pltpu.SemaphoreType.DMA((2, 4)),
                pltpu.SemaphoreType.DMA((3,)),
            ],
        ),
        compiler_params=pltpu.CompilerParams(
            dimension_semantics=("arbitrary",), vmem_limit_bytes=VMEM_LIMIT
        ),
        cost_estimate=cost(
            flops=2 * macs, bytes_accessed=moved, transcendentals=total * FF
        ),
        name="experts",
    )(place, *acts, *dys, weights, *earlier)


def weight_grad_kernel(per, x_ref, gdy_ref, h_ref, dg_ref, du_ref, *out_refs):
    first = ((0,), (0,))

    def write(out_ref):
        shape = (out_ref.shape[0], out_ref.shape[2], FF)
        x = x_ref[...]
        out_ref[:, 0] = dot(x, dg_ref[...], first).astype(bf16).reshape(shape)
        out_ref[:, 1] = dot(x, du_ref[...], first).astype(bf16).reshape(shape)
        out_ref[:, 2] = dot(gdy_ref[...], h_ref[...], first).astype(bf16).reshape(shape)

    if len(out_refs) == 1:
        write(out_refs[0].at[:, 0])
    else:
        for c, out_ref in enumerate(out_refs):
            pl.when(lax.div(pl.program_id(0), per) == c)(functools.partial(write, out_ref))


def weight_grads(x, gdy, hidden, dgate, dup, z, local, split):
    total = x.shape[0]
    wide = 384
    per = MODEL_WIDTH // 2 // wide
    full = pl.BlockSpec((total, FF), lambda i: (0, 0))
    column = pl.BlockSpec((total, wide), lambda i: (0, i))
    block = wide // local
    if split:
        shapes = [jax.ShapeDtypeStruct((z, 3, local, FF), bf16)] * 2
        specs = [
            pl.BlockSpec((block, 3, local, FF), lambda i: (jnp.minimum(i, per - 1), 0, 0, 0)),
            pl.BlockSpec((block, 3, local, FF), lambda i: (jnp.maximum(i - per, 0), 0, 0, 0)),
        ]
    else:
        shapes = [jax.ShapeDtypeStruct((z, 2, 3, local, FF), bf16)]
        specs = [
            pl.BlockSpec(
                (block, 1, 3, local, FF), lambda i: (lax.rem(i, per), lax.div(i, per), 0, 0, 0)
            )
        ]
    return pl.pallas_call(
        functools.partial(weight_grad_kernel, per),
        out_shape=shapes,
        grid=(MODEL_WIDTH // wide,),
        in_specs=[column, column, full, full, full],
        out_specs=specs,
        compiler_params=pltpu.CompilerParams(
            dimension_semantics=("arbitrary",), vmem_limit_bytes=VMEM_LIMIT
        ),
        cost_estimate=cost(
            flops=6 * total * MODEL_WIDTH * FF,
            bytes_accessed=2 * (total * (2 * MODEL_WIDTH + 3 * FF) + 3 * MODEL_WIDTH * FF),
            transcendentals=0,
        ),
        name="weight_grads",
    )(x, gdy, hidden, dgate, dup)


SCORE = math.log2(math.e) / math.sqrt(HEAD_SIZE)
STRIP = 512


def roll_half(x):
    return pltpu.roll(x, HEAD_SIZE // 2, 1)


def masked(scores):
    key = lax.broadcasted_iota(jnp.int32, (STRIP, STRIP), 0)
    seen = key <= lax.broadcasted_iota(jnp.int32, (STRIP, STRIP), 1)
    square = jnp.where(seen, scores[-STRIP:], mask_fill)
    return jnp.concatenate([scores[:-STRIP], square], axis=0) if scores.shape[0] > STRIP else square


def attend_kernel(place, q_ref, ko_ref, vo_ref, kr_ref, vr_ref, cos_ref, sin_ref, rot_ref, mix_ref, log_ref):
    last = ((1,), (1,))
    first = ((0,), (0,))
    for m in range(PAIR):
        lanes = pl.ds(m * HEAD_SIZE, HEAD_SIZE)
        q = q_ref[:, lanes]
        rot_ref[:, lanes] = (q * cos_ref[...] + roll_half(q) * sin_ref[...]).astype(bf16)
    for r in range(q_ref.shape[0] // STRIP):
        rows = pl.ds(r * STRIP, STRIP)
        seen = (r + 1) * STRIP
        for m in range(PAIR):
            lanes = pl.ds(m * HEAD_SIZE, HEAD_SIZE)
            q = rot_ref[rows, lanes]
            far = dot(kr_ref[...], q, last)
            near = masked(dot(ko_ref[:seen, :], q, last))
            far_peak = jnp.where(place[0] > 0, jnp.max(far, axis=0, keepdims=True), mask_fill)
            peak = jnp.maximum(far_peak, jnp.max(near, axis=0, keepdims=True)) * SCORE
            far = jnp.exp2(far * SCORE - jnp.where(place[0] > 0, peak, -mask_fill))
            near = jnp.exp2(near * SCORE - peak)
            total = jnp.sum(far, axis=0, keepdims=True) + jnp.sum(near, axis=0, keepdims=True)
            out = dot(vr_ref[...], far.astype(bf16), first)
            out = out + dot(vo_ref[:seen, :], near.astype(bf16), first)
            mix_ref[rows, lanes] = (out / total).T.astype(bf16)
            log_ref[m, :, rows] = peak + jnp.log2(total)


def key_value_kernel(x_ref, cos_ref, sin_ref, out_ref):
    for h in range(KEY_VALUE_HEADS):
        at = pl.ds(h * HEAD_SIZE, HEAD_SIZE)
        x = x_ref[:, at]
        out_ref[:, at] = (x * cos_ref[...] + roll_half(x) * sin_ref[...]).astype(bf16)
    out_ref[:, KV_WIDTH:] = x_ref[:, KV_WIDTH:].astype(bf16)


def key_value(qkv, cosine, sine):
    tokens = qkv.shape[0]
    table = pl.BlockSpec((tokens, HEAD_SIZE), lambda i: (0, 0))
    return pl.pallas_call(
        key_value_kernel,
        out_shape=jax.ShapeDtypeStruct((tokens, 2 * KV_WIDTH), bf16),
        grid=(1,),
        in_specs=[
            pl.BlockSpec((tokens, 2 * KV_WIDTH), lambda i: (0, Q_WIDTH // (2 * KV_WIDTH))),
            table,
            table,
        ],
        out_specs=pl.BlockSpec((tokens, 2 * KV_WIDTH), lambda i: (0, 0)),
        cost_estimate=cost(
            flops=tokens * KV_WIDTH * 4, bytes_accessed=tokens * KV_WIDTH * 14, transcendentals=0
        ),
        name="key_value",
    )(qkv, cosine, sine)


def key_value_back_kernel(near_ref, came_ref, cos_ref, sin_ref, out_ref):
    for h in range(KEY_VALUE_HEADS):
        at = pl.ds(h * HEAD_SIZE, HEAD_SIZE)
        x = near_ref[:, at] + came_ref[:, at].astype(f32)
        out_ref[:, at] = (x * cos_ref[...] - roll_half(x) * sin_ref[...]).astype(bf16)
    out_ref[:, KV_WIDTH:] = (
        near_ref[:, KV_WIDTH:] + came_ref[:, KV_WIDTH:].astype(f32)
    ).astype(bf16)


def key_value_back(near, came, cosine, sine):
    tokens = near.shape[0]
    return pl.pallas_call(
        key_value_back_kernel,
        out_shape=jax.ShapeDtypeStruct((tokens, 2 * KV_WIDTH), bf16),
        cost_estimate=cost(
            flops=tokens * KV_WIDTH * 6, bytes_accessed=tokens * KV_WIDTH * 18, transcendentals=0
        ),
        name="key_value_back",
    )(near, came, cosine, sine)


PAIR = 6


def attention_specs(tokens):
    head = pl.BlockSpec((tokens, PAIR * HEAD_SIZE), lambda h, place: (0, h))
    key = pl.BlockSpec((tokens, HEAD_SIZE), lambda h, place: (0, h * PAIR // GROUP))
    value = pl.BlockSpec(
        (tokens, HEAD_SIZE), lambda h, place: (0, KEY_VALUE_HEADS + h * PAIR // GROUP)
    )
    table = pl.BlockSpec((tokens, HEAD_SIZE), lambda h, place: (0, 0))
    log = pl.BlockSpec((PAIR, 1, tokens), lambda h, place: (h, 0, 0))
    return head, key, value, table, log


def attention(context, qkv, near, far, cosine, sine):
    tokens = qkv.shape[0]
    head, key, value, table, log = attention_specs(tokens)
    pairs = 2 * tokens * tokens * QUERY_HEADS
    return pl.pallas_call(
        attend_kernel,
        out_shape=(
            jax.ShapeDtypeStruct((tokens, Q_WIDTH), bf16),
            jax.ShapeDtypeStruct((tokens, Q_WIDTH), bf16),
            jax.ShapeDtypeStruct((QUERY_HEADS, 1, tokens), f32),
        ),
        grid_spec=pltpu.PrefetchScalarGridSpec(
            num_scalar_prefetch=1,
            grid=(QUERY_HEADS // PAIR,),
            in_specs=[head, key, value, key, value, table, table],
            out_specs=(head, head, log),
        ),
        compiler_params=pltpu.CompilerParams(
            dimension_semantics=("arbitrary",), vmem_limit_bytes=VMEM_LIMIT
        ),
        cost_estimate=cost(
            flops=4 * pairs * HEAD_SIZE, bytes_accessed=tokens * Q_WIDTH * 10, transcendentals=pairs
        ),
        name="attention",
    )(context, qkv, near, near, far, far, cosine, sine)


def attend_back_kernel(
    place, q_ref, dout_ref, ko_ref, vo_ref, kr_ref, vr_ref, log_ref, cos_ref, sin_ref,
    dq_ref, near_ref, far_ref, dko_ref, dvo_ref, dkr_ref, dvr_ref,
):
    last = ((1,), (1,))
    first = ((0,), (0,))
    scale = 1.0 / math.sqrt(HEAD_SIZE)
    pair = pl.program_id(0)

    @pl.when(lax.rem(pair, GROUP // PAIR) == 0)
    def _():
        for ref in (dko_ref, dvo_ref, dkr_ref, dvr_ref):
            ref[...] = jnp.zeros_like(ref)

    for r in range(q_ref.shape[0] // STRIP):
        rows = pl.ds(r * STRIP, STRIP)
        seen = (r + 1) * STRIP
        dvr = dvo = dkr = dko = 0.0
        for m in range(PAIR):
            lanes = pl.ds(m * HEAD_SIZE, HEAD_SIZE)
            q = q_ref[rows, lanes]
            dout = dout_ref[rows, lanes]
            logs = log_ref[m, :, rows]
            far = dot(kr_ref[...], q, last)
            near = masked(dot(ko_ref[:seen, :], q, last))
            far = jnp.exp2(far * SCORE - jnp.where(place[0] > 0, logs, -mask_fill))
            near = jnp.exp2(near * SCORE - logs)
            dvr = dvr + dot(far.astype(bf16), dout)
            dvo = dvo + dot(near.astype(bf16), dout)
            dfar = dot(vr_ref[...], dout, last)
            dnear = dot(vo_ref[:seen, :], dout, last)
            inner = jnp.sum(far * dfar, axis=0, keepdims=True)
            inner = inner + jnp.sum(near * dnear, axis=0, keepdims=True)
            dfar = (far * (dfar - inner)).astype(bf16)
            dnear = (near * (dnear - inner)).astype(bf16)
            dkr = dkr + dot(dfar, q)
            dko = dko + dot(dnear, q)
            dq = dot(kr_ref[...], dfar, first) + dot(ko_ref[:seen, :], dnear, first)
            dq = dq.T * scale
            dq_ref[rows, lanes] = (dq * cos_ref[rows, :] - roll_half(dq) * sin_ref[rows, :]).astype(bf16)
        dvr_ref[...] += dvr
        dvo_ref[:seen, :] += dvo
        dkr_ref[...] += dkr
        dko_ref[:seen, :] += dko

    for h in range(KEY_VALUE_HEADS):

        @pl.when(pair == (h + 1) * GROUP // PAIR - 1)
        def _(h=h):
            key = pl.ds(h * HEAD_SIZE, HEAD_SIZE)
            value = pl.ds(KV_WIDTH + h * HEAD_SIZE, HEAD_SIZE)
            near_ref[:, key] = dko_ref[...] * scale
            near_ref[:, value] = dvo_ref[...]
            far_ref[:, key] = (dkr_ref[...] * scale).astype(bf16)
            far_ref[:, value] = dvr_ref[...].astype(bf16)


def attention_back(context, query, dmixed, near, far, logs, cosine, sine):
    tokens = query.shape[0]
    head, key, value, table, log = attention_specs(tokens)
    pairs = 2 * tokens * tokens * QUERY_HEADS
    side = pl.BlockSpec((tokens, 2 * KV_WIDTH), lambda h, place: (0, 0))
    return pl.pallas_call(
        attend_back_kernel,
        out_shape=(
            jax.ShapeDtypeStruct((tokens, Q_WIDTH), bf16),
            jax.ShapeDtypeStruct((tokens, 2 * KV_WIDTH), f32),
            jax.ShapeDtypeStruct((tokens, 2 * KV_WIDTH), bf16),
        ),
        grid_spec=pltpu.PrefetchScalarGridSpec(
            num_scalar_prefetch=1,
            grid=(QUERY_HEADS // PAIR,),
            in_specs=[head, head, key, value, key, value, log, table, table],
            out_specs=(head, side, side),
            scratch_shapes=[pltpu.VMEM((tokens, HEAD_SIZE), f32)] * 4,
        ),
        compiler_params=pltpu.CompilerParams(
            dimension_semantics=("arbitrary",), vmem_limit_bytes=VMEM_LIMIT
        ),
        cost_estimate=cost(
            flops=10 * pairs * HEAD_SIZE, bytes_accessed=tokens * Q_WIDTH * 8, transcendentals=pairs
        ),
        name="attention_back",
    )(context, query, dmixed, near, near, far, far, logs, cosine, sine)


def add_all(own, came):
    total = own.astype(f32)
    for c in came:
        total = total + c.astype(f32)
    return total


def scatter_line(total):
    z = lax.axis_size("dp")
    me = lax.axis_index("dp")
    share = lax.dynamic_index_in_dim(total, me, 0, keepdims=False).astype(f32)
    for s in range(1, z):
        sent = lax.dynamic_index_in_dim(total, lax.rem(me + s, z), 0, keepdims=False)
        came = lax.ppermute(sent, "dp", [(i, (i + s) % z) for i in range(z)])
        share = share + came.astype(f32)
    return share.astype(bf16)


def join_rows(share, expert):
    count = lax.axis_size("expert")
    blocks = jnp.stack([share] + [flip(share, k) for k in range(1, count)])
    pieces = [lax.dynamic_index_in_dim(blocks, expert ^ e, 0, keepdims=False) for e in range(count)]
    return jnp.concatenate(pieces, axis=0).astype(f32)


def local(
    hidden_in,
    out_grad,
    routes,
    attn_gain,
    w_query,
    key_projection,
    value_projection,
    w_out,
    ffn_gain,
    w_router,
    w_gate,
    w_up,
    w_down,
):
    expert = lax.axis_index("expert")
    context = lax.axis_index("context")
    count = lax.axis_size("expert")
    z = lax.axis_size("dp")
    tokens = hidden_in.shape[1]
    experts_all = EXP_DEV * count
    per_core = EXP_DEV // 2
    capacity = tokens * TOP * 5 // (4 * experts_all)
    rows = w_query.shape[0]
    piece = rows // count

    def chunk(j):
        parts = []
        for at in range(j, EXP_DEV, per_core):
            parts += [w_gate[at], w_up[at], w_down[at].T]
        return jnp.concatenate([p.astype(bf16) for p in parts], axis=0)

    chunks = [chunk(j) for j in range(per_core)]

    def quarter(parts):
        cut = [
            lax.dynamic_slice_in_dim(p, expert * piece, piece, axis=0).astype(bf16) for p in parts
        ]
        return jnp.concatenate(cut, axis=1)

    pad = jnp.zeros((rows, SMALL - experts_all - 2), f32)
    first_pack = quarter(
        [
            w_query,
            key_projection,
            value_projection,
            w_router,
            attn_gain[:, None],
            ffn_gain[:, None],
            pad,
        ]
    )
    second_both = lax.all_gather(quarter([w_out]), ("context", "dp"), axis=0, tiled=False)
    second_both = second_both.reshape(2, z, piece, MODEL_WIDTH)
    first_pack, chunks[0] = tie(first_pack, chunks[0])
    first_z = lax.all_gather(first_pack, "dp", axis=0, tiled=False)
    own_one, other_one = spread(first_z)
    gathered = [lax.all_gather(chunks[0], ("context", "dp"), axis=0, tiled=False)]
    for sent in chunks[1:]:
        sent = after(sent, first_z)
        gathered.append(lax.all_gather(sent, ("context", "dp"), axis=0, tiled=False))
    gathered = [came.reshape(2 * z, 2, 3, rows, FF) for came in gathered]
    second_z = lax.dynamic_index_in_dim(second_both, context, 0, keepdims=False)
    second_other = lax.dynamic_index_in_dim(second_both, 1 - context, 0, keepdims=False)
    second_came = gather_first(after(second_z, *own_one[1:3]))
    packed = assemble(own_one, other_one, context, expert)
    qkv_w = packed[:, : Q_WIDTH + 2 * KV_WIDTH]
    router_w = packed[:, Q_WIDTH + 2 * KV_WIDTH :][:, :experts_all]
    small = packed[:, Q_WIDTH + 2 * KV_WIDTH :].T
    gain_one = small[experts_all].astype(f32)
    gain_two = small[experts_all + 1].astype(f32)

    route_t = routes[0].T
    expert_ids = jnp.arange(experts_all, dtype=jnp.int32)
    named = jnp.any(route_t[:, None, :] == expert_ids[None, :, None], axis=0)
    earlier = (
        jnp.arange(tokens, dtype=jnp.int32)[:, None] < jnp.arange(tokens, dtype=jnp.int32)[None, :]
    )
    ranks = dot(named.astype(bf16), earlier.astype(bf16))
    slot_code = jnp.where(named & (ranks < capacity), ranks, -1.0)

    inputs_f = hidden_in[0].astype(f32)
    scale_one, norm_one = norm_parts(inputs_f)
    act_one = (norm_one * gain_one).astype(bf16)
    qkv = dot(act_one, qkv_w)
    (qkv,), second_came = tie_lists((qkv,), second_came)
    own_two = [second_z, *second_came, *gather_second(second_came)]
    other_two = [second_other] + [swap(b) for b in own_two[1:]]
    dy_half = after(out_grad[0], *own_two[1:])
    dy_came = gather_first(dy_half)
    cosine, sine = rope_tables(context * tokens, tokens, HEAD_SIZE)
    cos_wide = jnp.concatenate([cosine, cosine], axis=1)
    sin_wide = jnp.concatenate([-sine, sine], axis=1)
    near = key_value(qkv, cos_wide, sin_wide)
    far = lax.ppermute(near, "context", [(0, 1)])
    where = context[None].astype(jnp.int32)
    query, mixed, logs = attention(where, qkv, near, far, cos_wide, sin_wide)
    (mixed,), dy_came = tie_lists((mixed,), dy_came)
    dys_own = [dy_half, *dy_came, *gather_second(dy_came)]
    dys_other = [swap(b) for b in dys_own]
    out_w = assemble(own_two, other_two, context, expert)
    resid_one = inputs_f + dot(mixed, out_w)
    scale_two, norm_two = norm_parts(resid_one)
    act_two = (norm_two * gain_two).astype(bf16)

    logits = dot(router_w, act_two, ((0,), (1,)))
    shown = jnp.where(named, logits, mask_fill)
    exped = jnp.where(named, jnp.exp(shown - jnp.max(shown, axis=0, keepdims=True)), 0.0)
    gates = exped / jnp.sum(exped, axis=0, keepdims=True)
    gates_high = gates.astype(bf16)
    gates_low = (gates - gates_high.astype(f32)).astype(bf16)
    meta = jnp.concatenate([gates_high, gates_low, slot_code.astype(bf16)], axis=1)
    meta = jnp.pad(meta, ((0, -experts_all % 32), (0, 0)))
    payload = jnp.concatenate([act_two, meta], axis=0)
    acts_own, acts_other = spread(after(payload, *dys_own[1:]))

    place = jnp.stack([expert * EXP_DEV + context * per_core, context]).astype(jnp.int32)
    step = jnp.array([1, 0], jnp.int32)
    sums, shares = (), []
    for j in range(per_core):
        final = j == per_core - 1
        *sums, x, gdy, hidden, dgate, dup = run_expert(
            acts_own + acts_other,
            dys_own + dys_other,
            gathered[j],
            place,
            capacity,
            sums,
            final and count == 4,
        )
        if final and count == 4:
            y_own, y_other, d_own, *d_apart = sums
            top = fold_half(d_own, swap(d_apart[0]), lambda i: 2 * i + 1, 0)
            bottom = fold_half(d_own, swap(d_apart[1]), lambda i: i + 2, 1)
            d_came = scatter_first([top, bottom])
            (x, y_other, *d_apart[2:]), (top, bottom) = tie_lists(
                (x, y_other, *d_apart[2:]), (top, bottom)
            )
            keep_top = fold_half(d_own, swap(d_apart[2]), lambda i: 2 * i, 0)
            keep_bottom = fold_half(d_own, swap(d_apart[3]), lambda i: i, 1)
            d_parts = [top, bottom, keep_top, keep_bottom]
        elif final:
            y_own, y_other, d_own, d_other = sums
            d_parts = block_parts(d_own, d_other)
            d_came = scatter_first(d_parts)
        grads = weight_grads(x, gdy, hidden, dgate, dup, z, rows, False)
        (place,), grads = tie_lists((place + step,), grads)
        if final:
            d_came, grads, d_parts = tie_lists(d_came, grads, d_parts)
            d_last = scatter_second(d_parts, d_came)
            y_parts = block_parts(y_own, y_other)
            d_last, y_parts, shares[-1] = tie_lists(d_last, y_parts, shares[-1])
        shares.append([lax.psum_scatter(g, "dp", scatter_dimension=0, tiled=False) for g in grads])
    dact = scatter_total(d_parts, d_came, d_last)
    y_came = scatter_first(y_parts)

    dy = out_grad[0].astype(f32)
    dgates = dact[tokens : tokens + experts_all, : 2 * tokens]
    dgates = dgates[:, :tokens] + dgates[:, tokens:]
    dlogits = (gates * (dgates - jnp.sum(gates * dgates, axis=0, keepdims=True))).astype(bf16)
    dact_two = dact[:tokens] + dot(dlogits, router_w, ((0,), (1,)))
    grad_gain_two = jnp.sum(dact_two * norm_two, axis=0)
    dn2 = dact_two * gain_two
    dresid = dy + scale_two * (dn2 - norm_two * jnp.mean(dn2 * norm_two, axis=-1, keepdims=True))
    dresid_b = dresid.astype(bf16)
    dmixed = dot(dresid_b, out_w, ((1,), (1,))).astype(bf16)

    dquery, near_grad, far_grad = attention_back(
        where, query, dmixed, near, far, logs, cos_wide, sin_wide
    )
    (far_grad,), y_came = tie_lists((far_grad,), y_came)
    came = lax.ppermute(far_grad, "context", [(1, 0)])
    y_last = scatter_second(y_parts, y_came)
    grad_query = dot(act_one, dquery, ((0,), (0,))).astype(bf16)
    dkv = key_value_back(near_grad, came, cos_wide, sin_wide)
    grad_kv = dot(act_one, dkv, ((0,), (0,))).astype(bf16)
    halves = [swap_halves(grad, context) for grad in (grad_query, grad_kv)]
    first_parts = dense_parts(halves, context, expert)
    first_came = scatter_first(first_parts)

    first_parts, (dquery, dkv, dlogits, dresid_b), y_last, shares[0] = tie_lists(
        first_parts, (dquery, dkv, dlogits, dresid_b), y_last, shares[0]
    )
    y_sum = scatter_total(y_parts, y_came, y_last)
    block_out = (resid_one + y_sum).astype(bf16)[None]
    out_halves = swap_halves(dot(mixed, dresid_b, ((0,), (0,))), context)
    dact_one = dot(dquery, qkv_w[:, :Q_WIDTH], ((1,), (1,)))
    dact_one = dact_one + dot(dkv, qkv_w[:, Q_WIDTH:], ((1,), (1,)))
    grad_gain_one = jnp.sum(dact_one * norm_one, axis=0)
    dn1 = dact_one * gain_one
    grad_in = dresid + scale_one * (dn1 - norm_one * jnp.mean(dn1 * norm_one, axis=-1, keepdims=True))
    small = jnp.concatenate(
        [
            dot(dlogits, act_two),
            grad_gain_one[None],
            grad_gain_two[None],
            jnp.zeros((SMALL - experts_all - 2, MODEL_WIDTH), f32),
        ],
        axis=0,
    )
    small = swap_halves(small.T, context)
    (out_theirs, small_theirs), first_came = tie_lists((out_halves[1], small[1]), first_came)
    first_last = scatter_second(first_parts, first_came)
    out_halves = [(out_halves[0], out_theirs), (small[0], small_theirs)]
    out_parts = dense_parts(out_halves, context, expert)
    out_came = scatter_first(out_parts)
    first_total = scatter_total(first_parts, first_came, first_last)
    (first_total,), shares[-1], out_parts = tie_lists(
        (first_total.astype(bf16),), shares[-1], out_parts
    )
    first_share = lax.psum_scatter(first_total, "dp", scatter_dimension=0, tiled=False)
    out_total = scatter_total(out_parts, out_came, scatter_second(out_parts, out_came))
    out_total, first_share = tie(out_total.astype(bf16), first_share)
    first = join_rows(first_share, expert)
    last = join_rows(scatter_line(out_total), expert)
    kv_at = Q_WIDTH + KV_WIDTH

    finals = []
    for pair in shares:
        low, high = pair if len(pair) == 2 else (pair[0][0], pair[0][1])
        keep = jnp.where(context == 0, low, high)
        came = swap(jnp.where(context == 0, high, low))
        finals.append((jnp.where(context == 0, keep, came), jnp.where(context == 0, came, keep)))
    stacked = jnp.stack([f[c] for c in range(2) for f in finals])
    stacked = stacked.astype(f32)
    return (
        block_out,
        grad_in[None],
        last[:, MODEL_WIDTH + experts_all],
        first[:, :Q_WIDTH],
        first[:, Q_WIDTH:kv_at],
        first[:, kv_at:],
        last[:, :MODEL_WIDTH],
        last[:, MODEL_WIDTH + experts_all + 1],
        last[:, MODEL_WIDTH : MODEL_WIDTH + experts_all],
        stacked[:, 0],
        stacked[:, 1],
        jnp.swapaxes(stacked[:, 2], 1, 2),
    )


def solution(mesh):
    tokens_at = P(("expert", "dp"), "context", None)
    vector = P(("context", "dp"))
    matrix = P(("context", "dp"), None)
    wide = P("expert", ("context", "dp"), None)
    down = P("expert", None, ("context", "dp"))
    return jax.shard_map(
        local,
        mesh=mesh,
        in_specs=(
            tokens_at,
            tokens_at,
            tokens_at,
            vector,
            matrix,
            matrix,
            matrix,
            matrix,
            vector,
            matrix,
            wide,
            wide,
            down,
        ),
        out_specs=(
            tokens_at,
            tokens_at,
            vector,
            matrix,
            matrix,
            matrix,
            matrix,
            vector,
            matrix,
            wide,
            wide,
            down,
        ),
        check_vma=False,
    )
```
